32 devices in a mesh: seq: 8 (over y, x, core), fsdp: 4 (over z).
Axes of the slice: x: 2, y: 2, z: 4, core: 2. Of those that a mesh axis runs over, the one named last changes fastest.
Arguments:
- tokens: bfloat16 [4, 8192, 1024], P('fsdp', 'seq'), may hold values from -6 to 6
- segment_ids: int32 [4, 8192], P('fsdp', 'seq'), may hold values from 0 to 2, as said below
- in_weight: bfloat16 [1024, 4384], P(('seq', 'fsdp')), may hold values from -0.1875 to 0.1875
- out_weight: bfloat16 [2048, 1024], P(('seq', 'fsdp')), may hold values from -0.125 to 0.125
- conv_weight: bfloat16 [4, 2304], P(None, ('seq', 'fsdp')), may hold values from -3 to 3
- conv_bias: bfloat16 [2304], P(('seq', 'fsdp')), may hold values from -0.5 to 0.5
- norm_gain: bfloat16 [1024], P(('seq', 'fsdp')), may hold values from 0.5 to 1.5
- gate_gain: bfloat16 [2048], P(('seq', 'fsdp')), may hold values from 0.5 to 1.5
- log_rate: float32 [32], replicated, may hold values from -11 to -1
- skip_gain: float32 [32], replicated, may hold values from 0.5 to 1.5
- step_bias: float32 [32], replicated, may hold values from -4 to -1
- cotangent: bfloat16 [4, 8192, 1024], P('fsdp', 'seq'), may hold values from -6 to 6
Outputs:
- block_out: bfloat16 [4, 8192, 1024], P('fsdp', 'seq')
- grad_tokens: float32 [4, 8192, 1024], P('fsdp', 'seq')
- grad_in_weight: float32 [1024, 4384], P(('seq', 'fsdp'))
- grad_out_weight: float32 [2048, 1024], P(('seq', 'fsdp'))
- grad_conv_weight: float32 [4, 2304], P(None, ('seq', 'fsdp'))
- grad_conv_bias: float32 [2304], P(('seq', 'fsdp'))
- grad_norm_gain: float32 [1024], P(('seq', 'fsdp'))
- grad_gate_gain: float32 [2048], P(('seq', 'fsdp'))
- grad_log_rate: float32 [32], replicated
- grad_skip_gain: float32 [32], replicated
- grad_step_bias: float32 [32], replicated
The draws below stay inside these ranges and needn't reach their ends.
Inputs may be any that keep to these rules, and one draw needn't show every extreme that they name: `segment_ids`: in each row the number rises by one at exactly two positions, one inside the first block of 1024 positions and one inside the last, at an offset from 1 to 1021 within its block.
All inputs are finite; a program needn't handle non-finite values.
Results may differ from the reference program's by a relative error of at most 0.0082.
Values may be sent and summed in bfloat16 or wider, within the bound.
No kernel may reach another device: no remote copies, remote signals or barrier semaphores. Data moves between devices by JAX's collectives and lax.ppermute only.
A program may use at most 320 MiB of HBM per device.

```python
import jax
import jax.numpy as jnp
from jax import lax

D = 1024
HEADS = 32
HEADDIM = 64
STATE = 128
CONV = 4
GROUP = 256
TOK_DEV = 1024
DI = 2048
CHANNELS = 2304
PROJ = 4384
LEN = 8192
SEQS = 4


def draw_segment_ids(key, part):
    key = jax.random.fold_in(key, 5)
    first_key, last_key = jax.random.split(key)
    first_start = jax.random.randint(first_key, (SEQS, 1), 1, TOK_DEV - 2)
    last_start = LEN - TOK_DEV + jax.random.randint(last_key, (SEQS, 1), 1, TOK_DEV - 2)
    places = jnp.arange(LEN)[None, :]
    return (places >= first_start).astype(jnp.int32) + (places >= last_start).astype(jnp.int32)


def draw_log_rate(key, part):
    key = jax.random.fold_in(key, 11)
    pick_key, shake_key = jax.random.split(key)
    share = 0.5
    slow_heads = jax.random.uniform(pick_key, (HEADS,)) < share
    shake = jax.random.uniform(shake_key, (HEADS,), minval=-0.5, maxval=0.5)
    return (jnp.where(slow_heads, jnp.log(2.0 / LEN), jnp.log(0.2)) + shake).astype(jnp.float32)


def block_scale(rng, extent, cuts, least, largest):
    level = 1.0
    for dim, blocks in cuts:
        draws = jax.random.uniform(jax.random.fold_in(jax.random.fold_in(rng, 6), dim), (blocks,), jnp.float32, least / len(cuts), largest / len(cuts))
        level = level * jnp.repeat(jnp.exp(draws), extent[dim] // blocks).reshape((-1,) + (1,) * (len(extent) - 1 - dim))
    return level


def scatter_about(rng, extent, deviation, reach, shards=(), held_as=jnp.bfloat16):
    level = block_scale(rng, extent, shards, -0.22, 0.18) if shards else 1.0
    result = jax.random.normal(rng, extent, jnp.float32) * deviation * level
    return jnp.minimum(jnp.maximum(result, -reach), reach).astype(held_as)


def setup_inputs(seed: int = 0) -> dict:
    key_of = jax.random.split(jax.random.key(seed), 13)
    tokens = scatter_about(key_of[0], (SEQS, LEN, D), 1.0, 6.0, ((0, 4), (1, 8)))
    segment_ids = draw_segment_ids(jax.random.fold_in(key_of[12], 71), 0)
    in_weight = scatter_about(key_of[2], (D, PROJ), D ** -0.5, 0.1875, ((0, 32),))
    out_weight = scatter_about(key_of[3], (DI, D), DI ** -0.5, 0.125, ((0, 32),))
    conv_weight = scatter_about(key_of[4], (CONV, CHANNELS), CONV ** -0.5, 3.0, ((1, 32),))
    conv_bias = jnp.clip(jax.random.uniform(key_of[5], (CHANNELS,), jnp.float32, -0.5, 0.5) * block_scale(key_of[5], (CHANNELS,), ((0, 32),), -0.4, 0.0), -0.5, 0.5).astype(jnp.bfloat16)
    norm_gain = jnp.clip(1.0 + 0.1 * jax.random.normal(key_of[6], (D,), jnp.float32), 0.5, 1.5).astype(jnp.bfloat16)
    gate_gain = jnp.clip(1.0 + 0.1 * jax.random.normal(key_of[7], (DI,), jnp.float32), 0.5, 1.5).astype(jnp.bfloat16)
    log_rate = draw_log_rate(jax.random.fold_in(key_of[12], 71), 0)
    skip_gain = jnp.clip(jax.random.uniform(key_of[9], (HEADS,), jnp.float32, 0.5, 1.5), 0.5, 1.5)
    step_bias = jnp.clip(jax.random.uniform(key_of[10], (HEADS,), jnp.float32, -4.0, -1.0), -4.0, -1.0)
    cotangent = scatter_about(key_of[11], (SEQS, LEN, D), 1.0, 6.0, ((0, 4), (1, 8)))
    return dict(tokens=tokens, segment_ids=segment_ids, in_weight=in_weight, out_weight=out_weight, conv_weight=conv_weight, conv_bias=conv_bias, norm_gain=norm_gain, gate_gain=gate_gain, log_rate=log_rate, skip_gain=skip_gain, step_bias=step_bias, cotangent=cotangent)


HIGH = lax.Precision.HIGHEST

@jax.custom_vjp
def low(v):
    return lax.optimization_barrier(v.astype(jnp.bfloat16)).astype(jnp.float32)

@jax.custom_vjp
def low_back(v):
    return v

def low_keep(v):
    return (low(v), None)

def low_pass(kept, grad):
    return (grad,)

def back_keep(v):
    return (v, None)

def back_low(kept, grad):
    return (low(grad),)
low.defvjp(low_keep, low_pass)
low_back.defvjp(back_keep, back_low)

def norm_scale(value, gain):
    return value * lax.rsqrt(lax.optimization_barrier(jnp.mean(value * value, axis=-1, keepdims=True)) + 1e-05) * gain

def group_step(carried_in, pieces):
    memory, before = carried_in
    values, keys_in, queries, decay_log, step_size, labels = pieces
    block_len = labels.shape[0]
    running = jnp.cumsum(decay_log, axis=0)
    places = jnp.arange(block_len)
    allowed = (places[:, None] >= places[None, :]) & (labels[:, None] == labels[None, :])
    differ = running[:, None, :] - running[None, :, :]
    factor = jnp.exp(jnp.where(allowed[:, :, None], differ, 0.0)) * allowed[:, :, None].astype(jnp.float32)
    scores = jnp.dot(queries, keys_in.T, precision=HIGH)
    mixing = factor * scores[:, :, None] * step_size[None, :, :]
    output = jnp.einsum('tsh,shp->thp', mixing, values, precision=HIGH)
    entering = jnp.exp(running) * (labels == before).astype(jnp.float32)[:, None]
    output = output + entering[:, :, None] * jnp.einsum('tn,hpn->thp', queries, memory, precision=HIGH)
    summed = running[-1]
    weight_tail = jnp.exp(summed[None, :] - running) * (labels == labels[-1]).astype(jnp.float32)[:, None] * step_size
    carried = jnp.exp(summed) * (labels[-1] == before).astype(jnp.float32)
    memory = carried[:, None, None] * memory + jnp.einsum('sh,shp,sn->hpn', weight_tail, values, keys_in, precision=HIGH)
    return ((memory, labels[-1]), output)

def conv_mix(conv_in, labels, conv_weight, conv_bias):
    kernel_len = conv_weight.shape[0]
    row_count = conv_in.shape[0]
    padded = jnp.concatenate([jnp.zeros((kernel_len - 1, conv_in.shape[1]), conv_in.dtype), conv_in], axis=0)
    label_pad = jnp.concatenate([jnp.full((kernel_len - 1,), -1, jnp.int32), labels], axis=0)
    summed = conv_bias[None, :] + jnp.zeros_like(conv_in)
    for offset in range(kernel_len):
        keep_mask = (label_pad[offset:offset + row_count] == labels).astype(jnp.float32)
        summed = summed + conv_weight[offset][None, :] * padded[offset:offset + row_count] * keep_mask[:, None]
    return jax.nn.silu(summed)

def one_sequence(inputs, labels, weights):
    in_weight, out_weight, conv_weight, conv_bias, norm_gain, gate_gain, log_rate, skip_gain, step_bias = weights
    row_count = inputs.shape[0]
    hidden = low(norm_scale(inputs, norm_gain))
    projected = low_back(low(jnp.dot(hidden, in_weight, precision=HIGH)))
    gate_part = projected[:, :DI]
    conv_in = projected[:, DI:2 * DI + 2 * STATE]
    raw_step = projected[:, 2 * DI + 2 * STATE:]
    mixed = conv_mix(conv_in, labels, conv_weight, conv_bias)
    values = mixed[:, :DI].reshape(row_count, HEADS, HEADDIM)
    keys_in = mixed[:, DI:DI + STATE]
    queries = mixed[:, DI + STATE:]
    step_size = jax.nn.softplus(raw_step + step_bias)
    decay_log = -jnp.exp(log_rate) * step_size
    blocks_count = row_count // GROUP
    pieces = (values.reshape(blocks_count, GROUP, HEADS, HEADDIM), keys_in.reshape(blocks_count, GROUP, STATE), queries.reshape(blocks_count, GROUP, STATE), decay_log.reshape(blocks_count, GROUP, HEADS), step_size.reshape(blocks_count, GROUP, HEADS), labels.reshape(blocks_count, GROUP))
    initial = (jnp.zeros((HEADS, HEADDIM, STATE), jnp.float32), jnp.int32(-1))
    ignored, outputs = lax.scan(jax.checkpoint(group_step), initial, pieces)
    mixed_out = outputs.reshape(row_count, HEADS, HEADDIM) + skip_gain[:, None] * values
    gated = mixed_out.reshape(row_count, DI) * jax.nn.silu(gate_part)
    normed = low(norm_scale(gated, gate_gain))
    return inputs + jnp.dot(normed, out_weight, precision=HIGH)

def reference(tokens, segment_ids, in_weight, out_weight, conv_weight, conv_bias, norm_gain, gate_gain, log_rate, skip_gain, step_bias, cotangent):
    weights = tuple((item.astype(jnp.float32) for item in (in_weight, out_weight, conv_weight, conv_bias, norm_gain, gate_gain, log_rate, skip_gain, step_bias)))

    def per_sequence(totals, entry):
        inputs, labels, upstream = entry

        def forward(inputs, weights):
            return one_sequence(inputs, labels, weights)
        block, pull = jax.vjp(forward, inputs, weights)
        grad_inputs, grad_weights = pull(upstream)
        totals = jax.tree.map(jnp.add, totals, grad_weights)
        return (totals, (block.astype(jnp.bfloat16), grad_inputs))
    zeros_start = jax.tree.map(jnp.zeros_like, weights)
    totals, outputs = lax.scan(per_sequence, zeros_start, (tokens.astype(jnp.float32), segment_ids, cotangent.astype(jnp.float32)))
    block_out, grad_tokens = outputs
    return (block_out, grad_tokens, totals[0], totals[1], totals[2], totals[3], totals[4], totals[5], totals[6], totals[7], totals[8])
```

```python
import functools

import jax
import jax.numpy as jnp
import numpy as np
from jax import lax
from jax.experimental import pallas as pl
from jax.experimental.pallas import tpu as pltpu
from jax.sharding import Mesh
from jax.sharding import PartitionSpec as P

HEADS = 32
HEADDIM = 64
STATE = 128
CHUNK = 128
LANES = 128
DI = HEADS * HEADDIM
CHANNELS = DI + 2 * STATE
WIDE = 512
NEG = -1e30
LOG2E = 1.4426950408889634
ALL = ("pair", "core", "fsdp")
BF = jnp.bfloat16
F32 = jnp.float32
NT = (((1,), (1,)), ((), ()))
TN = (((0,), (0,)), ((), ()))
NN = (((1,), (0,)), ((), ()))
PARAMS = pltpu.CompilerParams(
    dimension_semantics=("arbitrary",), vmem_limit_bytes=56 * 1024 * 1024
)


def mm(a, b, dims=NN):
    return lax.dot_general(a, b, dims, preferred_element_type=F32)


def pieces(x, count):
    out = []
    for _ in range(count):
        part = x.astype(BF)
        out.append(part)
        x = x - part.astype(F32)
    return out


def spread(x, expand):
    hi, lo = pieces(x, 2)
    return mm(hi, expand) + mm(lo, expand)


def head_sum(x, expand):
    hi, lo = pieces(x, 2)
    return mm(hi, expand, NT) + mm(lo, expand, NT)


def cumulate(tri, x):
    a, b, c = pieces(x, 3)
    return mm(tri, a) + mm(tri, b) + mm(tri, c)


def mm3(a, b, dims=NN):
    a_hi, a_lo = pieces(a, 2)
    b_hi, b_lo = pieces(b, 2)
    return mm(a_hi, b_hi, dims) + (mm(a_lo, b_hi, dims) + mm(a_hi, b_lo, dims))


def sigmoid(x):
    return 1.0 / (1.0 + jnp.exp(-x))


def iota2(shape, dim):
    return lax.broadcasted_iota(jnp.int32, shape, dim)


def rows8(x):
    return jnp.sum(x.reshape(x.shape[0] // 8, 8, x.shape[1]), axis=0)


def prep_kernel(
    x_ref, raw_ref, info_ref, halo_ref, w_ref, b_ref, rate_ref, sbias_ref, e_ref,
    z_ref, v_ref, k_ref, q_ref, rc_ref, rs_ref, pack_ref,
    state, thru, carry, pad,
):
    step = pl.program_id(0)

    @pl.when(step == 0)
    def _():
        carry[...] = halo_ref[...]
        state[...] = jnp.zeros_like(state)
        thru[...] = jnp.ones_like(thru)
        pad[...] = jnp.zeros_like(pad)

    info = info_ref[...]
    age = jnp.broadcast_to(info[:, 1:2], (CHUNK, LANES))
    masks = [(age >= d).astype(F32) for d in (1.0, 2.0, 3.0)]
    for tile in range(CHANNELS // LANES):
        sl = slice(tile * LANES, (tile + 1) * LANES)
        x = x_ref[:, sl].astype(F32)
        ext = jnp.concatenate([carry[:, sl], x], axis=0)
        z = b_ref[:, sl] + w_ref[3:4, sl] * x
        for d in (1, 2, 3):
            z = z + w_ref[3 - d : 4 - d, sl] * (ext[8 - d : 8 - d + CHUNK] * masks[d - 1])
        carry[:, sl] = x[CHUNK - 8 :]
        z_ref[:, sl] = z.astype(BF)
        value = z * sigmoid(z)
        if tile < DI // LANES:
            v_ref[:, sl] = value.astype(BF)
        elif tile == DI // LANES:
            k_ref[...] = value
        else:
            q_ref[...] = value

    raw = raw_ref[...].astype(F32) + sbias_ref[...]
    size = jnp.maximum(raw, 0.0) + jnp.log1p(jnp.exp(-jnp.abs(raw)))
    decay = -jnp.exp(rate_ref[...]) * size * LOG2E
    tri = (iota2((CHUNK, CHUNK), 0) >= iota2((CHUNK, CHUNK), 1)).astype(BF)
    running = cumulate(tri, decay)
    shifted = running - jnp.log2(jnp.maximum(size, 1e-37))
    rc_ref[...] = running
    pad[:, :HEADS] = shifted
    rs_ref[...] = pad[...].T[:HEADS]
    total = running[CHUNK - 1 :]
    weight = jnp.exp2(total - shifted) * info[:, 3:4]
    carried = jnp.exp2(running[CHUNK - 8 :]) * info[CHUNK - 8 :, 2:3]
    keys = k_ref[...].astype(BF)
    for g in range(DI // WIDE):
        sl = slice(g * WIDE, (g + 1) * WIDE)
        scaled = (spread(weight, e_ref[:, sl]) * v_ref[:, sl].astype(F32)).astype(BF)
        factor = spread(carried, e_ref[:, sl])[7:8]
        state[:, sl] = factor * state[:, sl] + mm(keys, scaled, TN)
        thru[:, sl] = factor * thru[:, sl]

    @pl.when(step == pl.num_programs(0) - 1)
    def _():
        pack_ref[:STATE] = state[...]
        hi, lo = pieces(thru[...], 2)
        row = iota2((16, DI), 0)
        pack_ref[STATE:] = jnp.where(
            row == 0, hi.astype(F32), jnp.where(row == 1, lo.astype(F32), 0.0)
        )


def shared(q_ref, k_ref, lc_ref, lr_ref):
    scores = mm3(q_ref[...], k_ref[...], NT)
    ok = (iota2((CHUNK, CHUNK), 0) >= iota2((CHUNK, CHUNK), 1)) & (
        lc_ref[:, 0:1] == lr_ref[0, 0:1, :]
    )
    bias = jnp.where(ok, 0.0, NEG)
    low_half = iota2((CHUNK, LANES), 1) < HEADDIM
    return scores, bias, low_half


def two_heads(v, low_half):
    zero = jnp.zeros_like(v)
    return jnp.concatenate([jnp.where(low_half, v, zero), jnp.where(low_half, zero, v)], axis=0)


def intra_kernel(q_ref, k_ref, v_ref, rc_ref, rs_ref, lc_ref, lr_ref, y_ref):
    scores, bias, low_half = shared(q_ref, k_ref, lc_ref, lr_ref)
    for pair in range(HEADS // 2):
        sl = slice(pair * LANES, (pair + 1) * LANES)
        mixing = []
        for h in (2 * pair, 2 * pair + 1):
            differ = (rc_ref[:, h : h + 1] - rs_ref[h : h + 1, :]) + bias
            mixing.append((jnp.exp2(differ) * scores).astype(BF))
        y_ref[:, sl] = mm(jnp.concatenate(mixing, axis=1), two_heads(v_ref[:, sl], low_half))


def gate_kernel(
    y_ref, q_ref, k_ref, v_ref, rc_ref, rs_ref, info_ref, gate_ref, dn_ref, sin_ref,
    skip_ref, gain_ref, e_ref,
    n_ref, dy_ref, dy_lo_ref, dgate_ref, u_ref, dq_ref, sc_ref, pack_ref, sums_ref,
    state, adj, reach, scan, enter, sums, pad,
):
    step = pl.program_id(0)

    @pl.when(step == 0)
    def _():
        state[...] = sin_ref[...]
        adj[...] = jnp.zeros_like(adj)
        reach[...] = jnp.ones_like(reach)
        sums[...] = jnp.zeros_like(sums)

    info = info_ref[...]
    running = rc_ref[...]
    pad[:HEADS] = rs_ref[...]
    shifted = pad[...].T[:, :HEADS]
    total = running[CHUNK - 1 :]
    weight = jnp.exp2(total - shifted) * info[:, 3:4]
    entering = jnp.exp2(running) * info[:, 2:3]
    queries, queries_lo = pieces(q_ref[...], 2)
    keys = k_ref[...].astype(BF)
    squares = jnp.zeros((CHUNK, LANES), F32)
    dots = jnp.zeros((CHUNK, LANES), F32)
    for g in range(DI // WIDE):
        sl = slice(g * WIDE, (g + 1) * WIDE)
        low_state, rest = pieces(state[:, sl], 2)
        sc_ref[:, sl] = low_state
        ent = spread(entering, e_ref[:, sl])
        enter[:, sl] = ent
        y = y_ref[:, sl] + ent * (
            mm(queries, low_state) + (mm(queries_lo, low_state) + mm(queries, rest))
        )
        scan[:, sl] = y
        gate = gate_ref[:, sl].astype(F32)
        gated = (y + skip_ref[:, sl] * v_ref[:, sl].astype(F32)) * (gate * sigmoid(gate))
        square = gated * gated
        dot = dn_ref[:, sl] * gain_ref[:, sl] * gated
        for t in range(WIDE // LANES):
            part = slice(t * LANES, (t + 1) * LANES)
            squares = squares + square[:, part]
            dots = dots + dot[:, part]
    inv = lax.rsqrt(jnp.sum(squares, axis=1, keepdims=True) * (1.0 / DI) + 1e-05)
    coef = inv * inv * inv * jnp.sum(dots, axis=1, keepdims=True) * (1.0 / DI)
    head_dots = jnp.zeros((CHUNK, HEADS), F32)
    dq = jnp.zeros((CHUNK, STATE), F32)
    for g in range(DI // WIDE):
        sl = slice(g * WIDE, (g + 1) * WIDE)
        y = scan[:, sl]
        v = v_ref[:, sl].astype(F32)
        gate = gate_ref[:, sl].astype(F32)
        sig = sigmoid(gate)
        silu = gate * sig
        mixed = y + skip_ref[:, sl] * v
        gated = mixed * silu
        gain = gain_ref[:, sl]
        dn = dn_ref[:, sl]
        unit = gated * inv
        n_ref[:, sl] = (unit * gain).astype(BF)
        sums[0:8, sl] += rows8(dn * unit)
        dg = dn * gain * inv - gated * coef
        dgate_ref[:, sl] = (dg * mixed * (sig + silu * (1.0 - sig))).astype(BF)
        dy = dg * silu
        sums[8:16, sl] += rows8(dy * v)
        low, rest = pieces(dy, 2)
        dy_ref[:, sl] = low
        dy_lo_ref[:, sl] = rest
        head_dots = head_dots + head_sum(low.astype(F32) * y, e_ref[:, sl])
        ent = enter[:, sl]
        dy_in, dy_in_lo = pieces(ent * dy, 2)
        state_hi, state_lo = pieces(state[:, sl], 2)
        dq = dq + (
            mm(dy_in, state_hi, NT) + (mm(dy_in_lo, state_hi, NT) + mm(dy_in, state_lo, NT))
        )
        adj[:, sl] += reach[:, sl] * mm(queries, dy_in, TN)
        factor = ent[CHUNK - 1 :]
        scaled = (spread(weight, e_ref[:, sl]) * v).astype(BF)
        state[:, sl] = factor * state[:, sl] + mm(keys, scaled, TN)
        reach[:, sl] = factor * reach[:, sl]
    u_ref[...] = head_dots
    dq_ref[...] = dq

    @pl.when(step == pl.num_programs(0) - 1)
    def _():
        pack_ref[:STATE] = adj[...].astype(BF)
        hi, lo = pieces(reach[...], 2)
        row = iota2((16, DI), 0)
        pack_ref[STATE:] = jnp.where(
            row == 0, hi.astype(F32), jnp.where(row == 1, lo.astype(F32), 0.0)
        ).astype(BF)
        sums_ref[...] = sums[...]


def intra_back_kernel(
    q_ref, k_ref, v_ref, dy_ref, dy_lo_ref, rc_ref, rs_ref, lc_ref, lr_ref, e_ref, dqin_ref,
    dv_ref, uv_ref, dq_ref, dk_ref,
):
    scores, bias, low_half = shared(q_ref, k_ref, lc_ref, lr_ref)
    dscores = jnp.zeros((CHUNK, CHUNK), F32)
    head_dots = jnp.zeros((CHUNK, HEADS), F32)
    for pair in range(HEADS // 2):
        sl = slice(pair * LANES, (pair + 1) * LANES)
        v = v_ref[:, sl]
        dy = dy_ref[:, sl]
        vv = two_heads(v, low_half)
        dmix = mm(
            jnp.concatenate([dy, dy_lo_ref[:, sl]], axis=1),
            jnp.concatenate([vv, vv], axis=1),
            NT,
        )
        mixing = []
        for i in range(2):
            h = 2 * pair + i
            differ = (rc_ref[:, h : h + 1] - rs_ref[h : h + 1, :]) + bias
            factor = jnp.exp2(differ)
            dscores = dscores + dmix[:, i * CHUNK : (i + 1) * CHUNK] * factor
            mixing.append((factor * scores).astype(BF))
        both = mm(jnp.concatenate(mixing, axis=1), dy, TN)
        dv = jnp.where(low_half, both[:CHUNK], both[CHUNK:])
        dv_ref[:, sl] = dv.astype(BF)
        head_dots = head_dots + head_sum(v.astype(F32) * dv, e_ref[:, sl])
    uv_ref[...] = head_dots
    dq_ref[...] = dqin_ref[...] + mm3(dscores, k_ref[...])
    dk_ref[...] = mm(dscores.astype(BF), q_ref[...].astype(BF), TN)


def back_kernel(
    x_ref, raw_ref, z_ref, v_ref, k_ref, q_ref, rc_ref, rs_ref, info_ref, dy_ref, dv_ref,
    uv_ref, u_ref, dq_ref, dk_ref, sc_ref, ain_ref, halo_ref, w_ref, rate_ref, sbias_ref,
    skip_ref, e_ref,
    dx_ref, dhalo_ref, csum_ref, hsum_ref,
    adj, nextz, nextage, csum, hsum, pad, dmix,
):
    step = pl.program_id(0)

    @pl.when(step == 0)
    def _():
        adj[...] = ain_ref[...]
        nextz[...] = jnp.zeros_like(nextz)
        nextage[...] = jnp.zeros_like(nextage)
        csum[...] = jnp.zeros_like(csum)
        hsum[...] = jnp.zeros_like(hsum)

    info = info_ref[...]
    running = rc_ref[...]
    pad[:HEADS] = rs_ref[...]
    shifted = pad[...].T[:, :HEADS]
    total = running[CHUNK - 1 :]
    weight = jnp.exp2(total - shifted) * info[:, 3:4]
    entering = jnp.exp2(running) * info[:, 2:3]
    queries = q_ref[...].astype(BF)
    keys = k_ref[...].astype(BF)
    dq = dq_ref[...]
    dk = dk_ref[...]
    later = jnp.zeros((CHUNK, HEADS), F32)
    through = jnp.zeros((8, HEADS), F32)
    for g in range(DI // WIDE):
        sl = slice(g * WIDE, (g + 1) * WIDE)
        e = e_ref[:, sl]
        v = v_ref[:, sl].astype(F32)
        dy = dy_ref[:, sl].astype(F32)
        ent = spread(entering, e)
        wide = spread(weight, e)
        dy_in = (ent * dy).astype(BF)
        scaled = (wide * v).astype(BF)
        adjoint = adj[:, sl]
        low_adj = adjoint.astype(BF)
        states = sc_ref[:, sl]
        dv = wide * mm(keys, low_adj)
        later = later + head_sum(v * dv, e)
        dk = dk + mm(scaled, low_adj, NT)
        factor = ent[CHUNK - 1 :]
        through = through + head_sum(rows8(adjoint * states.astype(F32)) * factor, e)
        adj[:, sl] = factor * adjoint + mm(queries, dy_in, TN)
        dmix[:, sl] = dv_ref[:, sl].astype(F32) + dv + skip_ref[:, sl] * dy
    dmix[:, DI : DI + STATE] = dk
    dmix[:, DI + STATE :] = dq

    age = jnp.broadcast_to(info[:, 1:2], (CHUNK, LANES))
    masks = [(age >= d).astype(F32) for d in (1.0, 2.0, 3.0)]
    ages = nextage[...]
    next_masks = [(ages >= d).astype(F32) for d in (1.0, 2.0, 3.0)]
    for tile in range(CHANNELS // LANES):
        sl = slice(tile * LANES, (tile + 1) * LANES)
        z = z_ref[:, sl].astype(F32)
        sig = sigmoid(z)
        dz = dmix[:, sl] * (sig + z * sig * (1.0 - sig))
        x = x_ref[:, sl].astype(F32)
        after = nextz[:, sl]
        dx = w_ref[3:4, sl] * dz
        csum[32:40, sl] += rows8(dz)
        csum[24:32, sl] += rows8(x * dz)
        for d in (1, 2, 3):
            ext = jnp.concatenate([dz * masks[d - 1], after * next_masks[d - 1]], axis=0)
            moved = ext[d : d + CHUNK]
            dx = dx + w_ref[3 - d : 4 - d, sl] * moved
            csum[8 * (3 - d) : 8 * (4 - d), sl] += rows8(x * moved)
        dx_ref[:, sl] = dx.astype(BF)
        nextz[:, sl] = dz[:8]

        @pl.when(step == pl.num_programs(0) - 1)
        def _():
            halo = halo_ref[:, sl]
            acc = jnp.zeros((8, LANES), F32)
            for d in (1, 2, 3):
                ext = jnp.concatenate(
                    [jnp.zeros((8, LANES), F32), dz[:8] * masks[d - 1][:8]], axis=0
                )
                moved = ext[d : d + 8]
                acc = acc + w_ref[3 - d : 4 - d, sl] * moved
                csum[8 * (3 - d) : 8 * (4 - d), sl] += halo * moved
            dhalo_ref[:, sl] = acc
    nextage[...] = age[:8]

    row = iota2((CHUNK, CHUNK), 0)
    col = iota2((CHUNK, CHUNK), 1)
    ddecay = (
        cumulate((col >= row).astype(BF), u_ref[...] - uv_ref[...])
        + cumulate((col < row).astype(BF), later)
        + jnp.sum(through, axis=0, keepdims=True)
    )
    raw = raw_ref[...].astype(F32) + sbias_ref[...]
    sig = sigmoid(raw)
    size = jnp.maximum(raw, 0.0) + jnp.log1p(jnp.exp(-jnp.abs(raw)))
    rate = -jnp.exp(rate_ref[...])
    ratio = jnp.where(raw < -15.0, 1.0, sig / jnp.maximum(size, 1e-37))
    draw = (uv_ref[...] + later) * ratio + ddecay * rate * sig
    dx_ref[:, CHANNELS:] = draw.astype(BF)
    hsum[0:8] += rows8(ddecay * rate * size)
    hsum[8:16] += rows8(draw)

    @pl.when(step == pl.num_programs(0) - 1)
    def _():
        csum_ref[...] = csum[...]
        hsum_ref[...] = hsum[...]


def whole(shape):
    return pl.BlockSpec(shape, lambda c: (0,) * len(shape))


def rows(width, count=None, per=CHUNK):
    if count is None:
        return pl.BlockSpec((per, width), lambda c: (c, 0))
    return pl.BlockSpec((per, width), lambda c: (count - 1 - c, 0))


def shape(dims, kind):
    return jax.ShapeDtypeStruct(dims, kind)


def cost(flops, moved):
    return pl.CostEstimate(flops=flops, bytes_accessed=moved, transcendentals=0)


def vm(dims, kind=F32):
    return pltpu.VMEM(dims, kind)


def pack(state, thru, kind):
    hi, lo = pieces(thru, 2)
    return jnp.concatenate([state.astype(kind), hi.astype(kind), lo.astype(kind)], axis=0)


def unpack(packed):
    packed = packed.astype(F32)
    return packed[:STATE], packed[STATE : STATE + 1] + packed[STATE + 1 : STATE + 2]


def carry_states(packed, pairs, backward):
    packed = packed[: STATE + 2]
    core = lax.axis_index("core")
    place = lax.axis_index("pair")
    half = packed.shape[1] // 2
    swap = [(0, 1), (1, 0)]
    left, right = packed[:, :half], packed[:, half:]
    mine = jnp.where(core == 0, left, right)
    theirs = lax.ppermute(jnp.where(core == 0, right, left), "core", swap)
    leads = (core == 1) if backward else (core == 0)
    first, first_thru = unpack(jnp.where(leads, mine, theirs))
    second, second_thru = unpack(jnp.where(leads, theirs, mine))
    total, total_thru = second + second_thru * first, second_thru * first_thru
    before, before_thru = jnp.zeros_like(total), jnp.ones_like(total_thru)
    distance = 1
    while distance < pairs:
        route = [(i, i ^ distance) for i in range(pairs)]
        other, other_thru = unpack(
            lax.ppermute(pack(total, total_thru, packed.dtype), "pair", route)
        )
        upper = (place & distance) != 0
        follows = jnp.logical_not(upper) if backward else upper
        before = jnp.where(follows, before + before_thru * other, before)
        before_thru = jnp.where(follows, before_thru * other_thru, before_thru)
        total = jnp.where(
            follows, total + total_thru * other, other + other_thru * total
        )
        total_thru = total_thru * other_thru
        distance *= 2
    after = first + first_thru * before
    keep = jnp.where(leads, before, after)
    other = lax.ppermute(
        jnp.where(leads, after, before).astype(packed.dtype), "core", swap
    ).astype(F32)
    return jnp.where(
        core == 0,
        jnp.concatenate([keep, other], axis=1),
        jnp.concatenate([other, keep], axis=1),
    )


def shift(block, count, by):
    moved = [(i, i + by) for i in range(count) if 0 <= i + by < count]
    return lax.ppermute(block, ("pair", "core"), moved)


def swap(block, axis, mask):
    count = lax.axis_size(axis)
    return lax.ppermute(block, axis, [(i, i ^ mask) for i in range(count)])


def bit_orders(pairs):
    bits = list(range(pairs.bit_length() - 1))
    cut = len(bits) // 2
    return bits, bits[cut:] + bits[:cut]


def part_ids(pairs, fsdp):
    out = []
    for part, order in enumerate(bit_orders(pairs)):
        ids = [(0, k) for k in range(part * fsdp // 2, (part + 1) * fsdp // 2)]
        for b in order:
            ids = ids + [(mask ^ (1 << b), k) for mask, k in ids]
        out.append(ids)
    return out


def shard_of(place_ref, fsdp, mask, flip, k):
    return ((place_ref[0] ^ mask) * 2 + (place_ref[1] ^ flip)) * fsdp + (place_ref[2] ^ k)


def place_rows(place, pieces_in, r, fsdp, total):
    jobs = [
        (i, at, mask, flip, k)
        for i, (_, flip, ids) in enumerate(pieces_in)
        for at, (mask, k) in enumerate(ids)
    ]

    def body(place_ref, *refs):
        dst, sem = refs[-2], refs[-1]
        copies = []
        for j, (i, at, mask, flip, k) in enumerate(jobs):
            row = pl.multiple_of(shard_of(place_ref, fsdp, mask, flip, k) * r, r)
            copies.append(
                pltpu.make_async_copy(
                    refs[i].at[pl.ds(at * r, r)], dst.at[pl.ds(row, r)], sem.at[j]
                )
            )
            copies[-1].start()
        for copy in copies:
            copy.wait()

    arrays = [a for a, _, _ in pieces_in]
    cols = arrays[0].shape[1]
    return pl.pallas_call(
        body,
        name="place_rows",
        in_specs=[pl.BlockSpec(memory_space=pltpu.SMEM)]
        + [pl.BlockSpec(memory_space=pl.ANY)] * len(arrays),
        out_specs=pl.BlockSpec(memory_space=pl.ANY),
        out_shape=jax.ShapeDtypeStruct((total, cols), arrays[0].dtype),
        scratch_shapes=[pltpu.SemaphoreType.DMA((len(jobs),))],
        cost_estimate=pl.CostEstimate(
            flops=0, bytes_accessed=4 * total * cols, transcendentals=0
        ),
    )(place, *arrays)


def pick_rows(place, whole_rows, r, pairs, fsdp):
    order = [i for ids in part_ids(pairs, fsdp) for i in ids]
    half = len(order) * r
    cols = whole_rows.shape[1]

    def body(place_ref, src, keep, give, sem):
        copies = []
        for flip, dst in ((1, give), (0, keep)):
            for at, (mask, k) in enumerate(order):
                row = pl.multiple_of(shard_of(place_ref, fsdp, mask, flip, k) * r, r)
                copies.append(
                    pltpu.make_async_copy(
                        src.at[pl.ds(row, r)], dst.at[pl.ds(at * r, r)], sem.at[len(copies)]
                    )
                )
                copies[-1].start()
        for copy in copies:
            copy.wait()

    return pl.pallas_call(
        body,
        name="pick_rows",
        in_specs=[
            pl.BlockSpec(memory_space=pltpu.SMEM), pl.BlockSpec(memory_space=pl.ANY),
        ],
        out_specs=[pl.BlockSpec(memory_space=pl.ANY)] * 2,
        out_shape=[jax.ShapeDtypeStruct((half, cols), whole_rows.dtype)] * 2,
        scratch_shapes=[pltpu.SemaphoreType.DMA((2 * len(order),))],
        cost_estimate=pl.CostEstimate(
            flops=0, bytes_accessed=8 * half * cols, transcendentals=0
        ),
    )(place, whole_rows)


def gather_rows(w, place, pairs):
    r, fsdp = w.shape[0], lax.axis_size("fsdp")
    if r % 16:
        return lax.all_gather(w, ALL, axis=0, tiled=True)
    line = [w] + [swap(w, "fsdp", k) for k in range(1, fsdp)]
    held = []
    for part, order in enumerate(bit_orders(pairs)):
        ks = range(part * fsdp // 2, (part + 1) * fsdp // 2)
        block = jnp.concatenate([line[k] for k in ks], axis=0)
        ids = [(0, k) for k in ks]
        held.append((block, 0, ids))
        for b in order:
            got = swap(block, "pair", 1 << b)
            got_ids = [(mask ^ (1 << b), k) for mask, k in ids]
            held.append((got, 0, got_ids))
            block = jnp.concatenate([block, got], axis=0)
            ids = ids + got_ids
    held = held + [(swap(a, "core", 1), 1, ids) for a, _, ids in held]
    return place_rows(place, held, r, fsdp, 2 * pairs * fsdp * r)


def reduce_rows(g, place, pairs):
    fsdp = lax.axis_size("fsdp")
    r = g.shape[0] // (2 * pairs * fsdp)
    if r % 16:
        return lax.psum_scatter(g.astype(F32), ALL, scatter_dimension=0, tiled=True)
    keep, give = pick_rows(place, g, r, pairs, fsdp)
    summed = keep.astype(F32) + swap(give, "core", 1).astype(F32)
    half = summed.shape[0] // 2
    ends = []
    for part, order in enumerate(bit_orders(pairs)):
        block = summed[part * half : (part + 1) * half]
        for b in reversed(order):
            cut = block.shape[0] // 2
            got = swap(block[cut:].astype(BF), "pair", 1 << b)
            block = block[:cut] + got.astype(F32)
        ends.append(block)
    total = ends[0][:r]
    for k in range(1, fsdp):
        at = (k % (fsdp // 2)) * r
        block = ends[k // (fsdp // 2)][at : at + r]
        total = total + swap(block.astype(BF), "fsdp", k).astype(F32)
    return total


def links(pairs, fsdp):
    out = [("fsdp", 1 << b) for b in range(fsdp.bit_length() - 1)]
    out.append(("core", 1))
    return out + [("pair", 1 << b) for b in range(pairs.bit_length() - 1)]


def gather_small(vec, place_index, pairs, fsdp):
    block = vec[None]
    for axis, mask in links(pairs, fsdp):
        block = jnp.concatenate([block, swap(block, axis, mask)], axis=0)
    count = block.shape[0]
    index = jnp.arange(count)
    pick = (index[:, None] == (index[None] ^ place_index)).astype(BF)
    return jnp.dot(pick, block, preferred_element_type=F32)


def sum_small(block, pairs, fsdp):
    for axis, mask in links(pairs, fsdp):
        block = block + swap(block, axis, mask)
    return block


def hidden_of(tokens, gain):
    x = tokens.astype(F32)
    return (x * lax.rsqrt(jnp.mean(x * x, axis=-1, keepdims=True) + 1e-05) * gain).astype(BF)


def on_device(
    pairs, tokens, segment_ids, in_weight, out_weight, conv_weight, conv_bias, norm_gain,
    gate_gain, log_rate, skip_gain, step_bias, cotangent,
):
    tokens, labels, upstream = tokens[0], segment_ids[0], cotangent[0]
    count, model = tokens.shape
    chunks = count // CHUNK
    taps = conv_weight.shape[0]
    own = (conv_weight.size, conv_bias.size, norm_gain.size, gate_gain.size)
    fsdp = lax.axis_size("fsdp")
    place = jnp.stack([lax.axis_index(a) for a in ALL])
    device = (place[0] * 2 + place[1]) * fsdp + place[2]
    small = jnp.concatenate([conv_weight.reshape(-1), conv_bias, norm_gain, gate_gain])
    small = gather_small(small, device, pairs, fsdp)
    conv_full = (
        small[:, : own[0]].reshape(-1, taps, own[0] // taps).transpose(1, 0, 2)
        .reshape(taps, CHANNELS).astype(F32)
    )
    at = own[0]
    bias_full = small[:, at : at + own[1]].reshape(1, CHANNELS).astype(F32)
    at += own[1]
    norm_full = small[:, at : at + own[2]].reshape(1, model).astype(F32)
    at += own[2]
    gate_full = small[:, at :].reshape(1, DI).astype(F32)
    w_mix = gather_rows(in_weight[:, DI:], place, pairs)
    w_gate = gather_rows(in_weight[:, :DI], place, pairs)
    w_out = gather_rows(out_weight, place, pairs)

    expand = jnp.asarray(np.repeat(np.eye(HEADS), HEADDIM, axis=1), BF)
    skip_wide = jnp.repeat(skip_gain, HEADDIM)[None]
    rate, sbias = log_rate[None], step_bias[None]
    before = jnp.concatenate([jnp.broadcast_to(labels[:1], (3,)), labels])
    age = sum((before[3 - d : 3 - d + count] == labels).astype(F32) for d in (1, 2, 3))
    by_chunk = labels.reshape(chunks, CHUNK)
    last = by_chunk[:, -1:]
    prior = jnp.concatenate([by_chunk[:1, :1], last[:-1]], axis=0)
    info = jnp.stack(
        [
            labels.astype(F32),
            age,
            (by_chunk == prior).astype(F32).reshape(-1),
            (by_chunk == last).astype(F32).reshape(-1),
        ]
        + [jnp.zeros((count,), F32)] * 4,
        axis=1,
    )
    label_rows = labels.astype(F32).reshape(chunks, 1, CHUNK)
    row_spec = pl.BlockSpec((1, 1, CHUNK), lambda c: (c, 0, 0))

    tail = shift(tokens[count - 8 :], 2 * pairs, 1)
    hidden = hidden_of(tokens, norm_full)
    halo_hidden = hidden_of(tail, norm_full)
    mix = jnp.dot(hidden, w_mix, preferred_element_type=F32).astype(BF)
    raw_step = mix[:, CHANNELS:]
    halo = jnp.dot(halo_hidden, w_mix[:, :CHANNELS], preferred_element_type=F32)
    halo = halo.astype(BF).astype(F32)

    z, v, k, q, rc, rs, packed = pl.pallas_call(
        prep_kernel,
        name="conv_states",
        grid=(chunks,),
        in_specs=[
            rows(CHANNELS), rows(HEADS), rows(8), whole((8, CHANNELS)), whole((taps, CHANNELS)),
            whole((1, CHANNELS)), whole((1, HEADS)), whole((1, HEADS)), whole((HEADS, DI)),
        ],
        out_specs=[
            rows(CHANNELS), rows(DI), rows(STATE), rows(STATE), rows(HEADS),
            rows(CHUNK, per=HEADS), whole((STATE + 16, DI)),
        ],
        out_shape=[
            shape((count, CHANNELS), BF), shape((count, DI), BF), shape((count, STATE), F32),
            shape((count, STATE), F32), shape((count, HEADS), F32),
            shape((chunks * HEADS, CHUNK), F32), shape((STATE + 16, DI), F32),
        ],
        scratch_shapes=[
            vm((STATE, DI)), vm((1, DI)), vm((8, CHANNELS)), vm((CHUNK, LANES)),
        ],
        compiler_params=PARAMS,
        cost_estimate=cost(10**9, 30 * 10**6),
    )(mix, raw_step, info, halo, conv_full, bias_full, rate, sbias, expand)

    incoming = carry_states(packed, pairs, False)

    y_local = pl.pallas_call(
        intra_kernel,
        name="intra",
        grid=(chunks,),
        in_specs=[
            rows(STATE), rows(STATE), rows(DI), rows(HEADS), rows(CHUNK, per=HEADS), rows(8),
            row_spec,
        ],
        out_specs=rows(DI),
        out_shape=shape((count, DI), F32),
        compiler_params=PARAMS,
        cost_estimate=cost(10**9, 30 * 10**6),
    )(q, k, v, rc, rs, info, label_rows)

    gate = jnp.dot(hidden, w_gate, preferred_element_type=F32).astype(BF)
    grad_normed = lax.dot_general(upstream, w_out, NT, preferred_element_type=F32)

    normed, dy, dy_lo, dgate, u, dq, states, packed_back, gate_sums = pl.pallas_call(
        gate_kernel,
        name="gate_norm",
        grid=(chunks,),
        in_specs=[
            rows(DI), rows(STATE), rows(STATE), rows(DI), rows(HEADS), rows(CHUNK, per=HEADS),
            rows(8), rows(DI), rows(DI), whole((STATE, DI)), whole((1, DI)), whole((1, DI)),
            whole((HEADS, DI)),
        ],
        out_specs=[
            rows(DI), rows(DI), rows(DI), rows(DI), rows(HEADS), rows(STATE), rows(DI),
            whole((STATE + 16, DI)), whole((16, DI)),
        ],
        out_shape=[
            shape((count, DI), BF), shape((count, DI), BF), shape((count, DI), BF),
            shape((count, DI), BF), shape((count, HEADS), F32), shape((count, STATE), F32),
            shape((chunks * STATE, DI), BF),
            shape((STATE + 16, DI), BF), shape((16, DI), F32),
        ],
        scratch_shapes=[
            vm((STATE, DI)), vm((STATE, DI)), vm((1, DI)), vm((CHUNK, DI)), vm((CHUNK, DI)),
            vm((16, DI)), vm((LANES, CHUNK)),
        ],
        compiler_params=PARAMS,
        cost_estimate=cost(10**9, 50 * 10**6),
    )(
        y_local, q, k, v, rc, rs, info, gate, grad_normed, incoming, skip_wide, gate_full,
        expand,
    )

    coming_back = carry_states(packed_back, pairs, True)

    grad_out_w = lax.dot_general(normed, upstream, TN, preferred_element_type=F32).astype(BF)
    out_shard = reduce_rows(grad_out_w, place, pairs)
    grad_gate_w = lax.dot_general(hidden, dgate, TN, preferred_element_type=F32).astype(BF)
    gate_shard = reduce_rows(grad_gate_w, place, pairs)
    block_out = (
        tokens.astype(F32) + jnp.dot(normed, w_out, preferred_element_type=F32)
    ).astype(BF)

    dv, uv, dq, dk = pl.pallas_call(
        intra_back_kernel,
        name="intra_back",
        grid=(chunks,),
        in_specs=[
            rows(STATE), rows(STATE), rows(DI), rows(DI), rows(DI), rows(HEADS),
            rows(CHUNK, per=HEADS), rows(8), row_spec, whole((HEADS, DI)), rows(STATE),
        ],
        out_specs=[rows(DI), rows(HEADS), rows(STATE), rows(STATE)],
        out_shape=[
            shape((count, DI), BF), shape((count, HEADS), F32), shape((count, STATE), F32),
            shape((count, STATE), F32),
        ],
        compiler_params=PARAMS,
        cost_estimate=cost(2 * 10**9, 40 * 10**6),
    )(q, k, v, dy, dy_lo, rc, rs, info, label_rows, expand, dq)

    back = functools.partial(rows, count=chunks)
    grad_mix, dhalo, conv_sums, head_sums = pl.pallas_call(
        back_kernel,
        name="states_conv_back",
        grid=(chunks,),
        in_specs=[
            back(CHANNELS), back(HEADS), back(CHANNELS), back(DI), back(STATE), back(STATE),
            back(HEADS), back(CHUNK, per=HEADS), back(8), back(DI), back(DI), back(HEADS),
            back(HEADS), back(STATE), back(STATE), back(DI), whole((STATE, DI)),
            whole((8, CHANNELS)), whole((taps, CHANNELS)), whole((1, HEADS)),
            whole((1, HEADS)), whole((1, DI)), whole((HEADS, DI)),
        ],
        out_specs=[
            back(CHANNELS + HEADS), whole((8, CHANNELS)), whole((40, CHANNELS)),
            whole((16, HEADS)),
        ],
        out_shape=[
            shape((count, CHANNELS + HEADS), BF), shape((8, CHANNELS), F32),
            shape((40, CHANNELS), F32), shape((16, HEADS), F32),
        ],
        scratch_shapes=[
            vm((STATE, DI)), vm((8, CHANNELS)), vm((8, LANES)), vm((40, CHANNELS)),
            vm((16, HEADS)), vm((LANES, CHUNK)), vm((CHUNK, CHANNELS)),
        ],
        compiler_params=PARAMS,
        cost_estimate=cost(2 * 10**9, 60 * 10**6),
    )(
        mix, raw_step, z, v, k, q, rc, rs, info, dy, dv, uv, u, dq, dk, states, coming_back,
        halo, conv_full, rate, sbias, skip_wide, expand,
    )

    edge = shift(dhalo, 2 * pairs, -1)
    edge = jnp.pad(edge, ((0, 0), (0, HEADS)))
    fixed = (grad_mix[count - 8 :].astype(F32) + edge).astype(BF)
    grad_mix = lax.dynamic_update_slice(grad_mix, fixed, (count - 8, 0))
    grad_mix_w = lax.dot_general(hidden, grad_mix, TN, preferred_element_type=F32).astype(BF)
    mix_shard = reduce_rows(grad_mix_w, place, pairs)
    grad_hidden = lax.dot_general(dgate, w_gate, NT, preferred_element_type=F32)
    grad_hidden = grad_hidden + lax.dot_general(grad_mix, w_mix, NT, preferred_element_type=F32)

    x = tokens.astype(F32)
    inv = lax.rsqrt(jnp.mean(x * x, axis=-1, keepdims=True) + 1e-05)
    unit = x * inv
    scaled = grad_hidden * norm_full
    mean = jnp.mean(scaled * unit, axis=-1, keepdims=True)
    grad_tokens = upstream.astype(F32) + inv * (scaled - unit * mean)
    grad_norm = jnp.sum(grad_hidden * unit, axis=0)

    conv_sums = conv_sums.reshape(taps + 1, 8, CHANNELS).sum(axis=1)
    gate_sums = gate_sums.reshape(2, 8, DI).sum(axis=1)
    head_sums = head_sums.reshape(2, 8, HEADS).sum(axis=1)
    grad_skip = gate_sums[1].reshape(HEADS, HEADDIM).sum(axis=1)
    devices = 2 * pairs * fsdp
    parts = jnp.concatenate(
        [
            conv_sums.reshape(taps + 1, devices, own[1]).transpose(1, 0, 2).reshape(devices, -1),
            grad_norm.reshape(devices, -1),
            gate_sums[0].reshape(devices, -1),
            jnp.broadcast_to(
                jnp.concatenate([head_sums[0], grad_skip, head_sums[1]])[None],
                (devices, 3 * HEADS),
            ),
        ],
        axis=1,
    )
    mine = lax.dynamic_slice(
        sum_small(parts, pairs, fsdp), (device, 0), (1, parts.shape[1])
    )[0]
    ends = np.cumsum([own[0], own[1], own[2], own[3], HEADS, HEADS, HEADS]).tolist()
    conv_shard, bias_shard, norm_shard, gain_shard, *heads = [
        mine[a:b] for a, b in zip([0] + ends[:-1], ends)
    ]
    conv_shard = conv_shard.reshape(taps, -1)
    in_shard = jnp.concatenate([gate_shard, mix_shard], axis=1)
    return (
        block_out[None],
        grad_tokens[None],
        in_shard,
        out_shard,
        conv_shard,
        bias_shard,
        norm_shard,
        gain_shard,
        heads[0],
        heads[1],
        heads[2],
    )


def solution(mesh):
    seq, fsdp = mesh.devices.shape
    fine = Mesh(mesh.devices.reshape(seq // 2, 2, fsdp), ALL)
    line = ("pair", "core")
    tokens, labels, mat = P("fsdp", line, None), P("fsdp", line), P(ALL, None)
    weights = (mat, mat, P(None, ALL), P(ALL), P(ALL), P(ALL), P(), P(), P())
    return jax.shard_map(
        functools.partial(on_device, seq // 2),
        mesh=fine,
        in_specs=(tokens, labels) + weights + (tokens,),
        out_specs=(tokens, tokens) + weights,
        check_vma=False,
    )
```

```python
import functools

import jax
import jax.numpy as jnp
import numpy as np
from jax import lax
from jax.experimental import pallas as pl
from jax.experimental.pallas import tpu as pltpu
from jax.sharding import Mesh
from jax.sharding import PartitionSpec as P

HEADS = 32
HEADDIM = 64
STATE = 128
CHUNK = 128
LANES = 128
DI = HEADS * HEADDIM
CHANNELS = DI + 2 * STATE
WIDE = 512
NEG = -1e30
LOG2E = 1.4426950408889634
ALL = ("pair", "core", "fsdp")
BF = jnp.bfloat16
F32 = jnp.float32
NT = (((1,), (1,)), ((), ()))
TN = (((0,), (0,)), ((), ()))
NN = (((1,), (0,)), ((), ()))
PARAMS = pltpu.CompilerParams(
    dimension_semantics=("arbitrary",), vmem_limit_bytes=56 * 1024 * 1024
)

PLAIN = pltpu.CompilerParams(vmem_limit_bytes=56 * 1024 * 1024)


def mm(a, b, dims=NN):
    return lax.dot_general(a, b, dims, preferred_element_type=F32)


def pieces(x, count):
    out = []
    for _ in range(count):
        part = x.astype(BF)
        out.append(part)
        x = x - part.astype(F32)
    return out


def spread(x, expand):
    hi, lo = pieces(x, 2)
    return mm(hi, expand) + mm(lo, expand)


def head_sum(x, expand):
    hi, lo = pieces(x, 2)
    return mm(hi, expand, NT) + mm(lo, expand, NT)


def cumulate(tri, x):
    a, b, c = pieces(x, 3)
    return mm(tri, a) + mm(tri, b) + mm(tri, c)


def mm3(a, b, dims=NN):
    a_hi, a_lo = pieces(a, 2)
    b_hi, b_lo = pieces(b, 2)
    return mm(a_hi, b_hi, dims) + (mm(a_lo, b_hi, dims) + mm(a_hi, b_lo, dims))


def sigmoid(x):
    return 1.0 / (1.0 + jnp.exp(-x))


def iota2(shape, dim):
    return lax.broadcasted_iota(jnp.int32, shape, dim)


def rows8(x):
    return jnp.sum(x.reshape(x.shape[0] // 8, 8, x.shape[1]), axis=0)


def prep_kernel(
    x_ref, raw_ref, info_ref, halo_ref, w_ref, b_ref, rate_ref, sbias_ref, e_ref,
    z_ref, v_ref, k_ref, q_ref, rc_ref, rs_ref, pack_ref,
    state, thru, carry, pad,
):
    step = pl.program_id(0)

    @pl.when(step == 0)
    def _():
        carry[...] = halo_ref[...]
        state[...] = jnp.zeros_like(state)
        thru[...] = jnp.ones_like(thru)
        pad[...] = jnp.zeros_like(pad)

    info = info_ref[...]
    age = jnp.broadcast_to(info[:, 1:2], (CHUNK, LANES))
    masks = [(age >= d).astype(F32) for d in (1.0, 2.0, 3.0)]
    for tile in range(CHANNELS // LANES):
        sl = slice(tile * LANES, (tile + 1) * LANES)
        x = x_ref[:, sl].astype(F32)
        ext = jnp.concatenate([carry[:, sl], x], axis=0)
        z = b_ref[:, sl] + w_ref[3:4, sl] * x
        for d in (1, 2, 3):
            z = z + w_ref[3 - d : 4 - d, sl] * (ext[8 - d : 8 - d + CHUNK] * masks[d - 1])
        carry[:, sl] = x[CHUNK - 8 :]
        z_ref[:, sl] = z.astype(BF)
        value = z * sigmoid(z)
        if tile < DI // LANES:
            v_ref[:, sl] = value.astype(BF)
        elif tile == DI // LANES:
            k_ref[...] = value
        else:
            q_ref[...] = value

    raw = raw_ref[...].astype(F32) + sbias_ref[...]
    size = jnp.maximum(raw, 0.0) + jnp.log1p(jnp.exp(-jnp.abs(raw)))
    decay = -jnp.exp(rate_ref[...]) * size * LOG2E
    tri = (iota2((CHUNK, CHUNK), 0) >= iota2((CHUNK, CHUNK), 1)).astype(BF)
    running = cumulate(tri, decay)
    shifted = running - jnp.log2(jnp.maximum(size, 1e-37))
    rc_ref[...] = running
    pad[:, :HEADS] = shifted
    rs_ref[...] = pad[...].T[:HEADS]
    total = running[CHUNK - 1 :]
    weight = jnp.exp2(total - shifted) * info[:, 3:4]
    carried = jnp.exp2(running[CHUNK - 8 :]) * info[CHUNK - 8 :, 2:3]
    keys = k_ref[...].astype(BF)
    for g in range(DI // WIDE):
        sl = slice(g * WIDE, (g + 1) * WIDE)
        scaled = (spread(weight, e_ref[:, sl]) * v_ref[:, sl].astype(F32)).astype(BF)
        factor = spread(carried, e_ref[:, sl])[7:8]
        state[:, sl] = factor * state[:, sl] + mm(keys, scaled, TN)
        thru[:, sl] = factor * thru[:, sl]

    @pl.when(step == pl.num_programs(0) - 1)
    def _():
        pack_ref[:STATE] = state[...]
        hi, lo = pieces(thru[...], 2)
        row = iota2((16, DI), 0)
        pack_ref[STATE:] = jnp.where(
            row == 0, hi.astype(F32), jnp.where(row == 1, lo.astype(F32), 0.0)
        )


def shared(q_ref, k_ref, lc_ref, lr_ref):
    scores = mm3(q_ref[...], k_ref[...], NT)
    ok = (iota2((CHUNK, CHUNK), 0) >= iota2((CHUNK, CHUNK), 1)) & (
        lc_ref[:, 0:1] == lr_ref[0, 0:1, :]
    )
    bias = jnp.where(ok, 0.0, NEG)
    low_half = iota2((CHUNK, LANES), 1) < HEADDIM
    return scores, bias, low_half


def two_heads(v, low_half):
    zero = jnp.zeros_like(v)
    return jnp.concatenate([jnp.where(low_half, v, zero), jnp.where(low_half, zero, v)], axis=0)


def intra_kernel(q_ref, k_ref, v_ref, rc_ref, rs_ref, lc_ref, lr_ref, y_ref):
    scores, bias, low_half = shared(q_ref, k_ref, lc_ref, lr_ref)
    for pair in range(HEADS // 2):
        sl = slice(pair * LANES, (pair + 1) * LANES)
        mixing = []
        for h in (2 * pair, 2 * pair + 1):
            differ = (rc_ref[:, h : h + 1] - rs_ref[h : h + 1, :]) + bias
            mixing.append((jnp.exp2(differ) * scores).astype(BF))
        y_ref[:, sl] = mm(jnp.concatenate(mixing, axis=1), two_heads(v_ref[:, sl], low_half))


def gate_kernel(
    y_ref, q_ref, k_ref, v_ref, rc_ref, rs_ref, info_ref, gate_ref, dn_ref, sin_ref,
    skip_ref, gain_ref, e_ref,
    n_ref, dy_ref, dy_lo_ref, dgate_ref, u_ref, dq_ref, sc_ref, pack_ref, sums_ref,
    state, adj, reach, scan, enter, sums, pad,
):
    step = pl.program_id(0)

    @pl.when(step == 0)
    def _():
        state[...] = sin_ref[...]
        adj[...] = jnp.zeros_like(adj)
        reach[...] = jnp.ones_like(reach)
        sums[...] = jnp.zeros_like(sums)

    info = info_ref[...]
    running = rc_ref[...]
    pad[:HEADS] = rs_ref[...]
    shifted = pad[...].T[:, :HEADS]
    total = running[CHUNK - 1 :]
    weight = jnp.exp2(total - shifted) * info[:, 3:4]
    entering = jnp.exp2(running) * info[:, 2:3]
    queries, queries_lo = pieces(q_ref[...], 2)
    keys = k_ref[...].astype(BF)
    squares = jnp.zeros((CHUNK, LANES), F32)
    dots = jnp.zeros((CHUNK, LANES), F32)
    for g in range(DI // WIDE):
        sl = slice(g * WIDE, (g + 1) * WIDE)
        low_state, rest = pieces(state[:, sl], 2)
        sc_ref[:, sl] = low_state
        ent = spread(entering, e_ref[:, sl])
        enter[:, sl] = ent
        y = y_ref[:, sl] + ent * (
            mm(queries, low_state) + (mm(queries_lo, low_state) + mm(queries, rest))
        )
        scan[:, sl] = y
        gate = gate_ref[:, sl].astype(F32)
        gated = (y + skip_ref[:, sl] * v_ref[:, sl].astype(F32)) * (gate * sigmoid(gate))
        square = gated * gated
        dot = dn_ref[:, sl] * gain_ref[:, sl] * gated
        for t in range(WIDE // LANES):
            part = slice(t * LANES, (t + 1) * LANES)
            squares = squares + square[:, part]
            dots = dots + dot[:, part]
    inv = lax.rsqrt(jnp.sum(squares, axis=1, keepdims=True) * (1.0 / DI) + 1e-05)
    coef = inv * inv * inv * jnp.sum(dots, axis=1, keepdims=True) * (1.0 / DI)
    head_dots = jnp.zeros((CHUNK, HEADS), F32)
    dq = jnp.zeros((CHUNK, STATE), F32)
    for g in range(DI // WIDE):
        sl = slice(g * WIDE, (g + 1) * WIDE)
        y = scan[:, sl]
        v = v_ref[:, sl].astype(F32)
        gate = gate_ref[:, sl].astype(F32)
        sig = sigmoid(gate)
        silu = gate * sig
        mixed = y + skip_ref[:, sl] * v
        gated = mixed * silu
        gain = gain_ref[:, sl]
        dn = dn_ref[:, sl]
        unit = gated * inv
        n_ref[:, sl] = (unit * gain).astype(BF)
        sums[0:8, sl] += rows8(dn * unit)
        dg = dn * gain * inv - gated * coef
        dgate_ref[:, sl] = (dg * mixed * (sig + silu * (1.0 - sig))).astype(BF)
        dy = dg * silu
        sums[8:16, sl] += rows8(dy * v)
        low, rest = pieces(dy, 2)
        dy_ref[:, sl] = low
        dy_lo_ref[:, sl] = rest
        head_dots = head_dots + head_sum(low.astype(F32) * y, e_ref[:, sl])
        ent = enter[:, sl]
        dy_in, dy_in_lo = pieces(ent * dy, 2)
        state_hi, state_lo = pieces(state[:, sl], 2)
        dq = dq + (
            mm(dy_in, state_hi, NT) + (mm(dy_in_lo, state_hi, NT) + mm(dy_in, state_lo, NT))
        )
        adj[:, sl] += reach[:, sl] * mm(queries, dy_in, TN)
        factor = ent[CHUNK - 1 :]
        scaled = (spread(weight, e_ref[:, sl]) * v).astype(BF)
        state[:, sl] = factor * state[:, sl] + mm(keys, scaled, TN)
        reach[:, sl] = factor * reach[:, sl]
    u_ref[...] = head_dots
    dq_ref[...] = dq

    @pl.when(step == pl.num_programs(0) - 1)
    def _():
        pack_ref[:STATE] = adj[...].astype(BF)
        hi, lo = pieces(reach[...], 2)
        row = iota2((16, DI), 0)
        pack_ref[STATE:] = jnp.where(
            row == 0, hi.astype(F32), jnp.where(row == 1, lo.astype(F32), 0.0)
        ).astype(BF)
        sums_ref[...] = sums[...]


def intra_back_kernel(
    q_ref, k_ref, v_ref, dy_ref, dy_lo_ref, rc_ref, rs_ref, lc_ref, lr_ref, e_ref, dqin_ref,
    dv_ref, uv_ref, dq_ref, dk_ref,
):
    scores, bias, low_half = shared(q_ref, k_ref, lc_ref, lr_ref)
    dscores = jnp.zeros((CHUNK, CHUNK), F32)
    head_dots = jnp.zeros((CHUNK, HEADS), F32)
    for pair in range(HEADS // 2):
        sl = slice(pair * LANES, (pair + 1) * LANES)
        v = v_ref[:, sl]
        dy = dy_ref[:, sl]
        vv = two_heads(v, low_half)
        dmix = mm(
            jnp.concatenate([dy, dy_lo_ref[:, sl]], axis=1),
            jnp.concatenate([vv, vv], axis=1),
            NT,
        )
        mixing = []
        for i in range(2):
            h = 2 * pair + i
            differ = (rc_ref[:, h : h + 1] - rs_ref[h : h + 1, :]) + bias
            factor = jnp.exp2(differ)
            dscores = dscores + dmix[:, i * CHUNK : (i + 1) * CHUNK] * factor
            mixing.append((factor * scores).astype(BF))
        both = mm(jnp.concatenate(mixing, axis=1), dy, TN)
        dv = jnp.where(low_half, both[:CHUNK], both[CHUNK:])
        dv_ref[:, sl] = dv.astype(BF)
        head_dots = head_dots + head_sum(v.astype(F32) * dv, e_ref[:, sl])
    uv_ref[...] = head_dots
    dq_ref[...] = dqin_ref[...] + mm3(dscores, k_ref[...])
    dk_ref[...] = mm(dscores.astype(BF), q_ref[...].astype(BF), TN)


def back_kernel(
    x_ref, raw_ref, z_ref, v_ref, k_ref, q_ref, rc_ref, rs_ref, info_ref, dy_ref, dv_ref,
    uv_ref, u_ref, dq_ref, dk_ref, sc_ref, ain_ref, halo_ref, w_ref, rate_ref, sbias_ref,
    skip_ref, e_ref,
    dx_ref, dhalo_ref, csum_ref, hsum_ref,
    adj, nextz, nextage, csum, hsum, pad, dmix,
):
    step = pl.program_id(0)

    @pl.when(step == 0)
    def _():
        adj[...] = ain_ref[...]
        nextz[...] = jnp.zeros_like(nextz)
        nextage[...] = jnp.zeros_like(nextage)
        csum[...] = jnp.zeros_like(csum)
        hsum[...] = jnp.zeros_like(hsum)

    info = info_ref[...]
    running = rc_ref[...]
    pad[:HEADS] = rs_ref[...]
    shifted = pad[...].T[:, :HEADS]
    total = running[CHUNK - 1 :]
    weight = jnp.exp2(total - shifted) * info[:, 3:4]
    entering = jnp.exp2(running) * info[:, 2:3]
    queries = q_ref[...].astype(BF)
    keys = k_ref[...].astype(BF)
    dq = dq_ref[...]
    dk = dk_ref[...]
    later = jnp.zeros((CHUNK, HEADS), F32)
    through = jnp.zeros((8, HEADS), F32)
    for g in range(DI // WIDE):
        sl = slice(g * WIDE, (g + 1) * WIDE)
        e = e_ref[:, sl]
        v = v_ref[:, sl].astype(F32)
        dy = dy_ref[:, sl].astype(F32)
        ent = spread(entering, e)
        wide = spread(weight, e)
        dy_in = (ent * dy).astype(BF)
        scaled = (wide * v).astype(BF)
        adjoint = adj[:, sl]
        low_adj = adjoint.astype(BF)
        states = sc_ref[:, sl]
        dv = wide * mm(keys, low_adj)
        later = later + head_sum(v * dv, e)
        dk = dk + mm(scaled, low_adj, NT)
        factor = ent[CHUNK - 1 :]
        through = through + head_sum(rows8(adjoint * states.astype(F32)) * factor, e)
        adj[:, sl] = factor * adjoint + mm(queries, dy_in, TN)
        dmix[:, sl] = dv_ref[:, sl].astype(F32) + dv + skip_ref[:, sl] * dy
    dmix[:, DI : DI + STATE] = dk
    dmix[:, DI + STATE :] = dq

    age = jnp.broadcast_to(info[:, 1:2], (CHUNK, LANES))
    masks = [(age >= d).astype(F32) for d in (1.0, 2.0, 3.0)]
    ages = nextage[...]
    next_masks = [(ages >= d).astype(F32) for d in (1.0, 2.0, 3.0)]
    for tile in range(CHANNELS // LANES):
        sl = slice(tile * LANES, (tile + 1) * LANES)
        z = z_ref[:, sl].astype(F32)
        sig = sigmoid(z)
        dz = dmix[:, sl] * (sig + z * sig * (1.0 - sig))
        x = x_ref[:, sl].astype(F32)
        after = nextz[:, sl]
        dx = w_ref[3:4, sl] * dz
        csum[32:40, sl] += rows8(dz)
        csum[24:32, sl] += rows8(x * dz)
        for d in (1, 2, 3):
            ext = jnp.concatenate([dz * masks[d - 1], after * next_masks[d - 1]], axis=0)
            moved = ext[d : d + CHUNK]
            dx = dx + w_ref[3 - d : 4 - d, sl] * moved
            csum[8 * (3 - d) : 8 * (4 - d), sl] += rows8(x * moved)
        dx_ref[:, sl] = dx.astype(BF)
        nextz[:, sl] = dz[:8]

        @pl.when(step == pl.num_programs(0) - 1)
        def _():
            halo = halo_ref[:, sl]
            acc = jnp.zeros((8, LANES), F32)
            for d in (1, 2, 3):
                ext = jnp.concatenate(
                    [jnp.zeros((8, LANES), F32), dz[:8] * masks[d - 1][:8]], axis=0
                )
                moved = ext[d : d + 8]
                acc = acc + w_ref[3 - d : 4 - d, sl] * moved
                csum[8 * (3 - d) : 8 * (4 - d), sl] += halo * moved
            dhalo_ref[:, sl] = acc
    nextage[...] = age[:8]

    row = iota2((CHUNK, CHUNK), 0)
    col = iota2((CHUNK, CHUNK), 1)
    ddecay = (
        cumulate((col >= row).astype(BF), u_ref[...] - uv_ref[...])
        + cumulate((col < row).astype(BF), later)
        + jnp.sum(through, axis=0, keepdims=True)
    )
    raw = raw_ref[...].astype(F32) + sbias_ref[...]
    sig = sigmoid(raw)
    size = jnp.maximum(raw, 0.0) + jnp.log1p(jnp.exp(-jnp.abs(raw)))
    rate = -jnp.exp(rate_ref[...])
    ratio = jnp.where(raw < -15.0, 1.0, sig / jnp.maximum(size, 1e-37))
    draw = (uv_ref[...] + later) * ratio + ddecay * rate * sig
    dx_ref[:, CHANNELS:] = draw.astype(BF)
    hsum[0:8] += rows8(ddecay * rate * size)
    hsum[8:16] += rows8(draw)

    @pl.when(step == pl.num_programs(0) - 1)
    def _():
        csum_ref[...] = csum[...]
        hsum_ref[...] = hsum[...]


def whole(shape):
    return pl.BlockSpec(shape, lambda c: (0,) * len(shape))


def rows(width, count=None, per=CHUNK):
    if count is None:
        return pl.BlockSpec((per, width), lambda c: (c, 0))
    return pl.BlockSpec((per, width), lambda c: (count - 1 - c, 0))


def shape(dims, kind):
    return jax.ShapeDtypeStruct(dims, kind)


def cost(flops, moved):
    return pl.CostEstimate(flops=flops, bytes_accessed=moved, transcendentals=0)


def vm(dims, kind=F32):
    return pltpu.VMEM(dims, kind)


def pack(state, thru, kind):
    hi, lo = pieces(thru, 2)
    return jnp.concatenate([state.astype(kind), hi.astype(kind), lo.astype(kind)], axis=0)


def unpack(packed):
    packed = packed.astype(F32)
    return packed[:STATE], packed[STATE : STATE + 1] + packed[STATE + 1 : STATE + 2]


def carry_states(packed, pairs, backward):
    packed = packed[: STATE + 2]
    core = lax.axis_index("core")
    place = lax.axis_index("pair")
    half = packed.shape[1] // 2
    swap = [(0, 1), (1, 0)]
    left, right = packed[:, :half], packed[:, half:]
    mine = jnp.where(core == 0, left, right)
    theirs = lax.ppermute(jnp.where(core == 0, right, left), "core", swap)
    leads = (core == 1) if backward else (core == 0)
    first, first_thru = unpack(jnp.where(leads, mine, theirs))
    second, second_thru = unpack(jnp.where(leads, theirs, mine))
    total, total_thru = second + second_thru * first, second_thru * first_thru
    before, before_thru = jnp.zeros_like(total), jnp.ones_like(total_thru)
    distance = 1
    while distance < pairs:
        route = [(i, i ^ distance) for i in range(pairs)]
        other, other_thru = unpack(
            lax.ppermute(pack(total, total_thru, packed.dtype), "pair", route)
        )
        upper = (place & distance) != 0
        follows = jnp.logical_not(upper) if backward else upper
        before = jnp.where(follows, before + before_thru * other, before)
        before_thru = jnp.where(follows, before_thru * other_thru, before_thru)
        total = jnp.where(
            follows, total + total_thru * other, other + other_thru * total
        )
        total_thru = total_thru * other_thru
        distance *= 2
    after = first + first_thru * before
    keep = jnp.where(leads, before, after)
    other = lax.ppermute(
        jnp.where(leads, after, before).astype(packed.dtype), "core", swap
    ).astype(F32)
    return jnp.where(
        core == 0,
        jnp.concatenate([keep, other], axis=1),
        jnp.concatenate([other, keep], axis=1),
    )


def shift(block, count, by):
    moved = [(i, i + by) for i in range(count) if 0 <= i + by < count]
    return lax.ppermute(block, ("pair", "core"), moved)


def swap(block, axis, mask):
    count = lax.axis_size(axis)
    return lax.ppermute(block, axis, [(i, i ^ mask) for i in range(count)])


def bit_orders(pairs):
    bits = list(range(pairs.bit_length() - 1))
    cut = len(bits) // 2
    return bits, bits[cut:] + bits[:cut]


def part_ids(pairs, fsdp):
    out = []
    for part, order in enumerate(bit_orders(pairs)):
        ids = [(0, k) for k in range(part * fsdp // 2, (part + 1) * fsdp // 2)]
        for b in order:
            ids = ids + [(mask ^ (1 << b), k) for mask, k in ids]
        out.append(ids)
    return out


def shard_of(place_ref, fsdp, mask, flip, k):
    return ((place_ref[0] ^ mask) * 2 + (place_ref[1] ^ flip)) * fsdp + (place_ref[2] ^ k)


def place_rows(place, held, r, fsdp, total):
    def body(place_ref, *refs):
        dst = refs[-1]
        for src, (_, flip, ids) in zip(refs, held):
            for at, (mask, k) in enumerate(ids):
                row = pl.multiple_of(shard_of(place_ref, fsdp, mask, flip, k) * r, r)
                dst[pl.ds(row, r), :] = src[at * r : (at + 1) * r, :]

    arrays = [a for a, _, _ in held]
    cols = arrays[0].shape[1]
    return pl.pallas_call(
        body,
        name="place_rows",
        in_specs=[pl.BlockSpec(memory_space=pltpu.SMEM)]
        + [pl.BlockSpec(memory_space=pltpu.VMEM)] * len(arrays),
        out_specs=pl.BlockSpec(memory_space=pltpu.VMEM),
        out_shape=jax.ShapeDtypeStruct((total, cols), arrays[0].dtype),
        compiler_params=PLAIN,
        cost_estimate=cost(0, 4 * total * cols),
    )(place, *arrays)


def pick_rows(place, arrays, r, pairs, fsdp):
    order = [i for ids in part_ids(pairs, fsdp) for i in ids]
    half = len(order) * r
    repeat = [a.shape[0] // (2 * half) for a in arrays]
    cols = sum(a.shape[1] * n for a, n in zip(arrays, repeat))

    def body(place_ref, *refs):
        for flip, dst in ((1, refs[-1]), (0, refs[-2])):
            for at, (mask, k) in enumerate(order):
                index = shard_of(place_ref, fsdp, mask, flip, k)
                col = 0
                for src, n in zip(refs, repeat):
                    for m in range(n):
                        row = pl.multiple_of((index * n + m) * r, r)
                        width = src.shape[1]
                        dst[at * r : (at + 1) * r, col : col + width] = src[pl.ds(row, r), :]
                        col += width

    return pl.pallas_call(
        body,
        name="pick_rows",
        in_specs=[pl.BlockSpec(memory_space=pltpu.SMEM)]
        + [pl.BlockSpec(memory_space=pltpu.VMEM)] * len(arrays),
        out_specs=[pl.BlockSpec(memory_space=pltpu.VMEM)] * 2,
        out_shape=[jax.ShapeDtypeStruct((half, cols), arrays[0].dtype)] * 2,
        compiler_params=PLAIN,
        cost_estimate=cost(0, 8 * half * cols),
    )(place, *arrays)


def unpack_weights(packed, r):
    total, model = packed.shape[0], (packed.shape[1] - DI) // 2
    if r % 16:
        tail = packed[:, DI:].reshape(total // r, r, 2, model).transpose(0, 2, 1, 3)
        return packed[:, :DI], tail.reshape(2 * total, model)
    per = min(total, 256)

    def body(src, gate, out):
        gate[...] = src[:, :DI]
        for i in range(per // r):
            for m in range(2):
                at, col = (2 * i + m) * r, DI + m * model
                out[at : at + r, :] = src[i * r : (i + 1) * r, col : col + model]

    return pl.pallas_call(
        body,
        name="unpack_weights",
        grid=(total // per,),
        in_specs=[rows(packed.shape[1], per=per)],
        out_specs=[rows(DI, per=per), rows(model, per=2 * per)],
        out_shape=[shape((total, DI), BF), shape((2 * total, model), BF)],
        compiler_params=PARAMS,
        cost_estimate=cost(0, 4 * total * packed.shape[1]),
    )(packed)


def gather_rows(w, place, pairs):
    r, fsdp = w.shape[0], lax.axis_size("fsdp")
    if r % 16:
        return lax.all_gather(w, ALL, axis=0, tiled=True)
    line = [w] + [swap(w, "fsdp", k) for k in range(1, fsdp)]
    held = []
    for part, order in enumerate(bit_orders(pairs)):
        ks = range(part * fsdp // 2, (part + 1) * fsdp // 2)
        block = jnp.concatenate([line[k] for k in ks], axis=0)
        for b in order:
            block = jnp.concatenate([block, swap(block, "pair", 1 << b)], axis=0)
        held.append((block, 0, part_ids(pairs, fsdp)[part]))
    held = held + [(swap(a, "core", 1), 1, ids) for a, _, ids in held]
    return place_rows(place, held, r, fsdp, 2 * pairs * fsdp * r)


def reduce_rows(arrays, place, pairs):
    fsdp = lax.axis_size("fsdp")
    r = arrays[0].shape[0] // (2 * pairs * fsdp)
    if r % 16:
        return [
            lax.psum_scatter(g.astype(F32), ALL, scatter_dimension=0, tiled=True) for g in arrays
        ]
    keep, give = pick_rows(place, arrays, r, pairs, fsdp)
    got = swap(give, "core", 1)
    half = keep.shape[0] // 2
    ends = []
    for part, order in enumerate(bit_orders(pairs)):
        at = slice(part * half, (part + 1) * half)
        block = keep[at].astype(F32) + got[at].astype(F32)
        for b in reversed(order):
            cut = block.shape[0] // 2
            other = swap(block[cut:].astype(BF), "pair", 1 << b)
            block = block[:cut] + other.astype(F32)
        ends.append(block)
    total = ends[0][:r]
    for k in range(1, fsdp):
        at = (k % (fsdp // 2)) * r
        block = ends[k // (fsdp // 2)][at : at + r]
        total = total + swap(block.astype(BF), "fsdp", k).astype(F32)
    out, col = [], 0
    for g in arrays:
        width = g.shape[1]
        count = g.shape[0] // arrays[0].shape[0]
        out.append(
            jnp.concatenate(
                [total[:, col + m * width : col + (m + 1) * width] for m in range(count)], axis=0
            )
        )
        col += count * width
    return out


def links(pairs, fsdp):
    out = [("fsdp", 1 << b) for b in range(fsdp.bit_length() - 1)]
    out.append(("core", 1))
    return out + [("pair", 1 << b) for b in range(pairs.bit_length() - 1)]


def gather_small(vec, place_index, pairs, fsdp):
    block = vec[None]
    for axis, mask in links(pairs, fsdp):
        block = jnp.concatenate([block, swap(block, axis, mask)], axis=0)
    count = block.shape[0]
    index = jnp.arange(count)
    pick = (index[:, None] == (index[None] ^ place_index)).astype(BF)
    return jnp.dot(pick, block, preferred_element_type=F32)


def sum_small(block, pairs, fsdp):
    for axis, mask in links(pairs, fsdp):
        block = block + swap(block, axis, mask)
    return block


def hidden_of(tokens, gain):
    x = tokens.astype(F32)
    return (x * lax.rsqrt(jnp.mean(x * x, axis=-1, keepdims=True) + 1e-05) * gain).astype(BF)


def on_device(
    pairs, tokens, segment_ids, in_weight, out_weight, conv_weight, conv_bias, norm_gain,
    gate_gain, log_rate, skip_gain, step_bias, cotangent,
):
    tokens, labels, upstream = tokens[0], segment_ids[0], cotangent[0]
    count, model = tokens.shape
    chunks = count // CHUNK
    taps = conv_weight.shape[0]
    own = (conv_weight.size, conv_bias.size, norm_gain.size, gate_gain.size)
    fsdp = lax.axis_size("fsdp")
    place = jnp.stack([lax.axis_index(a) for a in ALL])
    device = (place[0] * 2 + place[1]) * fsdp + place[2]
    small = jnp.concatenate([conv_weight.reshape(-1), conv_bias, norm_gain, gate_gain])
    small = gather_small(small, device, pairs, fsdp)
    conv_full = (
        small[:, : own[0]].reshape(-1, taps, own[0] // taps).transpose(1, 0, 2)
        .reshape(taps, CHANNELS).astype(F32)
    )
    at = own[0]
    bias_full = small[:, at : at + own[1]].reshape(1, CHANNELS).astype(F32)
    at += own[1]
    norm_full = small[:, at : at + own[2]].reshape(1, model).astype(F32)
    at += own[2]
    gate_full = small[:, at :].reshape(1, DI).astype(F32)
    w_mix = gather_rows(in_weight[:, DI:], place, pairs)
    r = in_weight.shape[0]
    packed_weights = jnp.concatenate(
        [in_weight[:, :DI], out_weight[:r], out_weight[r:]], axis=1
    )
    packed_weights = lax.all_gather(packed_weights, ALL, axis=0, tiled=True)
    w_gate, w_out = unpack_weights(packed_weights, r)

    expand = jnp.asarray(np.repeat(np.eye(HEADS), HEADDIM, axis=1), BF)
    skip_wide = jnp.repeat(skip_gain, HEADDIM)[None]
    rate, sbias = log_rate[None], step_bias[None]
    before = jnp.concatenate([jnp.broadcast_to(labels[:1], (3,)), labels])
    age = sum((before[3 - d : 3 - d + count] == labels).astype(F32) for d in (1, 2, 3))
    by_chunk = labels.reshape(chunks, CHUNK)
    last = by_chunk[:, -1:]
    prior = jnp.concatenate([by_chunk[:1, :1], last[:-1]], axis=0)
    info = jnp.stack(
        [
            labels.astype(F32),
            age,
            (by_chunk == prior).astype(F32).reshape(-1),
            (by_chunk == last).astype(F32).reshape(-1),
        ]
        + [jnp.zeros((count,), F32)] * 4,
        axis=1,
    )
    label_rows = labels.astype(F32).reshape(chunks, 1, CHUNK)
    row_spec = pl.BlockSpec((1, 1, CHUNK), lambda c: (c, 0, 0))

    tail = shift(tokens[count - 8 :], 2 * pairs, 1)
    hidden = hidden_of(tokens, norm_full)
    halo_hidden = hidden_of(tail, norm_full)
    mix = jnp.dot(hidden, w_mix, preferred_element_type=F32).astype(BF)
    raw_step = mix[:, CHANNELS:]
    halo = jnp.dot(halo_hidden, w_mix[:, :CHANNELS], preferred_element_type=F32)
    halo = halo.astype(BF).astype(F32)

    z, v, k, q, rc, rs, packed = pl.pallas_call(
        prep_kernel,
        name="conv_states",
        grid=(chunks,),
        in_specs=[
            rows(CHANNELS), rows(HEADS), rows(8), whole((8, CHANNELS)), whole((taps, CHANNELS)),
            whole((1, CHANNELS)), whole((1, HEADS)), whole((1, HEADS)), whole((HEADS, DI)),
        ],
        out_specs=[
            rows(CHANNELS), rows(DI), rows(STATE), rows(STATE), rows(HEADS),
            rows(CHUNK, per=HEADS), whole((STATE + 16, DI)),
        ],
        out_shape=[
            shape((count, CHANNELS), BF), shape((count, DI), BF), shape((count, STATE), F32),
            shape((count, STATE), F32), shape((count, HEADS), F32),
            shape((chunks * HEADS, CHUNK), F32), shape((STATE + 16, DI), F32),
        ],
        scratch_shapes=[
            vm((STATE, DI)), vm((1, DI)), vm((8, CHANNELS)), vm((CHUNK, LANES)),
        ],
        compiler_params=PARAMS,
        cost_estimate=cost(10**9, 30 * 10**6),
    )(mix, raw_step, info, halo, conv_full, bias_full, rate, sbias, expand)

    incoming = carry_states(packed, pairs, False)

    y_local = pl.pallas_call(
        intra_kernel,
        name="intra",
        grid=(chunks,),
        in_specs=[
            rows(STATE), rows(STATE), rows(DI), rows(HEADS), rows(CHUNK, per=HEADS), rows(8),
            row_spec,
        ],
        out_specs=rows(DI),
        out_shape=shape((count, DI), F32),
        compiler_params=PARAMS,
        cost_estimate=cost(10**9, 30 * 10**6),
    )(q, k, v, rc, rs, info, label_rows)

    gate = jnp.dot(hidden, w_gate, preferred_element_type=F32).astype(BF)
    grad_normed = lax.dot_general(upstream, w_out, NT, preferred_element_type=F32)

    normed, dy, dy_lo, dgate, u, dq, states, packed_back, gate_sums = pl.pallas_call(
        gate_kernel,
        name="gate_norm",
        grid=(chunks,),
        in_specs=[
            rows(DI), rows(STATE), rows(STATE), rows(DI), rows(HEADS), rows(CHUNK, per=HEADS),
            rows(8), rows(DI), rows(DI), whole((STATE, DI)), whole((1, DI)), whole((1, DI)),
            whole((HEADS, DI)),
        ],
        out_specs=[
            rows(DI), rows(DI), rows(DI), rows(DI), rows(HEADS), rows(STATE), rows(DI),
            whole((STATE + 16, DI)), whole((16, DI)),
        ],
        out_shape=[
            shape((count, DI), BF), shape((count, DI), BF), shape((count, DI), BF),
            shape((count, DI), BF), shape((count, HEADS), F32), shape((count, STATE), F32),
            shape((chunks * STATE, DI), BF),
            shape((STATE + 16, DI), BF), shape((16, DI), F32),
        ],
        scratch_shapes=[
            vm((STATE, DI)), vm((STATE, DI)), vm((1, DI)), vm((CHUNK, DI)), vm((CHUNK, DI)),
            vm((16, DI)), vm((LANES, CHUNK)),
        ],
        compiler_params=PARAMS,
        cost_estimate=cost(10**9, 50 * 10**6),
    )(
        y_local, q, k, v, rc, rs, info, gate, grad_normed, incoming, skip_wide, gate_full,
        expand,
    )

    coming_back = carry_states(packed_back, pairs, True)

    grad_out_w = lax.dot_general(normed, upstream, TN, preferred_element_type=F32).astype(BF)
    grad_gate_w = lax.dot_general(hidden, dgate, TN, preferred_element_type=F32).astype(BF)
    gate_shard, out_shard = reduce_rows([grad_gate_w, grad_out_w], place, pairs)
    block_out = (
        tokens.astype(F32) + jnp.dot(normed, w_out, preferred_element_type=F32)
    ).astype(BF)

    dv, uv, dq, dk = pl.pallas_call(
        intra_back_kernel,
        name="intra_back",
        grid=(chunks,),
        in_specs=[
            rows(STATE), rows(STATE), rows(DI), rows(DI), rows(DI), rows(HEADS),
            rows(CHUNK, per=HEADS), rows(8), row_spec, whole((HEADS, DI)), rows(STATE),
        ],
        out_specs=[rows(DI), rows(HEADS), rows(STATE), rows(STATE)],
        out_shape=[
            shape((count, DI), BF), shape((count, HEADS), F32), shape((count, STATE), F32),
            shape((count, STATE), F32),
        ],
        compiler_params=PARAMS,
        cost_estimate=cost(2 * 10**9, 40 * 10**6),
    )(q, k, v, dy, dy_lo, rc, rs, info, label_rows, expand, dq)

    back = functools.partial(rows, count=chunks)
    grad_mix, dhalo, conv_sums, head_sums = pl.pallas_call(
        back_kernel,
        name="states_conv_back",
        grid=(chunks,),
        in_specs=[
            back(CHANNELS), back(HEADS), back(CHANNELS), back(DI), back(STATE), back(STATE),
            back(HEADS), back(CHUNK, per=HEADS), back(8), back(DI), back(DI), back(HEADS),
            back(HEADS), back(STATE), back(STATE), back(DI), whole((STATE, DI)),
            whole((8, CHANNELS)), whole((taps, CHANNELS)), whole((1, HEADS)),
            whole((1, HEADS)), whole((1, DI)), whole((HEADS, DI)),
        ],
        out_specs=[
            back(CHANNELS + HEADS), whole((8, CHANNELS)), whole((40, CHANNELS)),
            whole((16, HEADS)),
        ],
        out_shape=[
            shape((count, CHANNELS + HEADS), BF), shape((8, CHANNELS), F32),
            shape((40, CHANNELS), F32), shape((16, HEADS), F32),
        ],
        scratch_shapes=[
            vm((STATE, DI)), vm((8, CHANNELS)), vm((8, LANES)), vm((40, CHANNELS)),
            vm((16, HEADS)), vm((LANES, CHUNK)), vm((CHUNK, CHANNELS)),
        ],
        compiler_params=PARAMS,
        cost_estimate=cost(2 * 10**9, 60 * 10**6),
    )(
        mix, raw_step, z, v, k, q, rc, rs, info, dy, dv, uv, u, dq, dk, states, coming_back,
        halo, conv_full, rate, sbias, skip_wide, expand,
    )

    edge = shift(dhalo, 2 * pairs, -1)
    edge = jnp.pad(edge, ((0, 0), (0, HEADS)))
    fixed = (grad_mix[count - 8 :].astype(F32) + edge).astype(BF)
    grad_mix = lax.dynamic_update_slice(grad_mix, fixed, (count - 8, 0))
    grad_mix_w = lax.dot_general(hidden, grad_mix, TN, preferred_element_type=F32).astype(BF)
    (mix_shard,) = reduce_rows([grad_mix_w], place, pairs)
    grad_hidden = lax.dot_general(dgate, w_gate, NT, preferred_element_type=F32)
    grad_hidden = grad_hidden + lax.dot_general(grad_mix, w_mix, NT, preferred_element_type=F32)

    x = tokens.astype(F32)
    inv = lax.rsqrt(jnp.mean(x * x, axis=-1, keepdims=True) + 1e-05)
    unit = x * inv
    scaled = grad_hidden * norm_full
    mean = jnp.mean(scaled * unit, axis=-1, keepdims=True)
    grad_tokens = upstream.astype(F32) + inv * (scaled - unit * mean)
    grad_norm = jnp.sum(grad_hidden * unit, axis=0)

    conv_sums = conv_sums.reshape(taps + 1, 8, CHANNELS).sum(axis=1)
    gate_sums = gate_sums.reshape(2, 8, DI).sum(axis=1)
    head_sums = head_sums.reshape(2, 8, HEADS).sum(axis=1)
    grad_skip = gate_sums[1].reshape(HEADS, HEADDIM).sum(axis=1)
    devices = 2 * pairs * fsdp
    parts = jnp.concatenate(
        [
            conv_sums.reshape(taps + 1, devices, own[1]).transpose(1, 0, 2).reshape(devices, -1),
            grad_norm.reshape(devices, -1),
            gate_sums[0].reshape(devices, -1),
            jnp.broadcast_to(
                jnp.concatenate([head_sums[0], grad_skip, head_sums[1]])[None],
                (devices, 3 * HEADS),
            ),
        ],
        axis=1,
    )
    mine = lax.dynamic_slice(
        sum_small(parts, pairs, fsdp), (device, 0), (1, parts.shape[1])
    )[0]
    ends = np.cumsum([own[0], own[1], own[2], own[3], HEADS, HEADS, HEADS]).tolist()
    conv_shard, bias_shard, norm_shard, gain_shard, *heads = [
        mine[a:b] for a, b in zip([0] + ends[:-1], ends)
    ]
    conv_shard = conv_shard.reshape(taps, -1)
    in_shard = jnp.concatenate([gate_shard, mix_shard], axis=1)
    return (
        block_out[None],
        grad_tokens[None],
        in_shard,
        out_shard,
        conv_shard,
        bias_shard,
        norm_shard,
        gain_shard,
        heads[0],
        heads[1],
        heads[2],
    )


def solution(mesh):
    seq, fsdp = mesh.devices.shape
    fine = Mesh(mesh.devices.reshape(seq // 2, 2, fsdp), ALL)
    line = ("pair", "core")
    tokens, labels, mat = P("fsdp", line, None), P("fsdp", line), P(ALL, None)
    weights = (mat, mat, P(None, ALL), P(ALL), P(ALL), P(ALL), P(), P(), P())
    return jax.shard_map(
        functools.partial(on_device, seq // 2),
        mesh=fine,
        in_specs=(tokens, labels) + weights + (tokens,),
        out_specs=(tokens, tokens) + weights,
        check_vma=False,
    )
```

```python
import functools

import jax
import jax.numpy as jnp
import numpy as np
from jax import lax
from jax.experimental import pallas as pl
from jax.experimental.pallas import tpu as pltpu
from jax.sharding import Mesh
from jax.sharding import PartitionSpec as P

HEADS = 32
HEADDIM = 64
STATE = 128
CHUNK = 128
LANES = 128
DI = HEADS * HEADDIM
CHANNELS = DI + 2 * STATE
WIDE = 512
MIX = CHANNELS + HEADS
MIX_WIDE = -(-MIX // 128) * 128
NEG = -1e30
LOG2E = 1.4426950408889634
ALL = ("pair", "core", "fsdp")
BF = jnp.bfloat16
F32 = jnp.float32
NT = (((1,), (1,)), ((), ()))
TN = (((0,), (0,)), ((), ()))
NN = (((1,), (0,)), ((), ()))
PARAMS = pltpu.CompilerParams(
    dimension_semantics=("arbitrary",), vmem_limit_bytes=56 * 1024 * 1024
)

PLAIN = pltpu.CompilerParams(vmem_limit_bytes=56 * 1024 * 1024)


def mm(a, b, dims=NN):
    return lax.dot_general(a, b, dims, preferred_element_type=F32)


def pieces(x, count):
    out = []
    for _ in range(count):
        part = x.astype(BF)
        out.append(part)
        x = x - part.astype(F32)
    return out


def spread(x, expand):
    hi, lo = pieces(x, 2)
    return mm(hi, expand) + mm(lo, expand)


def head_sum(x, expand):
    hi, lo = pieces(x, 2)
    return mm(hi, expand, NT) + mm(lo, expand, NT)


def cumulate(tri, x):
    a, b, c = pieces(x, 3)
    return mm(tri, a) + mm(tri, b) + mm(tri, c)


def mm3(a, b, dims=NN):
    a_hi, a_lo = pieces(a, 2)
    b_hi, b_lo = pieces(b, 2)
    return mm(a_hi, b_hi, dims) + (mm(a_lo, b_hi, dims) + mm(a_hi, b_lo, dims))


def sigmoid(x):
    return 1.0 / (1.0 + jnp.exp(-x))


def iota2(shape, dim):
    return lax.broadcasted_iota(jnp.int32, shape, dim)


def rows8(x):
    return jnp.sum(x.reshape(x.shape[0] // 8, 8, x.shape[1]), axis=0)


def prep_kernel(
    x_ref, raw_ref, info_ref, halo_ref, w_ref, b_ref, rate_ref, sbias_ref, e_ref,
    z_ref, v_ref, k_ref, q_ref, rc_ref, rs_ref, pack_ref,
    state, thru, carry, pad,
):
    step = pl.program_id(0)

    @pl.when(step == 0)
    def _():
        carry[...] = halo_ref[...]
        state[...] = jnp.zeros_like(state)
        thru[...] = jnp.ones_like(thru)
        pad[...] = jnp.zeros_like(pad)

    info = info_ref[...]
    age = jnp.broadcast_to(info[:, 1:2], (CHUNK, LANES))
    masks = [(age >= d).astype(F32) for d in (1.0, 2.0, 3.0)]
    for tile in range(CHANNELS // LANES):
        sl = slice(tile * LANES, (tile + 1) * LANES)
        x = x_ref[:, sl].astype(F32)
        ext = jnp.concatenate([carry[:, sl], x], axis=0)
        z = b_ref[:, sl] + w_ref[3:4, sl] * x
        for d in (1, 2, 3):
            z = z + w_ref[3 - d : 4 - d, sl] * (ext[8 - d : 8 - d + CHUNK] * masks[d - 1])
        carry[:, sl] = x[CHUNK - 8 :]
        z_ref[:, sl] = z.astype(BF)
        value = z * sigmoid(z)
        if tile < DI // LANES:
            v_ref[:, sl] = value.astype(BF)
        elif tile == DI // LANES:
            k_ref[...] = value
        else:
            q_ref[...] = value

    raw = raw_ref[:, :HEADS].astype(F32) + sbias_ref[...]
    size = jnp.maximum(raw, 0.0) + jnp.log1p(jnp.exp(-jnp.abs(raw)))
    decay = -jnp.exp(rate_ref[...]) * size * LOG2E
    tri = (iota2((CHUNK, CHUNK), 0) >= iota2((CHUNK, CHUNK), 1)).astype(BF)
    running = cumulate(tri, decay)
    shifted = running - jnp.log2(jnp.maximum(size, 1e-37))
    rc_ref[...] = running
    pad[:, :HEADS] = shifted
    rs_ref[...] = pad[...].T[:HEADS]
    total = running[CHUNK - 1 :]
    weight = jnp.exp2(total - shifted) * info[:, 3:4]
    carried = jnp.exp2(running[CHUNK - 8 :]) * info[CHUNK - 8 :, 2:3]
    keys = k_ref[...].astype(BF)
    for g in range(DI // WIDE):
        sl = slice(g * WIDE, (g + 1) * WIDE)
        scaled = (spread(weight, e_ref[:, sl]) * v_ref[:, sl].astype(F32)).astype(BF)
        factor = spread(carried, e_ref[:, sl])[7:8]
        state[:, sl] = factor * state[:, sl] + mm(keys, scaled, TN)
        thru[:, sl] = factor * thru[:, sl]

    @pl.when(step == pl.num_programs(0) - 1)
    def _():
        pack_ref[:STATE] = state[...]
        hi, lo = pieces(thru[...], 2)
        row = iota2((16, DI), 0)
        pack_ref[STATE:] = jnp.where(
            row == 0, hi.astype(F32), jnp.where(row == 1, lo.astype(F32), 0.0)
        )


def shared(q_ref, k_ref, lc_ref, lr_ref):
    scores = mm3(q_ref[...], k_ref[...], NT)
    ok = (iota2((CHUNK, CHUNK), 0) >= iota2((CHUNK, CHUNK), 1)) & (
        lc_ref[:, 0:1] == lr_ref[0, 0:1, :]
    )
    bias = jnp.where(ok, 0.0, NEG)
    low_half = iota2((CHUNK, LANES), 1) < HEADDIM
    return scores, bias, low_half


def two_heads(v, low_half):
    zero = jnp.zeros_like(v)
    return jnp.concatenate([jnp.where(low_half, v, zero), jnp.where(low_half, zero, v)], axis=0)


def intra_kernel(q_ref, k_ref, v_ref, rc_ref, rs_ref, lc_ref, lr_ref, y_ref):
    scores, bias, low_half = shared(q_ref, k_ref, lc_ref, lr_ref)
    for pair in range(HEADS // 2):
        sl = slice(pair * LANES, (pair + 1) * LANES)
        mixing = []
        for h in (2 * pair, 2 * pair + 1):
            differ = (rc_ref[:, h : h + 1] - rs_ref[h : h + 1, :]) + bias
            mixing.append((jnp.exp2(differ) * scores).astype(BF))
        y_ref[:, sl] = mm(jnp.concatenate(mixing, axis=1), two_heads(v_ref[:, sl], low_half))


def gate_kernel(
    y_ref, q_ref, k_ref, v_ref, rc_ref, rs_ref, info_ref, gate_ref, dn_ref, sin_ref,
    skip_ref, gain_ref, e_ref,
    n_ref, dy_ref, dy_lo_ref, dgate_ref, u_ref, dq_ref, sc_ref, pack_ref, sums_ref,
    state, adj, reach, scan, enter, sums, pad,
):
    step = pl.program_id(0)

    @pl.when(step == 0)
    def _():
        state[...] = sin_ref[...]
        adj[...] = jnp.zeros_like(adj)
        reach[...] = jnp.ones_like(reach)
        sums[...] = jnp.zeros_like(sums)

    info = info_ref[...]
    running = rc_ref[...]
    pad[:HEADS] = rs_ref[...]
    shifted = pad[...].T[:, :HEADS]
    total = running[CHUNK - 1 :]
    weight = jnp.exp2(total - shifted) * info[:, 3:4]
    entering = jnp.exp2(running) * info[:, 2:3]
    queries, queries_lo = pieces(q_ref[...], 2)
    keys = k_ref[...].astype(BF)
    squares = jnp.zeros((CHUNK, LANES), F32)
    dots = jnp.zeros((CHUNK, LANES), F32)
    for g in range(DI // WIDE):
        sl = slice(g * WIDE, (g + 1) * WIDE)
        low_state, rest = pieces(state[:, sl], 2)
        sc_ref[:, sl] = low_state
        ent = spread(entering, e_ref[:, sl])
        enter[:, sl] = ent
        y = y_ref[:, sl] + ent * (
            mm(queries, low_state) + (mm(queries_lo, low_state) + mm(queries, rest))
        )
        scan[:, sl] = y
        gate = gate_ref[:, sl].astype(F32)
        gated = (y + skip_ref[:, sl] * v_ref[:, sl].astype(F32)) * (gate * sigmoid(gate))
        square = gated * gated
        dot = dn_ref[:, sl] * gain_ref[:, sl] * gated
        for t in range(WIDE // LANES):
            part = slice(t * LANES, (t + 1) * LANES)
            squares = squares + square[:, part]
            dots = dots + dot[:, part]
    inv = lax.rsqrt(jnp.sum(squares, axis=1, keepdims=True) * (1.0 / DI) + 1e-05)
    coef = inv * inv * inv * jnp.sum(dots, axis=1, keepdims=True) * (1.0 / DI)
    head_dots = jnp.zeros((CHUNK, HEADS), F32)
    dq = jnp.zeros((CHUNK, STATE), F32)
    for g in range(DI // WIDE):
        sl = slice(g * WIDE, (g + 1) * WIDE)
        y = scan[:, sl]
        v = v_ref[:, sl].astype(F32)
        gate = gate_ref[:, sl].astype(F32)
        sig = sigmoid(gate)
        silu = gate * sig
        mixed = y + skip_ref[:, sl] * v
        gated = mixed * silu
        gain = gain_ref[:, sl]
        dn = dn_ref[:, sl]
        unit = gated * inv
        n_ref[:, sl] = (unit * gain).astype(BF)
        sums[0:8, sl] += rows8(dn * unit)
        dg = dn * gain * inv - gated * coef
        dgate_ref[:, sl] = (dg * mixed * (sig + silu * (1.0 - sig))).astype(BF)
        dy = dg * silu
        sums[8:16, sl] += rows8(dy * v)
        low, rest = pieces(dy, 2)
        dy_ref[:, sl] = low
        dy_lo_ref[:, sl] = rest
        head_dots = head_dots + head_sum(low.astype(F32) * y, e_ref[:, sl])
        ent = enter[:, sl]
        dy_in, dy_in_lo = pieces(ent * dy, 2)
        state_hi, state_lo = pieces(state[:, sl], 2)
        dq = dq + (
            mm(dy_in, state_hi, NT) + (mm(dy_in_lo, state_hi, NT) + mm(dy_in, state_lo, NT))
        )
        adj[:, sl] += reach[:, sl] * mm(queries, dy_in, TN)
        factor = ent[CHUNK - 1 :]
        scaled = (spread(weight, e_ref[:, sl]) * v).astype(BF)
        state[:, sl] = factor * state[:, sl] + mm(keys, scaled, TN)
        reach[:, sl] = factor * reach[:, sl]
    u_ref[...] = head_dots
    dq_ref[...] = dq

    @pl.when(step == pl.num_programs(0) - 1)
    def _():
        pack_ref[:STATE] = adj[...].astype(BF)
        hi, lo = pieces(reach[...], 2)
        row = iota2((16, DI), 0)
        pack_ref[STATE:] = jnp.where(
            row == 0, hi.astype(F32), jnp.where(row == 1, lo.astype(F32), 0.0)
        ).astype(BF)
        sums_ref[...] = sums[...]


def intra_back_kernel(
    q_ref, k_ref, v_ref, dy_ref, dy_lo_ref, rc_ref, rs_ref, lc_ref, lr_ref, e_ref, dqin_ref,
    dv_ref, uv_ref, dq_ref, dk_ref,
):
    scores, bias, low_half = shared(q_ref, k_ref, lc_ref, lr_ref)
    dscores = jnp.zeros((CHUNK, CHUNK), F32)
    head_dots = jnp.zeros((CHUNK, HEADS), F32)
    for pair in range(HEADS // 2):
        sl = slice(pair * LANES, (pair + 1) * LANES)
        v = v_ref[:, sl]
        dy = dy_ref[:, sl]
        vv = two_heads(v, low_half)
        dmix = mm(
            jnp.concatenate([dy, dy_lo_ref[:, sl]], axis=1),
            jnp.concatenate([vv, vv], axis=1),
            NT,
        )
        mixing = []
        for i in range(2):
            h = 2 * pair + i
            differ = (rc_ref[:, h : h + 1] - rs_ref[h : h + 1, :]) + bias
            factor = jnp.exp2(differ)
            dscores = dscores + dmix[:, i * CHUNK : (i + 1) * CHUNK] * factor
            mixing.append((factor * scores).astype(BF))
        both = mm(jnp.concatenate(mixing, axis=1), dy, TN)
        dv = jnp.where(low_half, both[:CHUNK], both[CHUNK:])
        dv_ref[:, sl] = dv.astype(BF)
        head_dots = head_dots + head_sum(v.astype(F32) * dv, e_ref[:, sl])
    uv_ref[...] = head_dots
    dq_ref[...] = dqin_ref[...] + mm3(dscores, k_ref[...])
    dk_ref[...] = mm(dscores.astype(BF), q_ref[...].astype(BF), TN)


def back_kernel(
    x_ref, raw_ref, z_ref, v_ref, k_ref, q_ref, rc_ref, rs_ref, info_ref, dy_ref, dv_ref,
    uv_ref, u_ref, dq_ref, dk_ref, sc_ref, ain_ref, halo_ref, w_ref, rate_ref, sbias_ref,
    skip_ref, e_ref,
    dx_ref, dhalo_ref, csum_ref, hsum_ref,
    adj, nextz, nextage, csum, hsum, pad, dmix,
):
    step = pl.program_id(0)

    @pl.when(step == 0)
    def _():
        adj[...] = ain_ref[...]
        nextz[...] = jnp.zeros_like(nextz)
        nextage[...] = jnp.zeros_like(nextage)
        csum[...] = jnp.zeros_like(csum)
        hsum[...] = jnp.zeros_like(hsum)

    info = info_ref[...]
    running = rc_ref[...]
    pad[:HEADS] = rs_ref[...]
    shifted = pad[...].T[:, :HEADS]
    total = running[CHUNK - 1 :]
    weight = jnp.exp2(total - shifted) * info[:, 3:4]
    entering = jnp.exp2(running) * info[:, 2:3]
    queries = q_ref[...].astype(BF)
    keys = k_ref[...].astype(BF)
    dq = dq_ref[...]
    dk = dk_ref[...]
    later = jnp.zeros((CHUNK, HEADS), F32)
    through = jnp.zeros((8, HEADS), F32)
    for g in range(DI // WIDE):
        sl = slice(g * WIDE, (g + 1) * WIDE)
        e = e_ref[:, sl]
        v = v_ref[:, sl].astype(F32)
        dy = dy_ref[:, sl].astype(F32)
        ent = spread(entering, e)
        wide = spread(weight, e)
        dy_in = (ent * dy).astype(BF)
        scaled = (wide * v).astype(BF)
        adjoint = adj[:, sl]
        low_adj = adjoint.astype(BF)
        states = sc_ref[:, sl]
        dv = wide * mm(keys, low_adj)
        later = later + head_sum(v * dv, e)
        dk = dk + mm(scaled, low_adj, NT)
        factor = ent[CHUNK - 1 :]
        through = through + head_sum(rows8(adjoint * states.astype(F32)) * factor, e)
        adj[:, sl] = factor * adjoint + mm(queries, dy_in, TN)
        dmix[:, sl] = dv_ref[:, sl].astype(F32) + dv + skip_ref[:, sl] * dy
    dmix[:, DI : DI + STATE] = dk
    dmix[:, DI + STATE :] = dq

    age = jnp.broadcast_to(info[:, 1:2], (CHUNK, LANES))
    masks = [(age >= d).astype(F32) for d in (1.0, 2.0, 3.0)]
    ages = nextage[...]
    next_masks = [(ages >= d).astype(F32) for d in (1.0, 2.0, 3.0)]
    for tile in range(CHANNELS // LANES):
        sl = slice(tile * LANES, (tile + 1) * LANES)
        z = z_ref[:, sl].astype(F32)
        sig = sigmoid(z)
        dz = dmix[:, sl] * (sig + z * sig * (1.0 - sig))
        x = x_ref[:, sl].astype(F32)
        after = nextz[:, sl]
        dx = w_ref[3:4, sl] * dz
        csum[32:40, sl] += rows8(dz)
        csum[24:32, sl] += rows8(x * dz)
        for d in (1, 2, 3):
            ext = jnp.concatenate([dz * masks[d - 1], after * next_masks[d - 1]], axis=0)
            moved = ext[d : d + CHUNK]
            dx = dx + w_ref[3 - d : 4 - d, sl] * moved
            csum[8 * (3 - d) : 8 * (4 - d), sl] += rows8(x * moved)
        dx_ref[:, sl] = dx.astype(BF)
        nextz[:, sl] = dz[:8]

        @pl.when(step == pl.num_programs(0) - 1)
        def _():
            halo = halo_ref[:, sl]
            acc = jnp.zeros((8, LANES), F32)
            for d in (1, 2, 3):
                ext = jnp.concatenate(
                    [jnp.zeros((8, LANES), F32), dz[:8] * masks[d - 1][:8]], axis=0
                )
                moved = ext[d : d + 8]
                acc = acc + w_ref[3 - d : 4 - d, sl] * moved
                csum[8 * (3 - d) : 8 * (4 - d), sl] += halo * moved
            dhalo_ref[:, sl] = acc
    nextage[...] = age[:8]

    row = iota2((CHUNK, CHUNK), 0)
    col = iota2((CHUNK, CHUNK), 1)
    ddecay = (
        cumulate((col >= row).astype(BF), u_ref[...] - uv_ref[...])
        + cumulate((col < row).astype(BF), later)
        + jnp.sum(through, axis=0, keepdims=True)
    )
    raw = raw_ref[:, :HEADS].astype(F32) + sbias_ref[...]
    sig = sigmoid(raw)
    size = jnp.maximum(raw, 0.0) + jnp.log1p(jnp.exp(-jnp.abs(raw)))
    rate = -jnp.exp(rate_ref[...])
    ratio = jnp.where(raw < -15.0, 1.0, sig / jnp.maximum(size, 1e-37))
    draw = (uv_ref[...] + later) * ratio + ddecay * rate * sig
    dx_ref[:, CHANNELS:MIX] = draw.astype(BF)
    dx_ref[:, MIX:] = jnp.zeros((CHUNK, MIX_WIDE - MIX), BF)
    hsum[0:8] += rows8(ddecay * rate * size)
    hsum[8:16] += rows8(draw)

    @pl.when(step == pl.num_programs(0) - 1)
    def _():
        csum_ref[...] = csum[...]
        hsum_ref[...] = hsum[...]


def whole(shape):
    return pl.BlockSpec(shape, lambda c: (0,) * len(shape))


def rows(width, count=None, per=CHUNK):
    if count is None:
        return pl.BlockSpec((per, width), lambda c: (c, 0))
    return pl.BlockSpec((per, width), lambda c: (count - 1 - c, 0))


def raw_rows(count=None):
    block = CHANNELS // LANES
    if count is None:
        return pl.BlockSpec((CHUNK, LANES), lambda c: (c, block))
    return pl.BlockSpec((CHUNK, LANES), lambda c: (count - 1 - c, block))


def shape(dims, kind):
    return jax.ShapeDtypeStruct(dims, kind)


def cost(flops, moved):
    return pl.CostEstimate(flops=flops, bytes_accessed=moved, transcendentals=0)


def vm(dims, kind=F32):
    return pltpu.VMEM(dims, kind)


def pack(state, thru, kind):
    hi, lo = pieces(thru, 2)
    return jnp.concatenate([state.astype(kind), hi.astype(kind), lo.astype(kind)], axis=0)


def unpack(packed):
    packed = packed.astype(F32)
    return packed[:STATE], packed[STATE : STATE + 1] + packed[STATE + 1 : STATE + 2]


class Steps:
    def __init__(self, steps):
        self.steps, self.result, self.flight = steps, None, None
        self.advance(None)

    def advance(self, landed):
        try:
            self.flight = self.steps.send(landed)
        except StopIteration as end:
            self.flight, self.result = None, end.value

    def beside(self, *work):
        if self.flight is None:
            return work
        landed, work = lax.optimization_barrier((self.flight, work))
        self.advance(landed)
        return work

    def finish(self):
        while self.flight is not None:
            self.advance(self.flight)
        return self.result


def carry_states(packed, pairs, backward):
    packed = packed[: STATE + 2]
    kind = packed.dtype
    core = lax.axis_index("core")
    place = lax.axis_index("pair")
    half = packed.shape[1] // 2
    left, right = packed[:, :half], packed[:, half:]
    mine = jnp.where(core == 0, left, right)
    (theirs,) = yield [swap(jnp.where(core == 0, right, left), "core", 1)]
    leads = (core == 1) if backward else (core == 0)
    first, first_thru = unpack(jnp.where(leads, mine, theirs))
    second, second_thru = unpack(jnp.where(leads, theirs, mine))
    total, total_thru = second + second_thru * first, second_thru * first_thru
    before, before_thru = jnp.zeros_like(total), jnp.ones_like(total_thru)
    distance = 1
    while distance < pairs:
        (other,) = yield [swap(pack(total, total_thru, kind), "pair", distance)]
        other, other_thru = unpack(other)
        upper = (place & distance) != 0
        follows = jnp.logical_not(upper) if backward else upper
        before = jnp.where(follows, before + before_thru * other, before)
        before_thru = jnp.where(follows, before_thru * other_thru, before_thru)
        total = jnp.where(follows, total + total_thru * other, other + other_thru * total)
        total_thru = total_thru * other_thru
        distance *= 2
    after = first + first_thru * before
    keep = jnp.where(leads, before, after)
    (other,) = yield [swap(jnp.where(leads, after, before).astype(kind), "core", 1)]
    other = other.astype(F32)
    return jnp.where(
        core == 0,
        jnp.concatenate([keep, other], axis=1),
        jnp.concatenate([other, keep], axis=1),
    )


def shift(block, count, by):
    moved = [(i, i + by) for i in range(count) if 0 <= i + by < count]
    return lax.ppermute(block, ("pair", "core"), moved)


def swap(block, axis, mask):
    count = lax.axis_size(axis)
    return lax.ppermute(block, axis, [(i, i ^ mask) for i in range(count)])


def bit_orders(pairs):
    bits = list(range(pairs.bit_length() - 1))
    cut = len(bits) // 2
    return bits, bits[cut:] + bits[:cut]


def part_ids(pairs, fsdp):
    out = []
    for part, order in enumerate(bit_orders(pairs)):
        ids = [(0, k) for k in range(part * fsdp // 2, (part + 1) * fsdp // 2)]
        for b in order:
            ids = ids + [(mask ^ (1 << b), k) for mask, k in ids]
        out.append(ids)
    return out


def shard_of(place_ref, fsdp, mask, flip, k):
    return ((place_ref[0] ^ mask) * 2 + (place_ref[1] ^ flip)) * fsdp + (place_ref[2] ^ k)


def place_rows(place, held, r, fsdp, total):
    def body(place_ref, *refs):
        dst = refs[-1]
        for src, (_, flip, ids) in zip(refs, held):
            for at, (mask, k) in enumerate(ids):
                row = pl.multiple_of(shard_of(place_ref, fsdp, mask, flip, k) * r, r)
                dst[pl.ds(row, r), :] = src[at * r : (at + 1) * r, :]

    arrays = [a for a, _, _ in held]
    cols = arrays[0].shape[1]
    return pl.pallas_call(
        body,
        name="place_rows",
        in_specs=[pl.BlockSpec(memory_space=pltpu.SMEM)]
        + [pl.BlockSpec(memory_space=pltpu.VMEM)] * len(arrays),
        out_specs=pl.BlockSpec(memory_space=pltpu.VMEM),
        out_shape=jax.ShapeDtypeStruct((total, cols), arrays[0].dtype),
        compiler_params=PLAIN,
        cost_estimate=cost(0, 4 * total * cols),
    )(place, *arrays)


def pick_rows(place, arrays, r, pairs, fsdp):
    order = [i for ids in part_ids(pairs, fsdp) for i in ids]
    half = len(order) * r
    repeat = [a.shape[0] // (2 * half) for a in arrays]
    cols = sum(a.shape[1] * n for a, n in zip(arrays, repeat))

    def body(place_ref, *refs):
        for flip, dst in ((1, refs[-1]), (0, refs[-2])):
            for at, (mask, k) in enumerate(order):
                index = shard_of(place_ref, fsdp, mask, flip, k)
                col = 0
                for src, n in zip(refs, repeat):
                    for m in range(n):
                        row = pl.multiple_of((index * n + m) * r, r)
                        width = src.shape[1]
                        dst[at * r : (at + 1) * r, col : col + width] = src[pl.ds(row, r), :]
                        col += width

    return pl.pallas_call(
        body,
        name="pick_rows",
        in_specs=[pl.BlockSpec(memory_space=pltpu.SMEM)]
        + [pl.BlockSpec(memory_space=pltpu.VMEM)] * len(arrays),
        out_specs=[pl.BlockSpec(memory_space=pltpu.VMEM)] * 2,
        out_shape=[jax.ShapeDtypeStruct((half, cols), arrays[0].dtype)] * 2,
        compiler_params=PLAIN,
        cost_estimate=cost(0, 8 * half * cols),
    )(place, *arrays)


def unpack_weights(packed, r):
    total, model = packed.shape[0], (packed.shape[1] - DI) // 2
    if r % 16:
        tail = packed[:, DI:].reshape(total // r, r, 2, model).transpose(0, 2, 1, 3)
        return packed[:, :DI], tail.reshape(2 * total, model)
    per = min(total, 256)

    def body(src, gate, out):
        gate[...] = src[:, :DI]
        for i in range(per // r):
            for m in range(2):
                at, col = (2 * i + m) * r, DI + m * model
                out[at : at + r, :] = src[i * r : (i + 1) * r, col : col + model]

    return pl.pallas_call(
        body,
        name="unpack_weights",
        grid=(total // per,),
        in_specs=[rows(packed.shape[1], per=per)],
        out_specs=[rows(DI, per=per), rows(model, per=2 * per)],
        out_shape=[shape((total, DI), BF), shape((2 * total, model), BF)],
        compiler_params=PARAMS,
        cost_estimate=cost(0, 4 * total * packed.shape[1]),
    )(packed)


def gather_rows(w, place, pairs):
    r, fsdp = w.shape[0], lax.axis_size("fsdp")
    if r % 16:
        return lax.all_gather(w, ALL, axis=0, tiled=True)
    line = [w] + [swap(w, "fsdp", k) for k in range(1, fsdp)]
    yield line[1:]
    held = []
    for part, order in enumerate(bit_orders(pairs)):
        ks = range(part * fsdp // 2, (part + 1) * fsdp // 2)
        block = jnp.concatenate([line[k] for k in ks], axis=0)
        for b in order:
            block = jnp.concatenate([block, swap(block, "pair", 1 << b)], axis=0)
        held.append((block, 0, part_ids(pairs, fsdp)[part]))
    held = held + [(swap(a, "core", 1), 1, ids) for a, _, ids in held]
    return place_rows(place, held, r, fsdp, 2 * pairs * fsdp * r)


def reduce_rows(arrays, place, pairs):
    fsdp = lax.axis_size("fsdp")
    r = arrays[0].shape[0] // (2 * pairs * fsdp)
    if r % 16:
        return [
            lax.psum_scatter(g.astype(F32), ALL, scatter_dimension=0, tiled=True) for g in arrays
        ]
    keep, give = pick_rows(place, arrays, r, pairs, fsdp)
    (got,) = yield [swap(give, "core", 1)]
    half = keep.shape[0] // 2
    orders = bit_orders(pairs)
    blocks = []
    for part in range(2):
        at = slice(part * half, (part + 1) * half)
        blocks.append(keep[at].astype(F32) + got[at].astype(F32))
    for level in reversed(range(len(orders[0]))):
        cut = blocks[0].shape[0] // 2
        others = yield [
            swap(block[cut:].astype(BF), "pair", 1 << order[level])
            for block, order in zip(blocks, orders)
        ]
        blocks = [block[:cut] + other.astype(F32) for block, other in zip(blocks, others)]
    others = yield [
        swap(
            blocks[k // (fsdp // 2)][(k % (fsdp // 2)) * r :][:r].astype(BF), "fsdp", k
        )
        for k in range(1, fsdp)
    ]
    total = blocks[0][:r]
    for other in others:
        total = total + other.astype(F32)
    out, col = [], 0
    for g in arrays:
        width = g.shape[1]
        count = g.shape[0] // arrays[0].shape[0]
        out.append(
            jnp.concatenate(
                [total[:, col + m * width : col + (m + 1) * width] for m in range(count)], axis=0
            )
        )
        col += count * width
    return out


def links(pairs, fsdp):
    out = [("fsdp", 1 << b) for b in range(fsdp.bit_length() - 1)]
    out.append(("core", 1))
    return out + [("pair", 1 << b) for b in range(pairs.bit_length() - 1)]


def gather_small(vec, place_index, pairs, fsdp):
    block = vec[None]
    for axis, mask in links(pairs, fsdp):
        block = jnp.concatenate([block, swap(block, axis, mask)], axis=0)
    count = block.shape[0]
    index = jnp.arange(count)
    pick = (index[:, None] == (index[None] ^ place_index)).astype(BF)
    return jnp.dot(pick, block, preferred_element_type=F32)


def sum_small(block, pairs, fsdp):
    for axis, mask in links(pairs, fsdp):
        block = block + swap(block, axis, mask)
    return block


def hidden_of(tokens, gain):
    x = tokens.astype(F32)
    return (x * lax.rsqrt(jnp.mean(x * x, axis=-1, keepdims=True) + 1e-05) * gain).astype(BF)


def on_device(
    pairs, tokens, segment_ids, in_weight, out_weight, conv_weight, conv_bias, norm_gain,
    gate_gain, log_rate, skip_gain, step_bias, cotangent,
):
    tokens, labels, upstream = tokens[0], segment_ids[0], cotangent[0]
    count, model = tokens.shape
    chunks = count // CHUNK
    taps = conv_weight.shape[0]
    own = (conv_weight.size, conv_bias.size, norm_gain.size, gate_gain.size)
    fsdp = lax.axis_size("fsdp")
    place = jnp.stack([lax.axis_index(a) for a in ALL])
    device = (place[0] * 2 + place[1]) * fsdp + place[2]
    small = jnp.concatenate([conv_weight.reshape(-1), conv_bias, norm_gain, gate_gain])
    r, slot = in_weight.shape[0], MIX_WIDE - MIX
    small_rows = -(-small.size // slot)
    small = jnp.pad(small, (0, r * slot - small.size)).reshape(r, slot)
    mix_gather = Steps(
        gather_rows(jnp.concatenate([in_weight[:, DI:], small], axis=1), place, pairs)
    )
    in_weight, out_weight = mix_gather.beside(in_weight, out_weight)
    packed_weights = jnp.concatenate(
        [in_weight[:, :DI], out_weight[:r], out_weight[r:]], axis=1
    )
    packed_weights = lax.all_gather(packed_weights, ALL, axis=0, tiled=True)
    w_mix = mix_gather.finish()
    small = w_mix[:, MIX:].reshape(-1, r, slot)[:, :small_rows].reshape(-1, small_rows * slot)
    small = small[:, : sum(own)]
    conv_full = (
        small[:, : own[0]].reshape(-1, taps, own[0] // taps).transpose(1, 0, 2)
        .reshape(taps, CHANNELS).astype(F32)
    )
    at = own[0]
    bias_full = small[:, at : at + own[1]].reshape(1, CHANNELS).astype(F32)
    at += own[1]
    norm_full = small[:, at : at + own[2]].reshape(1, model).astype(F32)
    at += own[2]
    gate_full = small[:, at :].reshape(1, DI).astype(F32)
    w_gate, w_out = unpack_weights(packed_weights, r)

    expand = jnp.asarray(np.repeat(np.eye(HEADS), HEADDIM, axis=1), BF)
    skip_wide = jnp.repeat(skip_gain, HEADDIM)[None]
    rate, sbias = log_rate[None], step_bias[None]
    before = jnp.concatenate([jnp.broadcast_to(labels[:1], (3,)), labels])
    age = sum((before[3 - d : 3 - d + count] == labels).astype(F32) for d in (1, 2, 3))
    by_chunk = labels.reshape(chunks, CHUNK)
    last = by_chunk[:, -1:]
    prior = jnp.concatenate([by_chunk[:1, :1], last[:-1]], axis=0)
    info = jnp.stack(
        [
            labels.astype(F32),
            age,
            (by_chunk == prior).astype(F32).reshape(-1),
            (by_chunk == last).astype(F32).reshape(-1),
        ]
        + [jnp.zeros((count,), F32)] * 4,
        axis=1,
    )
    label_rows = labels.astype(F32).reshape(chunks, 1, CHUNK)
    row_spec = pl.BlockSpec((1, 1, CHUNK), lambda c: (c, 0, 0))

    tail = shift(tokens[count - 8 :], 2 * pairs, 1)
    hidden = hidden_of(tokens, norm_full)
    halo_hidden = hidden_of(tail, norm_full)
    mix = jnp.dot(hidden, w_mix, preferred_element_type=F32).astype(BF)
    halo = jnp.dot(halo_hidden, w_mix[:, :CHANNELS], preferred_element_type=F32)
    halo = halo.astype(BF).astype(F32)

    z, v, k, q, rc, rs, packed = pl.pallas_call(
        prep_kernel,
        name="conv_states",
        grid=(chunks,),
        in_specs=[
            rows(CHANNELS), raw_rows(), rows(8), whole((8, CHANNELS)), whole((taps, CHANNELS)),
            whole((1, CHANNELS)), whole((1, HEADS)), whole((1, HEADS)), whole((HEADS, DI)),
        ],
        out_specs=[
            rows(CHANNELS), rows(DI), rows(STATE), rows(STATE), rows(HEADS),
            rows(CHUNK, per=HEADS), whole((STATE + 16, DI)),
        ],
        out_shape=[
            shape((count, CHANNELS), BF), shape((count, DI), BF), shape((count, STATE), F32),
            shape((count, STATE), F32), shape((count, HEADS), F32),
            shape((chunks * HEADS, CHUNK), F32), shape((STATE + 16, DI), F32),
        ],
        scratch_shapes=[
            vm((STATE, DI)), vm((1, DI)), vm((8, CHANNELS)), vm((CHUNK, LANES)),
        ],
        compiler_params=PARAMS,
        cost_estimate=cost(10**9, 30 * 10**6),
    )(mix, mix, info, halo, conv_full, bias_full, rate, sbias, expand)

    forward = Steps(carry_states(packed, pairs, False))
    forward.beside()

    y_local = pl.pallas_call(
        intra_kernel,
        name="intra",
        grid=(chunks,),
        in_specs=[
            rows(STATE), rows(STATE), rows(DI), rows(HEADS), rows(CHUNK, per=HEADS), rows(8),
            row_spec,
        ],
        out_specs=rows(DI),
        out_shape=shape((count, DI), F32),
        compiler_params=PARAMS,
        cost_estimate=cost(10**9, 30 * 10**6),
    )(q, k, v, rc, rs, info, label_rows)

    (y_local,) = forward.beside(y_local)
    gate = jnp.dot(hidden, w_gate, preferred_element_type=F32).astype(BF)
    grad_normed = lax.dot_general(upstream, w_out, NT, preferred_element_type=F32)
    gate, grad_normed = forward.beside(gate, grad_normed)
    incoming = forward.finish()

    normed, dy, dy_lo, dgate, u, dq, states, packed_back, gate_sums = pl.pallas_call(
        gate_kernel,
        name="gate_norm",
        grid=(chunks,),
        in_specs=[
            rows(DI), rows(STATE), rows(STATE), rows(DI), rows(HEADS), rows(CHUNK, per=HEADS),
            rows(8), rows(DI), rows(DI), whole((STATE, DI)), whole((1, DI)), whole((1, DI)),
            whole((HEADS, DI)),
        ],
        out_specs=[
            rows(DI), rows(DI), rows(DI), rows(DI), rows(HEADS), rows(STATE), rows(DI),
            whole((STATE + 16, DI)), whole((16, DI)),
        ],
        out_shape=[
            shape((count, DI), BF), shape((count, DI), BF), shape((count, DI), BF),
            shape((count, DI), BF), shape((count, HEADS), F32), shape((count, STATE), F32),
            shape((chunks * STATE, DI), BF),
            shape((STATE + 16, DI), BF), shape((16, DI), F32),
        ],
        scratch_shapes=[
            vm((STATE, DI)), vm((STATE, DI)), vm((1, DI)), vm((CHUNK, DI)), vm((CHUNK, DI)),
            vm((16, DI)), vm((LANES, CHUNK)),
        ],
        compiler_params=PARAMS,
        cost_estimate=cost(10**9, 50 * 10**6),
    )(
        y_local, q, k, v, rc, rs, info, gate, grad_normed, incoming, skip_wide, gate_full,
        expand,
    )

    backward = Steps(carry_states(packed_back, pairs, True))
    grad_gate_w = lax.dot_general(hidden, dgate, TN, preferred_element_type=F32).astype(BF)
    (grad_gate_w,) = backward.beside(grad_gate_w)
    grad_out_w = lax.dot_general(normed, upstream, TN, preferred_element_type=F32).astype(BF)
    (grad_out_w,) = backward.beside(grad_out_w)
    gate_steps = Steps(reduce_rows([grad_gate_w, grad_out_w], place, pairs))
    block_out = (
        tokens.astype(F32) + jnp.dot(normed, w_out, preferred_element_type=F32)
    ).astype(BF)
    (block_out,) = gate_steps.beside(block_out)
    block_out, dy = backward.beside(block_out, dy)

    dv, uv, dq, dk = pl.pallas_call(
        intra_back_kernel,
        name="intra_back",
        grid=(chunks,),
        in_specs=[
            rows(STATE), rows(STATE), rows(DI), rows(DI), rows(DI), rows(HEADS),
            rows(CHUNK, per=HEADS), rows(8), row_spec, whole((HEADS, DI)), rows(STATE),
        ],
        out_specs=[rows(DI), rows(HEADS), rows(STATE), rows(STATE)],
        out_shape=[
            shape((count, DI), BF), shape((count, HEADS), F32), shape((count, STATE), F32),
            shape((count, STATE), F32),
        ],
        compiler_params=PARAMS,
        cost_estimate=cost(2 * 10**9, 40 * 10**6),
    )(q, k, v, dy, dy_lo, rc, rs, info, label_rows, expand, dq)

    (dv,) = gate_steps.beside(dv)
    (dv,) = backward.beside(dv)
    coming_back = backward.finish()
    back = functools.partial(rows, count=chunks)
    grad_mix, dhalo, conv_sums, head_sums = pl.pallas_call(
        back_kernel,
        name="states_conv_back",
        grid=(chunks,),
        in_specs=[
            back(CHANNELS), raw_rows(chunks), back(CHANNELS), back(DI), back(STATE), back(STATE),
            back(HEADS), back(CHUNK, per=HEADS), back(8), back(DI), back(DI), back(HEADS),
            back(HEADS), back(STATE), back(STATE), back(DI), whole((STATE, DI)),
            whole((8, CHANNELS)), whole((taps, CHANNELS)), whole((1, HEADS)),
            whole((1, HEADS)), whole((1, DI)), whole((HEADS, DI)),
        ],
        out_specs=[
            back(MIX_WIDE), whole((8, CHANNELS)), whole((40, CHANNELS)),
            whole((16, HEADS)),
        ],
        out_shape=[
            shape((count, MIX_WIDE), BF), shape((8, CHANNELS), F32),
            shape((40, CHANNELS), F32), shape((16, HEADS), F32),
        ],
        scratch_shapes=[
            vm((STATE, DI)), vm((8, CHANNELS)), vm((8, LANES)), vm((40, CHANNELS)),
            vm((16, HEADS)), vm((LANES, CHUNK)), vm((CHUNK, CHANNELS)),
        ],
        compiler_params=PARAMS,
        cost_estimate=cost(2 * 10**9, 60 * 10**6),
    )(
        mix, mix, z, v, k, q, rc, rs, info, dy, dv, uv, u, dq, dk, states, coming_back,
        halo, conv_full, rate, sbias, skip_wide, expand,
    )

    grad_mix, dhalo = gate_steps.beside(grad_mix, dhalo)
    edge = shift(dhalo, 2 * pairs, -1)
    edge = jnp.pad(edge, ((0, 0), (0, MIX_WIDE - CHANNELS)))
    fixed = (grad_mix[count - 8 :].astype(F32) + edge).astype(BF)
    grad_mix = lax.dynamic_update_slice(grad_mix, fixed, (count - 8, 0))
    grad_mix_w = lax.dot_general(hidden, grad_mix, TN, preferred_element_type=F32).astype(BF)
    mix_steps = Steps(reduce_rows([grad_mix_w], place, pairs))
    grad_hidden = lax.dot_general(dgate, w_gate, NT, preferred_element_type=F32)
    grad_hidden = grad_hidden + lax.dot_general(grad_mix, w_mix, NT, preferred_element_type=F32)

    x = tokens.astype(F32)
    inv = lax.rsqrt(jnp.mean(x * x, axis=-1, keepdims=True) + 1e-05)
    unit = x * inv
    scaled = grad_hidden * norm_full
    mean = jnp.mean(scaled * unit, axis=-1, keepdims=True)
    grad_tokens = upstream.astype(F32) + inv * (scaled - unit * mean)
    grad_norm = jnp.sum(grad_hidden * unit, axis=0)

    conv_sums = conv_sums.reshape(taps + 1, 8, CHANNELS).sum(axis=1)
    gate_sums = gate_sums.reshape(2, 8, DI).sum(axis=1)
    head_sums = head_sums.reshape(2, 8, HEADS).sum(axis=1)
    grad_skip = gate_sums[1].reshape(HEADS, HEADDIM).sum(axis=1)
    devices = 2 * pairs * fsdp
    parts = jnp.concatenate(
        [
            conv_sums.reshape(taps + 1, devices, own[1]).transpose(1, 0, 2).reshape(devices, -1),
            grad_norm.reshape(devices, -1),
            gate_sums[0].reshape(devices, -1),
            jnp.broadcast_to(
                jnp.concatenate([head_sums[0], grad_skip, head_sums[1]])[None],
                (devices, 3 * HEADS),
            ),
        ],
        axis=1,
    )
    mine = lax.dynamic_slice(
        sum_small(parts, pairs, fsdp), (device, 0), (1, parts.shape[1])
    )[0]
    ends = np.cumsum([own[0], own[1], own[2], own[3], HEADS, HEADS, HEADS]).tolist()
    conv_shard, bias_shard, norm_shard, gain_shard, *heads = [
        mine[a:b] for a, b in zip([0] + ends[:-1], ends)
    ]
    conv_shard = conv_shard.reshape(taps, -1)
    (mix_shard,) = mix_steps.finish()
    gate_shard, out_shard = gate_steps.finish()
    in_shard = jnp.concatenate([gate_shard, mix_shard[:, :MIX]], axis=1)
    return (
        block_out[None],
        grad_tokens[None],
        in_shard,
        out_shard,
        conv_shard,
        bias_shard,
        norm_shard,
        gain_shard,
        heads[0],
        heads[1],
        heads[2],
    )


def solution(mesh):
    seq, fsdp = mesh.devices.shape
    fine = Mesh(mesh.devices.reshape(seq // 2, 2, fsdp), ALL)
    line = ("pair", "core")
    tokens, labels, mat = P("fsdp", line, None), P("fsdp", line), P(ALL, None)
    weights = (mat, mat, P(None, ALL), P(ALL), P(ALL), P(ALL), P(), P(), P())
    return jax.shard_map(
        functools.partial(on_device, seq // 2),
        mesh=fine,
        in_specs=(tokens, labels) + weights + (tokens,),
        out_specs=(tokens, tokens) + weights,
        check_vma=False,
    )
```

```python
import functools

import jax
import jax.numpy as jnp
import numpy as np
from jax import lax
from jax.experimental import pallas as pl
from jax.experimental.pallas import tpu as pltpu
from jax.sharding import Mesh
from jax.sharding import PartitionSpec as P

HEADS = 32
HEADDIM = 64
STATE = 128
CHUNK = 128
LANES = 128
DI = HEADS * HEADDIM
CHANNELS = DI + 2 * STATE
WIDE = 512
MIX = CHANNELS + HEADS
MIX_WIDE = -(-MIX // 128) * 128
NEG = -1e30
LOG2E = 1.4426950408889634
ALL = ("pair", "core", "fsdp")
BF = jnp.bfloat16
F32 = jnp.float32
NT = (((1,), (1,)), ((), ()))
TN = (((0,), (0,)), ((), ()))
NN = (((1,), (0,)), ((), ()))
PARAMS = pltpu.CompilerParams(
    dimension_semantics=("arbitrary",), vmem_limit_bytes=56 * 1024 * 1024
)

PLAIN = pltpu.CompilerParams(vmem_limit_bytes=56 * 1024 * 1024)


def mm(a, b, dims=NN):
    return lax.dot_general(a, b, dims, preferred_element_type=F32)


def pieces(x, count):
    out = []
    for _ in range(count):
        part = x.astype(BF)
        out.append(part)
        x = x - part.astype(F32)
    return out


def spread(x, expand):
    both = jnp.concatenate(pieces(x, 2), axis=1)
    return mm(both, jnp.concatenate([expand, expand], axis=0))


def head_sum(x, expand):
    hi, lo = pieces(x, 2)
    if x.shape[1] == LANES:
        return mm(
            jnp.concatenate([hi, lo], axis=1), jnp.concatenate([expand, expand], axis=1), NT
        )
    return mm(hi, expand, NT) + mm(lo, expand, NT)


def cumulate(tri, x):
    a, b, c = pieces(x, 3)
    return mm(tri, a) + mm(tri, b) + mm(tri, c)


def mm3(a, b, dims=NN):
    a_hi, a_lo = pieces(a, 2)
    b_hi, b_lo = pieces(b, 2)
    return mm(a_hi, b_hi, dims) + (mm(a_lo, b_hi, dims) + mm(a_hi, b_lo, dims))


def sigmoid(x):
    return 0.5 * jnp.tanh(0.5 * x) + 0.5


def iota2(shape, dim):
    return lax.broadcasted_iota(jnp.int32, shape, dim)


def rows8(x):
    return jnp.sum(x.reshape(x.shape[0] // 8, 8, x.shape[1]), axis=0)


def prep_kernel(
    x_ref, raw_ref, info_ref, halo_ref, w_ref, b_ref, rate_ref, sbias_ref, e_ref,
    z_ref, v_ref, k_ref, q_ref, rc_ref, rs_ref, pack_ref,
    state, thru, carry, pad,
):
    step = pl.program_id(0)

    @pl.when(step == 0)
    def _():
        carry[...] = halo_ref[:8].astype(F32)
        state[...] = jnp.zeros_like(state)
        thru[...] = jnp.ones_like(thru)
        pad[...] = jnp.zeros_like(pad)

    info = info_ref[...]
    age = jnp.broadcast_to(info[:, 1:2], (CHUNK, LANES))
    masks = [(age >= d).astype(F32) for d in (1.0, 2.0, 3.0)]
    for tile in range(CHANNELS // LANES):
        sl = slice(tile * LANES, (tile + 1) * LANES)
        x = x_ref[:, sl].astype(F32)
        ext = jnp.concatenate([carry[:, sl], x], axis=0)
        z = b_ref[:, sl] + w_ref[3:4, sl] * x
        for d in (1, 2, 3):
            z = z + w_ref[3 - d : 4 - d, sl] * (ext[8 - d : 8 - d + CHUNK] * masks[d - 1])
        carry[:, sl] = x[CHUNK - 8 :]
        z_ref[:, sl] = z.astype(BF)
        value = z * sigmoid(z)
        if tile < DI // LANES:
            v_ref[:, sl] = value.astype(BF)
        elif tile == DI // LANES:
            k_ref[...] = value
        else:
            q_ref[...] = value

    raw = raw_ref[:, :HEADS].astype(F32) + sbias_ref[...]
    size = jnp.maximum(raw, 0.0) + jnp.log1p(jnp.exp(-jnp.abs(raw)))
    decay = -jnp.exp(rate_ref[...]) * size * LOG2E
    tri = (iota2((CHUNK, CHUNK), 0) >= iota2((CHUNK, CHUNK), 1)).astype(BF)
    running = cumulate(tri, decay)
    shifted = running - jnp.log2(jnp.maximum(size, 1e-37))
    rc_ref[...] = running
    pad[:, :HEADS] = shifted
    rs_ref[...] = pad[...].T[:HEADS]
    total = running[CHUNK - 1 :]
    weight = jnp.exp2(total - shifted) * info[:, 3:4]
    carried = jnp.exp2(running[CHUNK - 8 :]) * info[CHUNK - 8 :, 2:3]
    keys = k_ref[...].astype(BF)
    for g in range(DI // WIDE):
        sl = slice(g * WIDE, (g + 1) * WIDE)
        scaled = (mm(weight.astype(BF), e_ref[:, sl]) * v_ref[:, sl].astype(F32)).astype(BF)
        factor = spread(carried, e_ref[:, sl])[7:8]
        state[:, sl] = factor * state[:, sl] + mm(keys, scaled, TN)
        thru[:, sl] = factor * thru[:, sl]

    @pl.when(step == pl.num_programs(0) - 1)
    def _():
        pack_ref[:STATE] = state[...]
        hi, lo = pieces(thru[...], 2)
        row = iota2((16, DI), 0)
        pack_ref[STATE:] = jnp.where(
            row == 0, hi.astype(F32), jnp.where(row == 1, lo.astype(F32), 0.0)
        )


def shared(q_ref, k_ref, lc_ref, lr_ref):
    scores = mm3(q_ref[...], k_ref[...], NT)
    ok = (iota2((CHUNK, CHUNK), 0) >= iota2((CHUNK, CHUNK), 1)) & (
        lc_ref[:, 0:1] == lr_ref[0, 0:1, :]
    )
    bias = jnp.where(ok, 0.0, NEG)
    low_half = iota2((CHUNK, LANES), 1) < HEADDIM
    return scores, bias, low_half


def two_heads(v, low_half):
    zero = jnp.zeros_like(v)
    return jnp.concatenate([jnp.where(low_half, v, zero), jnp.where(low_half, zero, v)], axis=0)


def intra_kernel(q_ref, k_ref, v_ref, rc_ref, rs_ref, lc_ref, lr_ref, y_ref):
    scores, bias, low_half = shared(q_ref, k_ref, lc_ref, lr_ref)
    for pair in range(HEADS // 2):
        sl = slice(pair * LANES, (pair + 1) * LANES)
        mixing = []
        for h in (2 * pair, 2 * pair + 1):
            differ = (rc_ref[:, h : h + 1] - rs_ref[h : h + 1, :]) + bias
            mixing.append((jnp.exp2(differ) * scores).astype(BF))
        y_ref[:, sl] = mm(jnp.concatenate(mixing, axis=1), two_heads(v_ref[:, sl], low_half))


def gate_kernel(
    y_ref, q_ref, k_ref, v_ref, rc_ref, rs_ref, info_ref, gate_ref, dn_ref, sin_ref,
    skip_ref, gain_ref, e_ref,
    n_ref, dy_ref, dy_lo_ref, dgate_ref, u_ref, dq_ref, sc_ref, pack_ref, sums_ref,
    state, adj, reach, scan, enter, sums, pad,
):
    step = pl.program_id(0)

    @pl.when(step == 0)
    def _():
        state[...] = sin_ref[...]
        adj[...] = jnp.zeros_like(adj)
        reach[...] = jnp.ones_like(reach)
        sums[...] = jnp.zeros_like(sums)

    info = info_ref[...]
    running = rc_ref[...]
    pad[:HEADS] = rs_ref[...]
    shifted = pad[...].T[:, :HEADS]
    total = running[CHUNK - 1 :]
    weight = jnp.exp2(total - shifted) * info[:, 3:4]
    entering = jnp.exp2(running) * info[:, 2:3]
    queries, queries_lo = pieces(q_ref[...], 2)
    keys = k_ref[...].astype(BF)
    low_weight = weight.astype(BF)
    both_queries = jnp.concatenate([queries, queries_lo], axis=1)
    squares = jnp.zeros((CHUNK, LANES), F32)
    dots = jnp.zeros((CHUNK, LANES), F32)
    for g in range(DI // WIDE):
        sl = slice(g * WIDE, (g + 1) * WIDE)
        low_state, rest = pieces(state[:, sl], 2)
        sc_ref[:, sl] = low_state
        ent = spread(entering, e_ref[:, sl])
        enter[:, sl] = ent
        y = y_ref[:, sl] + ent * (
            mm(both_queries, jnp.concatenate([low_state, low_state], axis=0))
            + mm(queries, rest)
        )
        scan[:, sl] = y
        gate = gate_ref[:, sl].astype(F32)
        gated = (y + skip_ref[:, sl] * v_ref[:, sl].astype(F32)) * (gate * sigmoid(gate))
        square = gated * gated
        dot = dn_ref[:, sl] * gain_ref[:, sl] * gated
        for t in range(WIDE // LANES):
            part = slice(t * LANES, (t + 1) * LANES)
            squares = squares + square[:, part]
            dots = dots + dot[:, part]
    inv = lax.rsqrt(jnp.sum(squares, axis=1, keepdims=True) * (1.0 / DI) + 1e-05)
    coef = inv * inv * inv * jnp.sum(dots, axis=1, keepdims=True) * (1.0 / DI)
    head_dots = jnp.zeros((CHUNK, HEADS), F32)
    dq = jnp.zeros((CHUNK, STATE), F32)
    for g in range(DI // WIDE):
        sl = slice(g * WIDE, (g + 1) * WIDE)
        y = scan[:, sl]
        v = v_ref[:, sl].astype(F32)
        gate = gate_ref[:, sl].astype(F32)
        sig = sigmoid(gate)
        silu = gate * sig
        mixed = y + skip_ref[:, sl] * v
        gated = mixed * silu
        gain = gain_ref[:, sl]
        dn = dn_ref[:, sl]
        unit = gated * inv
        n_ref[:, sl] = (unit * gain).astype(BF)
        sums[0:8, sl] += rows8(dn * unit)
        dg = dn * gain * inv - gated * coef
        dgate_ref[:, sl] = (dg * mixed * (sig + silu * (1.0 - sig))).astype(BF)
        dy = dg * silu
        sums[8:16, sl] += rows8(dy * v)
        low, rest = pieces(dy, 2)
        dy_ref[:, sl] = low
        dy_lo_ref[:, sl] = rest
        head_dots = head_dots + head_sum(low.astype(F32) * y, e_ref[:, sl])
        ent = enter[:, sl]
        dy_in, dy_in_lo = pieces(ent * dy, 2)
        state_hi, state_lo = pieces(state[:, sl], 2)
        both = mm(dy_in, jnp.concatenate([state_hi, state_lo], axis=0), NT)
        dq = dq + (both[:, :STATE] + (both[:, STATE:] + mm(dy_in_lo, state_hi, NT)))
        adj[:, sl] += reach[:, sl] * mm(queries, dy_in, TN)
        factor = ent[CHUNK - 1 :]
        scaled = (mm(low_weight, e_ref[:, sl]) * v).astype(BF)
        state[:, sl] = factor * state[:, sl] + mm(keys, scaled, TN)
        reach[:, sl] = factor * reach[:, sl]
    u_ref[...] = head_dots
    dq_ref[...] = dq

    @pl.when(step == pl.num_programs(0) - 1)
    def _():
        pack_ref[:STATE] = adj[...].astype(BF)
        hi, lo = pieces(reach[...], 2)
        row = iota2((16, DI), 0)
        pack_ref[STATE:] = jnp.where(
            row == 0, hi.astype(F32), jnp.where(row == 1, lo.astype(F32), 0.0)
        ).astype(BF)
        sums_ref[...] = sums[...]


def intra_back_kernel(
    q_ref, k_ref, v_ref, dy_ref, dy_lo_ref, rc_ref, rs_ref, lc_ref, lr_ref, e_ref, dqin_ref,
    dv_ref, uv_ref, dq_ref, dk_ref,
):
    scores, bias, low_half = shared(q_ref, k_ref, lc_ref, lr_ref)
    dscores = jnp.zeros((CHUNK, CHUNK), F32)
    head_dots = jnp.zeros((CHUNK, HEADS), F32)
    for pair in range(HEADS // 2):
        sl = slice(pair * LANES, (pair + 1) * LANES)
        v = v_ref[:, sl]
        dy = dy_ref[:, sl]
        vv = two_heads(v, low_half)
        dmix = mm(
            jnp.concatenate([dy, dy_lo_ref[:, sl]], axis=1),
            jnp.concatenate([vv, vv], axis=1),
            NT,
        )
        mixing = []
        for i in range(2):
            h = 2 * pair + i
            differ = (rc_ref[:, h : h + 1] - rs_ref[h : h + 1, :]) + bias
            factor = jnp.exp2(differ)
            dscores = dscores + dmix[:, i * CHUNK : (i + 1) * CHUNK] * factor
            mixing.append((factor * scores).astype(BF).T)
        dv = mm(jnp.concatenate(mixing, axis=1), two_heads(dy, low_half))
        dv_ref[:, sl] = dv.astype(BF)
        head_dots = head_dots + head_sum(v.astype(F32) * dv, e_ref[:, sl])
    uv_ref[...] = head_dots
    dq_ref[...] = dqin_ref[...] + mm3(dscores, k_ref[...])
    dk_ref[...] = mm(dscores.astype(BF), q_ref[...].astype(BF), TN)


def back_kernel(
    x_ref, raw_ref, z_ref, v_ref, k_ref, q_ref, rc_ref, rs_ref, info_ref, dy_ref, dv_ref,
    uv_ref, u_ref, dq_ref, dk_ref, sc_ref, ain_ref, halo_ref, w_ref, rate_ref, sbias_ref,
    skip_ref, e_ref,
    dx_ref, dhalo_ref, csum_ref, hsum_ref,
    adj, nextz, nextage, csum, hsum, pad, dmix,
):
    step = pl.program_id(0)

    @pl.when(step == 0)
    def _():
        adj[...] = ain_ref[...]
        nextz[...] = jnp.zeros_like(nextz)
        nextage[...] = jnp.zeros_like(nextage)
        csum[...] = jnp.zeros_like(csum)
        hsum[...] = jnp.zeros_like(hsum)

    info = info_ref[...]
    running = rc_ref[...]
    pad[:HEADS] = rs_ref[...]
    shifted = pad[...].T[:, :HEADS]
    total = running[CHUNK - 1 :]
    weight = jnp.exp2(total - shifted) * info[:, 3:4]
    entering = jnp.exp2(running) * info[:, 2:3]
    queries = q_ref[...].astype(BF)
    keys = k_ref[...].astype(BF)
    dq = dq_ref[...]
    dk = dk_ref[...]
    low_weight = weight.astype(BF)
    low_entering = entering.astype(BF)
    later = jnp.zeros((CHUNK, HEADS), F32)
    through = jnp.zeros((8, HEADS), F32)
    for g in range(DI // WIDE):
        sl = slice(g * WIDE, (g + 1) * WIDE)
        e = e_ref[:, sl]
        v = v_ref[:, sl].astype(F32)
        dy = dy_ref[:, sl].astype(F32)
        wide = mm(low_weight, e)
        dy_in = (mm(low_entering, e) * dy).astype(BF)
        scaled = (wide * v).astype(BF)
        adjoint = adj[:, sl]
        low_adj = adjoint.astype(BF)
        states = sc_ref[:, sl]
        dv = wide * mm(keys, low_adj)
        later = later + mm((v * dv).astype(BF), e, NT)
        dk = dk + mm(scaled, low_adj, NT)
        factor = spread(entering[CHUNK - 8 :], e)[7:8]
        through = through + head_sum(rows8(adjoint * states.astype(F32)) * factor, e)
        adj[:, sl] = factor * adjoint + mm(queries, dy_in, TN)
        dmix[:, sl] = dv_ref[:, sl].astype(F32) + dv + skip_ref[:, sl] * dy
    dmix[:, DI : DI + STATE] = dk
    dmix[:, DI + STATE :] = dq

    age = jnp.broadcast_to(info[:, 1:2], (CHUNK, LANES))
    masks = [(age >= d).astype(F32) for d in (1.0, 2.0, 3.0)]
    ages = nextage[...]
    next_masks = [(ages >= d).astype(F32) for d in (1.0, 2.0, 3.0)]
    for tile in range(CHANNELS // LANES):
        sl = slice(tile * LANES, (tile + 1) * LANES)
        z = z_ref[:, sl].astype(F32)
        sig = sigmoid(z)
        dz = dmix[:, sl] * (sig + z * sig * (1.0 - sig))
        x = x_ref[:, sl].astype(F32)
        after = nextz[:, sl]
        dx = w_ref[3:4, sl] * dz
        csum[32:40, sl] += rows8(dz)
        csum[24:32, sl] += rows8(x * dz)
        for d in (1, 2, 3):
            ext = jnp.concatenate([dz * masks[d - 1], after * next_masks[d - 1]], axis=0)
            moved = ext[d : d + CHUNK]
            dx = dx + w_ref[3 - d : 4 - d, sl] * moved
            csum[8 * (3 - d) : 8 * (4 - d), sl] += rows8(x * moved)
        dx_ref[:, sl] = dx.astype(BF)
        nextz[:, sl] = dz[:8]

        @pl.when(step == pl.num_programs(0) - 1)
        def _():
            halo = halo_ref[:8, sl].astype(F32)
            acc = jnp.zeros((8, LANES), F32)
            for d in (1, 2, 3):
                ext = jnp.concatenate(
                    [jnp.zeros((8, LANES), F32), dz[:8] * masks[d - 1][:8]], axis=0
                )
                moved = ext[d : d + 8]
                acc = acc + w_ref[3 - d : 4 - d, sl] * moved
                csum[8 * (3 - d) : 8 * (4 - d), sl] += halo * moved
            dhalo_ref[:, sl] = acc
    nextage[...] = age[:8]

    row = iota2((CHUNK, CHUNK), 0)
    col = iota2((CHUNK, CHUNK), 1)
    ddecay = (
        cumulate((col >= row).astype(BF), u_ref[...] - uv_ref[...])
        + cumulate((col < row).astype(BF), later)
        + jnp.sum(through, axis=0, keepdims=True)
    )
    raw = raw_ref[:, :HEADS].astype(F32) + sbias_ref[...]
    sig = sigmoid(raw)
    size = jnp.maximum(raw, 0.0) + jnp.log1p(jnp.exp(-jnp.abs(raw)))
    rate = -jnp.exp(rate_ref[...])
    ratio = jnp.where(raw < -15.0, 1.0, sig / jnp.maximum(size, 1e-37))
    draw = (uv_ref[...] + later) * ratio + ddecay * rate * sig
    dx_ref[:, CHANNELS:MIX] = draw.astype(BF)
    dx_ref[:, MIX:] = jnp.zeros((CHUNK, MIX_WIDE - MIX), BF)
    hsum[0:8] += rows8(ddecay * rate * size)
    hsum[8:16] += rows8(draw)

    @pl.when(step == pl.num_programs(0) - 1)
    def _():
        csum_ref[...] = csum[...]
        hsum_ref[...] = hsum[...]


def whole(shape):
    return pl.BlockSpec(shape, lambda c: (0,) * len(shape))


def rows(width, count=None, per=CHUNK):
    if count is None:
        return pl.BlockSpec((per, width), lambda c: (c, 0))
    return pl.BlockSpec((per, width), lambda c: (count - 1 - c, 0))


def raw_rows(count=None):
    block = CHANNELS // LANES
    if count is None:
        return pl.BlockSpec((CHUNK, LANES), lambda c: (c, block))
    return pl.BlockSpec((CHUNK, LANES), lambda c: (count - 1 - c, block))


def shape(dims, kind):
    return jax.ShapeDtypeStruct(dims, kind)


def cost(flops, moved):
    return pl.CostEstimate(flops=flops, bytes_accessed=moved, transcendentals=0)


def vm(dims, kind=F32):
    return pltpu.VMEM(dims, kind)


def pack(state, thru, kind):
    hi, lo = pieces(thru, 2)
    return jnp.concatenate([state.astype(kind), hi.astype(kind), lo.astype(kind)], axis=0)


def unpack(packed):
    packed = packed.astype(F32)
    return packed[:STATE], packed[STATE : STATE + 1] + packed[STATE + 1 : STATE + 2]


class Steps:
    def __init__(self, steps):
        self.steps, self.result, self.flight = steps, None, None
        self.advance(None)

    def advance(self, landed):
        try:
            self.flight = self.steps.send(landed)
        except StopIteration as end:
            self.flight, self.result = None, end.value

    def beside(self, *work):
        if self.flight is None:
            return work
        landed, work = lax.optimization_barrier((self.flight, work))
        self.advance(landed)
        return work

    def finish(self):
        while self.flight is not None:
            self.advance(self.flight)
        return self.result


def carry_states(packed, pairs, backward):
    packed = packed[: STATE + 2]
    kind = packed.dtype
    core = lax.axis_index("core")
    place = lax.axis_index("pair")
    half = packed.shape[1] // 2
    left, right = packed[:, :half], packed[:, half:]
    mine = jnp.where(core == 0, left, right)
    (theirs,) = yield [swap(jnp.where(core == 0, right, left), "core", 1)]
    leads = (core == 1) if backward else (core == 0)
    first, first_thru = unpack(jnp.where(leads, mine, theirs))
    second, second_thru = unpack(jnp.where(leads, theirs, mine))
    total, total_thru = second + second_thru * first, second_thru * first_thru
    before, before_thru = jnp.zeros_like(total), jnp.ones_like(total_thru)
    distance = 1
    while distance < pairs:
        (other,) = yield [swap(pack(total, total_thru, kind), "pair", distance)]
        other, other_thru = unpack(other)
        upper = (place & distance) != 0
        follows = jnp.logical_not(upper) if backward else upper
        before = jnp.where(follows, before + before_thru * other, before)
        before_thru = jnp.where(follows, before_thru * other_thru, before_thru)
        total = jnp.where(follows, total + total_thru * other, other + other_thru * total)
        total_thru = total_thru * other_thru
        distance *= 2
    after = first + first_thru * before
    keep = jnp.where(leads, before, after)
    (other,) = yield [swap(jnp.where(leads, after, before).astype(kind), "core", 1)]
    other = other.astype(F32)
    return jnp.where(
        core == 0,
        jnp.concatenate([keep, other], axis=1),
        jnp.concatenate([other, keep], axis=1),
    )


def shift(block, count, by):
    moved = [(i, i + by) for i in range(count) if 0 <= i + by < count]
    return lax.ppermute(block, ("pair", "core"), moved)


def swap(block, axis, mask):
    count = lax.axis_size(axis)
    return lax.ppermute(block, axis, [(i, i ^ mask) for i in range(count)])


def bit_orders(pairs):
    bits = list(range(pairs.bit_length() - 1))
    cut = len(bits) // 2
    return bits, bits[cut:] + bits[:cut]


def part_ids(pairs, fsdp):
    out = []
    for part, order in enumerate(bit_orders(pairs)):
        ids = [(0, k) for k in range(part * fsdp // 2, (part + 1) * fsdp // 2)]
        for b in order:
            ids = ids + [(mask ^ (1 << b), k) for mask, k in ids]
        out.append(ids)
    return out


def shard_of(place_ref, fsdp, mask, flip, k):
    return ((place_ref[0] ^ mask) * 2 + (place_ref[1] ^ flip)) * fsdp + (place_ref[2] ^ k)


def place_rows(place, held, r, fsdp, total):
    def body(place_ref, *refs):
        dst = refs[-1]
        for src, (_, flip, ids) in zip(refs, held):
            for at, (mask, k) in enumerate(ids):
                row = pl.multiple_of(shard_of(place_ref, fsdp, mask, flip, k) * r, r)
                dst[pl.ds(row, r), :] = src[at * r : (at + 1) * r, :]

    arrays = [a for a, _, _ in held]
    cols = arrays[0].shape[1]
    return pl.pallas_call(
        body,
        name="place_rows",
        in_specs=[pl.BlockSpec(memory_space=pltpu.SMEM)]
        + [pl.BlockSpec(memory_space=pltpu.VMEM)] * len(arrays),
        out_specs=pl.BlockSpec(memory_space=pltpu.VMEM),
        out_shape=jax.ShapeDtypeStruct((total, cols), arrays[0].dtype),
        compiler_params=PLAIN,
        cost_estimate=cost(0, 4 * total * cols),
    )(place, *arrays)


def pick_rows(place, arrays, r, pairs, fsdp):
    order = [i for ids in part_ids(pairs, fsdp) for i in ids]
    half = len(order) * r
    repeat = [a.shape[0] // (2 * half) for a in arrays]
    cols = sum(a.shape[1] * n for a, n in zip(arrays, repeat))
    quarter = len(order) // 4

    def body(place_ref, *refs):
        for flip in range(2):
            for spot, (mask, k) in enumerate(order):
                index = shard_of(place_ref, fsdp, mask, flip, k)
                dst, at = refs[-1], spot
                if not flip:
                    dst, at = refs[spot // quarter - 5], spot % quarter
                col = 0
                for src, n in zip(refs, repeat):
                    for m in range(n):
                        row = pl.multiple_of((index * n + m) * r, r)
                        width = src.shape[1]
                        dst[at * r : (at + 1) * r, col : col + width] = src[pl.ds(row, r), :]
                        col += width

    return pl.pallas_call(
        body,
        name="pick_rows",
        in_specs=[pl.BlockSpec(memory_space=pltpu.SMEM)]
        + [pl.BlockSpec(memory_space=pltpu.VMEM)] * len(arrays),
        out_specs=[pl.BlockSpec(memory_space=pltpu.VMEM)] * 5,
        out_shape=[jax.ShapeDtypeStruct((half // 4, cols), arrays[0].dtype)] * 4
        + [jax.ShapeDtypeStruct((half, cols), arrays[0].dtype)],
        compiler_params=PLAIN,
        cost_estimate=cost(0, 8 * half * cols),
    )(place, *arrays)


def unpack_weights(packed, r):
    total, model = packed.shape[0], (packed.shape[1] - DI) // 2
    if r % 16:
        tail = packed[:, DI:].reshape(total // r, r, 2, model).transpose(0, 2, 1, 3)
        return packed[:, :DI], tail.reshape(2 * total, model)
    per = min(total, 256)

    def body(src, gate, out):
        gate[...] = src[:, :DI]
        for i in range(per // r):
            for m in range(2):
                at, col = (2 * i + m) * r, DI + m * model
                out[at : at + r, :] = src[i * r : (i + 1) * r, col : col + model]

    return pl.pallas_call(
        body,
        name="unpack_weights",
        grid=(total // per,),
        in_specs=[rows(packed.shape[1], per=per)],
        out_specs=[rows(DI, per=per), rows(model, per=2 * per)],
        out_shape=[shape((total, DI), BF), shape((2 * total, model), BF)],
        compiler_params=PARAMS,
        cost_estimate=cost(0, 4 * total * packed.shape[1]),
    )(packed)


def gather_rows(w, place, pairs):
    r, fsdp = w.shape[0], lax.axis_size("fsdp")
    if r % 16:
        return lax.all_gather(w, ALL, axis=0, tiled=True)
    line = [w] + [swap(w, "fsdp", k) for k in range(1, fsdp)]
    orders = bit_orders(pairs)
    blocks = [
        jnp.concatenate(line[part * fsdp // 2 : (part + 1) * fsdp // 2], axis=0)
        for part in range(2)
    ]
    for level in range(len(orders[0])):
        got = [swap(a, "pair", 1 << order[level]) for a, order in zip(blocks, orders)]
        if level == 0:
            got = yield got
        blocks = [jnp.concatenate([a, b], axis=0) for a, b in zip(blocks, got)]
    held = [(a, 0, ids) for a, ids in zip(blocks, part_ids(pairs, fsdp))]
    held = held + [(swap(a, "core", 1), 1, ids) for a, _, ids in held]
    return place_rows(place, held, r, fsdp, 2 * pairs * fsdp * r)


def reduce_rows(arrays, place, pairs):
    fsdp = lax.axis_size("fsdp")
    r = arrays[0].shape[0] // (2 * pairs * fsdp)
    if r % 16:
        return [
            lax.psum_scatter(g.astype(F32), ALL, scatter_dimension=0, tiled=True) for g in arrays
        ]
    *keep, give = pick_rows(place, arrays, r, pairs, fsdp)
    (got,) = yield [swap(give, "core", 1)]
    cut = keep[0].shape[0]
    orders = bit_orders(pairs)
    quarters = [
        (a.astype(F32) + got[i * cut : (i + 1) * cut].astype(F32)).astype(BF)
        for i, a in enumerate(keep)
    ]
    near, far = quarters[0::2], quarters[1::2]
    for level in reversed(range(len(orders[0]))):
        others = yield [
            swap(a, "pair", 1 << order[level]) for a, order in zip(far, orders)
        ]
        blocks = [(a, b) for a, b in zip(near, others)]
        if level:
            cut = near[0].shape[0] // 2
            near = [
                (a[:cut].astype(F32) + b[:cut].astype(F32)).astype(BF) for a, b in blocks
            ]
            far = [(a[cut:].astype(F32) + b[cut:].astype(F32)).astype(BF) for a, b in blocks]
    blocks = [a.astype(F32) + b.astype(F32) for a, b in blocks]
    others = yield [
        swap(
            blocks[k // (fsdp // 2)][(k % (fsdp // 2)) * r :][:r].astype(BF), "fsdp", k
        )
        for k in range(1, fsdp)
    ]
    total = blocks[0][:r]
    for other in others:
        total = total + other.astype(F32)
    out, col = [], 0
    for g in arrays:
        width = g.shape[1]
        count = g.shape[0] // arrays[0].shape[0]
        out.append(
            jnp.concatenate(
                [total[:, col + m * width : col + (m + 1) * width] for m in range(count)], axis=0
            )
        )
        col += count * width
    return out


def links(pairs, fsdp):
    out = [("fsdp", 1 << b) for b in range(fsdp.bit_length() - 1)]
    out.append(("core", 1))
    return out + [("pair", 1 << b) for b in range(pairs.bit_length() - 1)]


def gather_small(vec, place_index, pairs, fsdp):
    block = vec[None]
    for axis, mask in links(pairs, fsdp):
        block = jnp.concatenate([block, swap(block, axis, mask)], axis=0)
    count = block.shape[0]
    index = jnp.arange(count)
    pick = (index[:, None] == (index[None] ^ place_index)).astype(BF)
    return jnp.dot(pick, block, preferred_element_type=F32)


def sum_small(block, pairs, fsdp):
    for axis, mask in links(pairs, fsdp):
        block = block + swap(block, axis, mask)
    return block


def hidden_of(tokens, gain):
    x = tokens.astype(F32)
    return (x * lax.rsqrt(jnp.mean(x * x, axis=-1, keepdims=True) + 1e-05) * gain).astype(BF)


def on_device(
    pairs, tokens, segment_ids, in_weight, out_weight, conv_weight, conv_bias, norm_gain,
    gate_gain, log_rate, skip_gain, step_bias, cotangent,
):
    tokens, labels, upstream = tokens[0], segment_ids[0], cotangent[0]
    count, model = tokens.shape
    chunks = count // CHUNK
    taps = conv_weight.shape[0]
    own = (conv_weight.size, conv_bias.size, norm_gain.size, gate_gain.size)
    fsdp = lax.axis_size("fsdp")
    place = jnp.stack([lax.axis_index(a) for a in ALL])
    device = (place[0] * 2 + place[1]) * fsdp + place[2]
    small = jnp.concatenate([conv_weight.reshape(-1), conv_bias, norm_gain, gate_gain])
    r, slot = in_weight.shape[0], MIX_WIDE - MIX
    small_rows = -(-small.size // slot)
    small = jnp.pad(small, (0, r * slot - small.size)).reshape(r, slot)
    mix_gather = Steps(
        gather_rows(jnp.concatenate([in_weight[:, DI:], small], axis=1), place, pairs)
    )
    in_weight, out_weight = mix_gather.beside(in_weight, out_weight)
    packed_weights = jnp.concatenate(
        [in_weight[:, :DI], out_weight[:r], out_weight[r:]], axis=1
    )
    packed_weights = lax.all_gather(packed_weights, ALL, axis=0, tiled=True)
    w_mix = mix_gather.finish()
    small = w_mix[:, MIX:].reshape(-1, r, slot)[:, :small_rows].reshape(-1, small_rows * slot)
    small = small[:, : sum(own)]
    conv_full = (
        small[:, : own[0]].reshape(-1, taps, own[0] // taps).transpose(1, 0, 2)
        .reshape(taps, CHANNELS).astype(F32)
    )
    at = own[0]
    bias_full = small[:, at : at + own[1]].reshape(1, CHANNELS).astype(F32)
    at += own[1]
    norm_full = small[:, at : at + own[2]].reshape(1, model).astype(F32)
    at += own[2]
    gate_full = small[:, at :].reshape(1, DI).astype(F32)
    w_gate, w_out = unpack_weights(packed_weights, r)

    expand = jnp.asarray(np.repeat(np.eye(HEADS), HEADDIM, axis=1), BF)
    skip_wide = jnp.repeat(skip_gain, HEADDIM)[None]
    rate, sbias = log_rate[None], step_bias[None]
    before = jnp.concatenate([jnp.broadcast_to(labels[:1], (3,)), labels])
    age = sum((before[3 - d : 3 - d + count] == labels).astype(F32) for d in (1, 2, 3))
    by_chunk = labels.reshape(chunks, CHUNK)
    last = by_chunk[:, -1:]
    prior = jnp.concatenate([by_chunk[:1, :1], last[:-1]], axis=0)
    info = jnp.stack(
        [
            labels.astype(F32),
            age,
            (by_chunk == prior).astype(F32).reshape(-1),
            (by_chunk == last).astype(F32).reshape(-1),
        ]
        + [jnp.zeros((count,), F32)] * 4,
        axis=1,
    )
    label_rows = labels.astype(F32).reshape(chunks, 1, CHUNK)
    row_spec = pl.BlockSpec((1, 1, CHUNK), lambda c: (c, 0, 0))
    halo_spec = pl.BlockSpec((16, CHANNELS), lambda c: (count // 16, 0))

    tail = shift(tokens[count - 8 :], 2 * pairs, 1)
    tail = jnp.concatenate([tail, jnp.zeros_like(tail)], axis=0)
    hidden = hidden_of(tokens, norm_full)
    mix = jnp.dot(
        hidden_of(jnp.concatenate([tokens, tail], axis=0), norm_full), w_mix,
        preferred_element_type=F32,
    ).astype(BF)

    z, v, k, q, rc, rs, packed = pl.pallas_call(
        prep_kernel,
        name="conv_states",
        grid=(chunks,),
        in_specs=[
            rows(CHANNELS), raw_rows(), rows(8), halo_spec, whole((taps, CHANNELS)),
            whole((1, CHANNELS)), whole((1, HEADS)), whole((1, HEADS)), whole((HEADS, DI)),
        ],
        out_specs=[
            rows(CHANNELS), rows(DI), rows(STATE), rows(STATE), rows(HEADS),
            rows(CHUNK, per=HEADS), whole((STATE + 16, DI)),
        ],
        out_shape=[
            shape((count, CHANNELS), BF), shape((count, DI), BF), shape((count, STATE), F32),
            shape((count, STATE), F32), shape((count, HEADS), F32),
            shape((chunks * HEADS, CHUNK), F32), shape((STATE + 16, DI), F32),
        ],
        scratch_shapes=[
            vm((STATE, DI)), vm((1, DI)), vm((8, CHANNELS)), vm((CHUNK, LANES)),
        ],
        compiler_params=PARAMS,
        cost_estimate=cost(10**9, 30 * 10**6),
    )(mix, mix, info, mix, conv_full, bias_full, rate, sbias, expand)

    forward = Steps(carry_states(packed, pairs, False))
    forward.beside()

    y_local = pl.pallas_call(
        intra_kernel,
        name="intra",
        grid=(chunks,),
        in_specs=[
            rows(STATE), rows(STATE), rows(DI), rows(HEADS), rows(CHUNK, per=HEADS), rows(8),
            row_spec,
        ],
        out_specs=rows(DI),
        out_shape=shape((count, DI), F32),
        compiler_params=PARAMS,
        cost_estimate=cost(10**9, 30 * 10**6),
    )(q, k, v, rc, rs, info, label_rows)

    (y_local,) = forward.beside(y_local)
    gate = jnp.dot(hidden, w_gate, preferred_element_type=F32).astype(BF)
    grad_normed = lax.dot_general(upstream, w_out, NT, preferred_element_type=F32)
    gate, grad_normed = forward.beside(gate, grad_normed)
    incoming = forward.finish()

    normed, dy, dy_lo, dgate, u, dq, states, packed_back, gate_sums = pl.pallas_call(
        gate_kernel,
        name="gate_norm",
        grid=(chunks,),
        in_specs=[
            rows(DI), rows(STATE), rows(STATE), rows(DI), rows(HEADS), rows(CHUNK, per=HEADS),
            rows(8), rows(DI), rows(DI), whole((STATE, DI)), whole((1, DI)), whole((1, DI)),
            whole((HEADS, DI)),
        ],
        out_specs=[
            rows(DI), rows(DI), rows(DI), rows(DI), rows(HEADS), rows(STATE), rows(DI),
            whole((STATE + 16, DI)), whole((16, DI)),
        ],
        out_shape=[
            shape((count, DI), BF), shape((count, DI), BF), shape((count, DI), BF),
            shape((count, DI), BF), shape((count, HEADS), F32), shape((count, STATE), F32),
            shape((chunks * STATE, DI), BF),
            shape((STATE + 16, DI), BF), shape((16, DI), F32),
        ],
        scratch_shapes=[
            vm((STATE, DI)), vm((STATE, DI)), vm((1, DI)), vm((CHUNK, DI)), vm((CHUNK, DI)),
            vm((16, DI)), vm((LANES, CHUNK)),
        ],
        compiler_params=PARAMS,
        cost_estimate=cost(10**9, 50 * 10**6),
    )(
        y_local, q, k, v, rc, rs, info, gate, grad_normed, incoming, skip_wide, gate_full,
        expand,
    )

    backward = Steps(carry_states(packed_back, pairs, True))
    grad_gate_w = lax.dot_general(hidden, dgate, TN, preferred_element_type=F32).astype(BF)
    (grad_gate_w,) = backward.beside(grad_gate_w)
    grad_out_w = lax.dot_general(normed, upstream, TN, preferred_element_type=F32).astype(BF)
    (grad_out_w,) = backward.beside(grad_out_w)
    gate_steps = Steps(reduce_rows([grad_gate_w, grad_out_w], place, pairs))
    block_out = (
        tokens.astype(F32) + jnp.dot(normed, w_out, preferred_element_type=F32)
    ).astype(BF)
    (block_out,) = gate_steps.beside(block_out)
    block_out, dy = backward.beside(block_out, dy)

    dv, uv, dq, dk = pl.pallas_call(
        intra_back_kernel,
        name="intra_back",
        grid=(chunks,),
        in_specs=[
            rows(STATE), rows(STATE), rows(DI), rows(DI), rows(DI), rows(HEADS),
            rows(CHUNK, per=HEADS), rows(8), row_spec, whole((HEADS, DI)), rows(STATE),
        ],
        out_specs=[rows(DI), rows(HEADS), rows(STATE), rows(STATE)],
        out_shape=[
            shape((count, DI), BF), shape((count, HEADS), F32), shape((count, STATE), F32),
            shape((count, STATE), F32),
        ],
        compiler_params=PARAMS,
        cost_estimate=cost(2 * 10**9, 40 * 10**6),
    )(q, k, v, dy, dy_lo, rc, rs, info, label_rows, expand, dq)

    (dv,) = gate_steps.beside(dv)
    (dv,) = backward.beside(dv)
    coming_back = backward.finish()
    back = functools.partial(rows, count=chunks)
    grad_mix, dhalo, conv_sums, head_sums = pl.pallas_call(
        back_kernel,
        name="states_conv_back",
        grid=(chunks,),
        in_specs=[
            back(CHANNELS), raw_rows(chunks), back(CHANNELS), back(DI), back(STATE), back(STATE),
            back(HEADS), back(CHUNK, per=HEADS), back(8), back(DI), back(DI), back(HEADS),
            back(HEADS), back(STATE), back(STATE), back(DI), whole((STATE, DI)),
            halo_spec, whole((taps, CHANNELS)), whole((1, HEADS)),
            whole((1, HEADS)), whole((1, DI)), whole((HEADS, DI)),
        ],
        out_specs=[
            back(MIX_WIDE), whole((8, CHANNELS)), whole((40, CHANNELS)),
            whole((16, HEADS)),
        ],
        out_shape=[
            shape((count, MIX_WIDE), BF), shape((8, CHANNELS), F32),
            shape((40, CHANNELS), F32), shape((16, HEADS), F32),
        ],
        scratch_shapes=[
            vm((STATE, DI)), vm((8, CHANNELS)), vm((8, LANES)), vm((40, CHANNELS)),
            vm((16, HEADS)), vm((LANES, CHUNK)), vm((CHUNK, CHANNELS)),
        ],
        compiler_params=PARAMS,
        cost_estimate=cost(2 * 10**9, 60 * 10**6),
    )(
        mix, mix, z, v, k, q, rc, rs, info, dy, dv, uv, u, dq, dk, states, coming_back,
        mix, conv_full, rate, sbias, skip_wide, expand,
    )

    grad_mix, dhalo = gate_steps.beside(grad_mix, dhalo)
    edge = shift(dhalo, 2 * pairs, -1)
    edge = jnp.pad(edge, ((0, 0), (0, MIX_WIDE - CHANNELS)))
    fixed = (grad_mix[count - 8 :].astype(F32) + edge).astype(BF)
    grad_mix = lax.dynamic_update_slice(grad_mix, fixed, (count - 8, 0))
    grad_mix_w = lax.dot_general(hidden, grad_mix, TN, preferred_element_type=F32).astype(BF)
    mix_steps = Steps(reduce_rows([grad_mix_w], place, pairs))
    grad_hidden = lax.dot_general(dgate, w_gate, NT, preferred_element_type=F32)
    grad_hidden = grad_hidden + lax.dot_general(grad_mix, w_mix, NT, preferred_element_type=F32)

    x = tokens.astype(F32)
    inv = lax.rsqrt(jnp.mean(x * x, axis=-1, keepdims=True) + 1e-05)
    unit = x * inv
    scaled = grad_hidden * norm_full
    mean = jnp.mean(scaled * unit, axis=-1, keepdims=True)
    grad_tokens = upstream.astype(F32) + inv * (scaled - unit * mean)
    grad_norm = jnp.sum(grad_hidden * unit, axis=0)

    conv_sums = conv_sums.reshape(taps + 1, 8, CHANNELS).sum(axis=1)
    gate_sums = gate_sums.reshape(2, 8, DI).sum(axis=1)
    head_sums = head_sums.reshape(2, 8, HEADS).sum(axis=1)
    grad_skip = gate_sums[1].reshape(HEADS, HEADDIM).sum(axis=1)
    devices = 2 * pairs * fsdp
    parts = jnp.concatenate(
        [
            conv_sums.reshape(taps + 1, devices, own[1]).transpose(1, 0, 2).reshape(devices, -1),
            grad_norm.reshape(devices, -1),
            gate_sums[0].reshape(devices, -1),
            jnp.broadcast_to(
                jnp.concatenate([head_sums[0], grad_skip, head_sums[1]])[None],
                (devices, 3 * HEADS),
            ),
        ],
        axis=1,
    )
    mine = lax.dynamic_slice(
        sum_small(parts, pairs, fsdp), (device, 0), (1, parts.shape[1])
    )[0]
    ends = np.cumsum([own[0], own[1], own[2], own[3], HEADS, HEADS, HEADS]).tolist()
    conv_shard, bias_shard, norm_shard, gain_shard, *heads = [
        mine[a:b] for a, b in zip([0] + ends[:-1], ends)
    ]
    conv_shard = conv_shard.reshape(taps, -1)
    (mix_shard,) = mix_steps.finish()
    gate_shard, out_shard = gate_steps.finish()
    in_shard = jnp.concatenate([gate_shard, mix_shard[:, :MIX]], axis=1)
    return (
        block_out[None],
        grad_tokens[None],
        in_shard,
        out_shard,
        conv_shard,
        bias_shard,
        norm_shard,
        gain_shard,
        heads[0],
        heads[1],
        heads[2],
    )


def solution(mesh):
    seq, fsdp = mesh.devices.shape
    fine = Mesh(mesh.devices.reshape(seq // 2, 2, fsdp), ALL)
    line = ("pair", "core")
    tokens, labels, mat = P("fsdp", line, None), P("fsdp", line), P(ALL, None)
    weights = (mat, mat, P(None, ALL), P(ALL), P(ALL), P(ALL), P(), P(), P())
    return jax.shard_map(
        functools.partial(on_device, seq // 2),
        mesh=fine,
        in_specs=(tokens, labels) + weights + (tokens,),
        out_specs=(tokens, tokens) + weights,
        check_vma=False,
    )
```

```python
import functools

import jax
import jax.numpy as jnp
import numpy as np
from jax import lax
from jax.experimental import pallas as pl
from jax.experimental.pallas import tpu as pltpu
from jax.sharding import Mesh
from jax.sharding import PartitionSpec as P

HEADS = 32
HEADDIM = 64
STATE = 128
CHUNK = 128
LANES = 128
DI = HEADS * HEADDIM
CHANNELS = DI + 2 * STATE
WIDE = 256
MIX = CHANNELS + HEADS
MIX_WIDE = -(-MIX // 128) * 128
NEG = -1e30
LOG2E = 1.4426950408889634
ALL = ("pair", "core", "fsdp")
BF = jnp.bfloat16
F32 = jnp.float32
NT = (((1,), (1,)), ((), ()))
TN = (((0,), (0,)), ((), ()))
NN = (((1,), (0,)), ((), ()))
PARAMS = pltpu.CompilerParams(
    dimension_semantics=("arbitrary",), vmem_limit_bytes=56 * 1024 * 1024
)

PLAIN = pltpu.CompilerParams(vmem_limit_bytes=56 * 1024 * 1024)


def mm(a, b, dims=NN):
    return lax.dot_general(a, b, dims, preferred_element_type=F32)


def pieces(x, count):
    out = []
    for _ in range(count):
        part = x.astype(BF)
        out.append(part)
        x = x - part.astype(F32)
    return out


def spread(x, expand):
    both = jnp.concatenate(pieces(x, 2), axis=1)
    return mm(both, jnp.concatenate([expand, expand], axis=0))


def head_sum(x, expand):
    hi, lo = pieces(x, 2)
    if x.shape[1] == LANES:
        return mm(
            jnp.concatenate([hi, lo], axis=1), jnp.concatenate([expand, expand], axis=1), NT
        )
    return mm(hi, expand, NT) + mm(lo, expand, NT)


def cumulate(tri, x):
    a, b, c = pieces(x, 3)
    return mm(tri, a) + mm(tri, b) + mm(tri, c)


def mm3(a, b, dims=NN):
    a_hi, a_lo = pieces(a, 2)
    b_hi, b_lo = pieces(b, 2)
    return mm(a_hi, b_hi, dims) + (mm(a_lo, b_hi, dims) + mm(a_hi, b_lo, dims))


def sigmoid(x):
    return 0.5 * jnp.tanh(0.5 * x) + 0.5


def iota2(shape, dim):
    return lax.broadcasted_iota(jnp.int32, shape, dim)


def rows8(x):
    return jnp.sum(x.reshape(x.shape[0] // 8, 8, x.shape[1]), axis=0)


def prep_kernel(
    x_ref, raw_ref, info_ref, halo_ref, w_ref, b_ref, rate_ref, sbias_ref, e_ref,
    z_ref, v_ref, k_ref, q_ref, rc_ref, rs_ref, pack_ref,
    state, thru, carry, pad,
):
    step = pl.program_id(0)

    @pl.when(step == 0)
    def _():
        carry[...] = halo_ref[:8].astype(F32)
        state[...] = jnp.zeros_like(state)
        thru[...] = jnp.ones_like(thru)
        pad[...] = jnp.zeros_like(pad)

    info = info_ref[...]
    age = jnp.broadcast_to(info[:, 1:2], (CHUNK, LANES))
    masks = [(age >= d).astype(F32) for d in (1.0, 2.0, 3.0)]
    for tile in range(CHANNELS // LANES):
        sl = slice(tile * LANES, (tile + 1) * LANES)
        x = x_ref[:, sl].astype(F32)
        ext = jnp.concatenate([carry[:, sl], x], axis=0)
        z = b_ref[:, sl] + w_ref[3:4, sl] * x
        for d in (1, 2, 3):
            z = z + w_ref[3 - d : 4 - d, sl] * (ext[8 - d : 8 - d + CHUNK] * masks[d - 1])
        carry[:, sl] = x[CHUNK - 8 :]
        z_ref[:, sl] = z.astype(BF)
        value = z * sigmoid(z)
        if tile < DI // LANES:
            v_ref[:, sl] = value.astype(BF)
        elif tile == DI // LANES:
            k_ref[...] = value
        else:
            q_ref[...] = value

    raw = raw_ref[:, :HEADS].astype(F32) + sbias_ref[...]
    size = jnp.maximum(raw, 0.0) + jnp.log1p(jnp.exp(-jnp.abs(raw)))
    decay = -jnp.exp(rate_ref[...]) * size * LOG2E
    tri = (iota2((CHUNK, CHUNK), 0) >= iota2((CHUNK, CHUNK), 1)).astype(BF)
    running = cumulate(tri, decay)
    shifted = running - jnp.log2(jnp.maximum(size, 1e-37))
    rc_ref[...] = running
    pad[:, :HEADS] = shifted
    rs_ref[...] = pad[...].T[:HEADS]
    total = running[CHUNK - 1 :]
    weight = jnp.exp2(total - shifted) * info[:, 3:4]
    carried = jnp.exp2(running[CHUNK - 8 :]) * info[CHUNK - 8 :, 2:3]
    keys = k_ref[...].astype(BF)
    for g in range(DI // WIDE):
        sl = slice(g * WIDE, (g + 1) * WIDE)
        scaled = (mm(weight.astype(BF), e_ref[:, sl]) * v_ref[:, sl].astype(F32)).astype(BF)
        factor = spread(carried, e_ref[:, sl])[7:8]
        state[:, sl] = factor * state[:, sl] + mm(keys, scaled, TN)
        thru[:, sl] = factor * thru[:, sl]

    @pl.when(step == pl.num_programs(0) - 1)
    def _():
        pack_ref[:STATE] = state[...]
        hi, lo = pieces(thru[...], 2)
        row = iota2((16, DI), 0)
        pack_ref[STATE:] = jnp.where(
            row == 0, hi.astype(F32), jnp.where(row == 1, lo.astype(F32), 0.0)
        )


def shared(q_ref, k_ref, lc_ref, lr_ref):
    scores = mm3(q_ref[...], k_ref[...], NT)
    ok = (iota2((CHUNK, CHUNK), 0) >= iota2((CHUNK, CHUNK), 1)) & (
        lc_ref[:, 0:1] == lr_ref[0, 0:1, :]
    )
    bias = jnp.where(ok, 0.0, NEG)
    low_half = iota2((CHUNK, LANES), 1) < HEADDIM
    return scores, bias, low_half


def two_heads(v, low_half):
    zero = jnp.zeros_like(v)
    return jnp.concatenate([jnp.where(low_half, v, zero), jnp.where(low_half, zero, v)], axis=0)


def intra_kernel(q_ref, k_ref, v_ref, rc_ref, rs_ref, lc_ref, lr_ref, y_ref):
    scores, bias, low_half = shared(q_ref, k_ref, lc_ref, lr_ref)
    for pair in range(HEADS // 2):
        sl = slice(pair * LANES, (pair + 1) * LANES)
        mixing = []
        for h in (2 * pair, 2 * pair + 1):
            differ = (rc_ref[:, h : h + 1] - rs_ref[h : h + 1, :]) + bias
            mixing.append((jnp.exp2(differ) * scores).astype(BF))
        y_ref[:, sl] = mm(jnp.concatenate(mixing, axis=1), two_heads(v_ref[:, sl], low_half))


def gate_kernel(
    y_ref, q_ref, k_ref, v_ref, rc_ref, rs_ref, info_ref, gate_ref, dn_ref, sin_ref,
    skip_ref, gain_ref, e_ref,
    n_ref, dy_ref, dy_lo_ref, dgate_ref, u_ref, dq_ref, sc_ref, pack_ref, sums_ref,
    state, adj, reach, scan, enter, sums, pad,
):
    step = pl.program_id(0)

    @pl.when(step == 0)
    def _():
        state[...] = sin_ref[...]
        adj[...] = jnp.zeros_like(adj)
        reach[...] = jnp.ones_like(reach)
        sums[...] = jnp.zeros_like(sums)

    info = info_ref[...]
    running = rc_ref[...]
    pad[:HEADS] = rs_ref[...]
    shifted = pad[...].T[:, :HEADS]
    total = running[CHUNK - 1 :]
    weight = jnp.exp2(total - shifted) * info[:, 3:4]
    entering = jnp.exp2(running) * info[:, 2:3]
    queries, queries_lo = pieces(q_ref[...], 2)
    keys = k_ref[...].astype(BF)
    low_weight = weight.astype(BF)
    both_queries = jnp.concatenate([queries, queries_lo], axis=1)
    squares = jnp.zeros((CHUNK, LANES), F32)
    dots = jnp.zeros((CHUNK, LANES), F32)
    for g in range(DI // WIDE):
        sl = slice(g * WIDE, (g + 1) * WIDE)
        low_state, rest = pieces(state[:, sl], 2)
        sc_ref[:, sl] = low_state
        ent = spread(entering, e_ref[:, sl])
        enter[:, sl] = ent
        y = y_ref[:, sl] + ent * (
            mm(both_queries, jnp.concatenate([low_state, low_state], axis=0))
            + mm(queries, rest)
        )
        scan[:, sl] = y
        gate = gate_ref[:, sl].astype(F32)
        gated = (y + skip_ref[:, sl] * v_ref[:, sl].astype(F32)) * (gate * sigmoid(gate))
        square = gated * gated
        dot = dn_ref[:, sl] * gain_ref[:, sl] * gated
        for t in range(WIDE // LANES):
            part = slice(t * LANES, (t + 1) * LANES)
            squares = squares + square[:, part]
            dots = dots + dot[:, part]
    inv = lax.rsqrt(jnp.sum(squares, axis=1, keepdims=True) * (1.0 / DI) + 1e-05)
    coef = inv * inv * inv * jnp.sum(dots, axis=1, keepdims=True) * (1.0 / DI)
    head_dots = jnp.zeros((CHUNK, HEADS), F32)
    dq = jnp.zeros((CHUNK, STATE), F32)
    for g in range(DI // WIDE):
        sl = slice(g * WIDE, (g + 1) * WIDE)
        y = scan[:, sl]
        v = v_ref[:, sl].astype(F32)
        gate = gate_ref[:, sl].astype(F32)
        sig = sigmoid(gate)
        silu = gate * sig
        mixed = y + skip_ref[:, sl] * v
        gated = mixed * silu
        gain = gain_ref[:, sl]
        dn = dn_ref[:, sl]
        unit = gated * inv
        n_ref[:, sl] = (unit * gain).astype(BF)
        sums[0:8, sl] += rows8(dn * unit)
        dg = dn * gain * inv - gated * coef
        dgate_ref[:, sl] = (dg * mixed * (sig + silu * (1.0 - sig))).astype(BF)
        dy = dg * silu
        sums[8:16, sl] += rows8(dy * v)
        low, rest = pieces(dy, 2)
        dy_ref[:, sl] = low
        dy_lo_ref[:, sl] = rest
        head_dots = head_dots + head_sum(low.astype(F32) * y, e_ref[:, sl])
        ent = enter[:, sl]
        dy_in, dy_in_lo = pieces(ent * dy, 2)
        state_hi, state_lo = pieces(state[:, sl], 2)
        both = mm(dy_in, jnp.concatenate([state_hi, state_lo], axis=0), NT)
        dq = dq + (both[:, :STATE] + (both[:, STATE:] + mm(dy_in_lo, state_hi, NT)))
        adj[:, sl] += reach[:, sl] * mm(queries, dy_in, TN)
        factor = ent[CHUNK - 1 :]
        scaled = (mm(low_weight, e_ref[:, sl]) * v).astype(BF)
        state[:, sl] = factor * state[:, sl] + mm(keys, scaled, TN)
        reach[:, sl] = factor * reach[:, sl]
    u_ref[...] = head_dots
    dq_ref[...] = dq

    @pl.when(step == pl.num_programs(0) - 1)
    def _():
        pack_ref[:STATE] = adj[...].astype(BF)
        hi, lo = pieces(reach[...], 2)
        row = iota2((16, DI), 0)
        pack_ref[STATE:] = jnp.where(
            row == 0, hi.astype(F32), jnp.where(row == 1, lo.astype(F32), 0.0)
        ).astype(BF)
        sums_ref[...] = sums[...]


def intra_back_kernel(
    q_ref, k_ref, v_ref, dy_ref, dy_lo_ref, rc_ref, rs_ref, lc_ref, lr_ref, e_ref, dqin_ref,
    dv_ref, uv_ref, dq_ref, dk_ref,
):
    scores, bias, low_half = shared(q_ref, k_ref, lc_ref, lr_ref)
    dscores = jnp.zeros((CHUNK, CHUNK), F32)
    head_dots = jnp.zeros((CHUNK, HEADS), F32)
    for pair in range(HEADS // 2):
        sl = slice(pair * LANES, (pair + 1) * LANES)
        v = v_ref[:, sl]
        dy = dy_ref[:, sl]
        vv = two_heads(v, low_half)
        dmix = mm(
            jnp.concatenate([dy, dy_lo_ref[:, sl]], axis=1),
            jnp.concatenate([vv, vv], axis=1),
            NT,
        )
        mixing = []
        for i in range(2):
            h = 2 * pair + i
            differ = (rc_ref[:, h : h + 1] - rs_ref[h : h + 1, :]) + bias
            factor = jnp.exp2(differ)
            dscores = dscores + dmix[:, i * CHUNK : (i + 1) * CHUNK] * factor
            mixing.append((factor * scores).astype(BF).T)
        dv = mm(jnp.concatenate(mixing, axis=1), two_heads(dy, low_half))
        dv_ref[:, sl] = dv.astype(BF)
        head_dots = head_dots + head_sum(v.astype(F32) * dv, e_ref[:, sl])
    uv_ref[...] = head_dots
    dq_ref[...] = dqin_ref[...] + mm3(dscores, k_ref[...])
    dk_ref[...] = mm(dscores.astype(BF), q_ref[...].astype(BF), TN)


def back_kernel(
    x_ref, raw_ref, z_ref, v_ref, k_ref, q_ref, rc_ref, rs_ref, info_ref, dy_ref, dv_ref,
    uv_ref, u_ref, dq_ref, dk_ref, sc_ref, ain_ref, halo_ref, w_ref, rate_ref, sbias_ref,
    skip_ref, e_ref,
    dx_ref, dhalo_ref, csum_ref, hsum_ref,
    adj, nextz, nextage, csum, hsum, pad, dmix,
):
    step = pl.program_id(0)

    @pl.when(step == 0)
    def _():
        adj[...] = ain_ref[...]
        nextz[...] = jnp.zeros_like(nextz)
        nextage[...] = jnp.zeros_like(nextage)
        csum[...] = jnp.zeros_like(csum)
        hsum[...] = jnp.zeros_like(hsum)

    info = info_ref[...]
    running = rc_ref[...]
    pad[:HEADS] = rs_ref[...]
    shifted = pad[...].T[:, :HEADS]
    total = running[CHUNK - 1 :]
    weight = jnp.exp2(total - shifted) * info[:, 3:4]
    entering = jnp.exp2(running) * info[:, 2:3]
    queries = q_ref[...].astype(BF)
    keys = k_ref[...].astype(BF)
    dq = dq_ref[...]
    dk = dk_ref[...]
    low_weight = weight.astype(BF)
    low_entering = entering.astype(BF)
    later = jnp.zeros((CHUNK, HEADS), F32)
    through = jnp.zeros((8, HEADS), F32)
    for g in range(DI // WIDE):
        sl = slice(g * WIDE, (g + 1) * WIDE)
        e = e_ref[:, sl]
        v = v_ref[:, sl].astype(F32)
        dy = dy_ref[:, sl].astype(F32)
        wide = mm(low_weight, e)
        dy_in = (mm(low_entering, e) * dy).astype(BF)
        scaled = (wide * v).astype(BF)
        adjoint = adj[:, sl]
        low_adj = adjoint.astype(BF)
        states = sc_ref[:, sl]
        dv = wide * mm(keys, low_adj)
        later = later + mm((v * dv).astype(BF), e, NT)
        dk = dk + mm(scaled, low_adj, NT)
        factor = spread(entering[CHUNK - 8 :], e)[7:8]
        through = through + head_sum(rows8(adjoint * states.astype(F32)) * factor, e)
        adj[:, sl] = factor * adjoint + mm(queries, dy_in, TN)
        dmix[:, sl] = dv_ref[:, sl].astype(F32) + dv + skip_ref[:, sl] * dy
    dmix[:, DI : DI + STATE] = dk
    dmix[:, DI + STATE :] = dq

    age = jnp.broadcast_to(info[:, 1:2], (CHUNK, LANES))
    masks = [(age >= d).astype(F32) for d in (1.0, 2.0, 3.0)]
    ages = nextage[...]
    next_masks = [(ages >= d).astype(F32) for d in (1.0, 2.0, 3.0)]
    for tile in range(CHANNELS // LANES):
        sl = slice(tile * LANES, (tile + 1) * LANES)
        z = z_ref[:, sl].astype(F32)
        sig = sigmoid(z)
        dz = dmix[:, sl] * (sig + z * sig * (1.0 - sig))
        x = x_ref[:, sl].astype(F32)
        after = nextz[:, sl]
        dx = w_ref[3:4, sl] * dz
        csum[32:40, sl] += rows8(dz)
        csum[24:32, sl] += rows8(x * dz)
        for d in (1, 2, 3):
            ext = jnp.concatenate([dz * masks[d - 1], after * next_masks[d - 1]], axis=0)
            moved = ext[d : d + CHUNK]
            dx = dx + w_ref[3 - d : 4 - d, sl] * moved
            csum[8 * (3 - d) : 8 * (4 - d), sl] += rows8(x * moved)
        dx_ref[:, sl] = dx.astype(BF)
        nextz[:, sl] = dz[:8]

        @pl.when(step == pl.num_programs(0) - 1)
        def _():
            halo = halo_ref[:8, sl].astype(F32)
            acc = jnp.zeros((8, LANES), F32)
            for d in (1, 2, 3):
                ext = jnp.concatenate(
                    [jnp.zeros((8, LANES), F32), dz[:8] * masks[d - 1][:8]], axis=0
                )
                moved = ext[d : d + 8]
                acc = acc + w_ref[3 - d : 4 - d, sl] * moved
                csum[8 * (3 - d) : 8 * (4 - d), sl] += halo * moved
            dhalo_ref[:, sl] = acc
    nextage[...] = age[:8]

    row = iota2((CHUNK, CHUNK), 0)
    col = iota2((CHUNK, CHUNK), 1)
    ddecay = (
        cumulate((col >= row).astype(BF), u_ref[...] - uv_ref[...])
        + cumulate((col < row).astype(BF), later)
        + jnp.sum(through, axis=0, keepdims=True)
    )
    raw = raw_ref[:, :HEADS].astype(F32) + sbias_ref[...]
    sig = sigmoid(raw)
    size = jnp.maximum(raw, 0.0) + jnp.log1p(jnp.exp(-jnp.abs(raw)))
    rate = -jnp.exp(rate_ref[...])
    ratio = jnp.where(raw < -15.0, 1.0, sig / jnp.maximum(size, 1e-37))
    draw = (uv_ref[...] + later) * ratio + ddecay * rate * sig
    dx_ref[:, CHANNELS:MIX] = draw.astype(BF)
    dx_ref[:, MIX:] = jnp.zeros((CHUNK, MIX_WIDE - MIX), BF)
    hsum[0:8] += rows8(ddecay * rate * size)
    hsum[8:16] += rows8(draw)

    @pl.when(step == pl.num_programs(0) - 1)
    def _():
        csum_ref[...] = csum[...]
        hsum_ref[...] = hsum[...]


def whole(shape):
    return pl.BlockSpec(shape, lambda c: (0,) * len(shape))


def rows(width, count=None, per=CHUNK):
    if count is None:
        return pl.BlockSpec((per, width), lambda c: (c, 0))
    return pl.BlockSpec((per, width), lambda c: (count - 1 - c, 0))


def raw_rows(count=None):
    block = CHANNELS // LANES
    if count is None:
        return pl.BlockSpec((CHUNK, LANES), lambda c: (c, block))
    return pl.BlockSpec((CHUNK, LANES), lambda c: (count - 1 - c, block))


def shape(dims, kind):
    return jax.ShapeDtypeStruct(dims, kind)


def cost(flops, moved):
    return pl.CostEstimate(flops=flops, bytes_accessed=moved, transcendentals=0)


def vm(dims, kind=F32):
    return pltpu.VMEM(dims, kind)


def pack(state, thru, kind):
    hi, lo = pieces(thru, 2)
    return jnp.concatenate([state.astype(kind), hi.astype(kind), lo.astype(kind)], axis=0)


def unpack(packed):
    packed = packed.astype(F32)
    return packed[:STATE], packed[STATE : STATE + 1] + packed[STATE + 1 : STATE + 2]


class Steps:
    def __init__(self, steps):
        self.steps, self.result, self.flight = steps, None, None
        self.advance(None)

    def advance(self, landed):
        try:
            self.flight = self.steps.send(landed)
        except StopIteration as end:
            self.flight, self.result = None, end.value

    def beside(self, *work):
        if self.flight is None:
            return work
        landed, work = lax.optimization_barrier((self.flight, work))
        self.advance(landed)
        return work

    def finish(self):
        while self.flight is not None:
            self.advance(self.flight)
        return self.result


def carry_states(packed, pairs, backward):
    packed = packed[: STATE + 2]
    kind = packed.dtype
    core = lax.axis_index("core")
    place = lax.axis_index("pair")
    half = packed.shape[1] // 2
    left, right = packed[:, :half], packed[:, half:]
    mine = jnp.where(core == 0, left, right)
    (theirs,) = yield [swap(jnp.where(core == 0, right, left), "core", 1)]
    leads = (core == 1) if backward else (core == 0)
    first, first_thru = unpack(jnp.where(leads, mine, theirs))
    second, second_thru = unpack(jnp.where(leads, theirs, mine))
    total, total_thru = second + second_thru * first, second_thru * first_thru
    before, before_thru = jnp.zeros_like(total), jnp.ones_like(total_thru)
    distance = 1
    while distance < pairs:
        (other,) = yield [swap(pack(total, total_thru, kind), "pair", distance)]
        other, other_thru = unpack(other)
        upper = (place & distance) != 0
        follows = jnp.logical_not(upper) if backward else upper
        before = jnp.where(follows, before + before_thru * other, before)
        before_thru = jnp.where(follows, before_thru * other_thru, before_thru)
        total = jnp.where(follows, total + total_thru * other, other + other_thru * total)
        total_thru = total_thru * other_thru
        distance *= 2
    after = first + first_thru * before
    keep = jnp.where(leads, before, after)
    (other,) = yield [swap(jnp.where(leads, after, before).astype(kind), "core", 1)]
    other = other.astype(F32)
    return jnp.where(
        core == 0,
        jnp.concatenate([keep, other], axis=1),
        jnp.concatenate([other, keep], axis=1),
    )


def shift(block, count, by):
    moved = [(i, i + by) for i in range(count) if 0 <= i + by < count]
    return lax.ppermute(block, ("pair", "core"), moved)


def swap(block, axis, mask):
    count = lax.axis_size(axis)
    return lax.ppermute(block, axis, [(i, i ^ mask) for i in range(count)])


def bit_orders(pairs):
    bits = list(range(pairs.bit_length() - 1))
    cut = len(bits) // 2
    return bits, bits[cut:] + bits[:cut]


def part_ids(pairs, fsdp):
    out = []
    for part, order in enumerate(bit_orders(pairs)):
        ids = [(0, k) for k in range(part * fsdp // 2, (part + 1) * fsdp // 2)]
        for b in order:
            ids = ids + [(mask ^ (1 << b), k) for mask, k in ids]
        out.append(ids)
    return out


def shard_of(place_ref, fsdp, mask, flip, k):
    return ((place_ref[0] ^ mask) * 2 + (place_ref[1] ^ flip)) * fsdp + (place_ref[2] ^ k)


def place_rows(place, held, r, fsdp, total):
    def body(place_ref, *refs):
        dst = refs[-1]
        for src, (_, flip, ids) in zip(refs, held):
            for at, (mask, k) in enumerate(ids):
                row = pl.multiple_of(shard_of(place_ref, fsdp, mask, flip, k) * r, r)
                dst[pl.ds(row, r), :] = src[at * r : (at + 1) * r, :]

    arrays = [a for a, _, _ in held]
    cols = arrays[0].shape[1]
    return pl.pallas_call(
        body,
        name="place_rows",
        in_specs=[pl.BlockSpec(memory_space=pltpu.SMEM)]
        + [pl.BlockSpec(memory_space=pltpu.VMEM)] * len(arrays),
        out_specs=pl.BlockSpec(memory_space=pltpu.VMEM),
        out_shape=jax.ShapeDtypeStruct((total, cols), arrays[0].dtype),
        compiler_params=PLAIN,
        cost_estimate=cost(0, 4 * total * cols),
    )(place, *arrays)


def pick_rows(place, arrays, r, pairs, fsdp):
    order = [i for ids in part_ids(pairs, fsdp) for i in ids]
    half = len(order) * r
    repeat = [a.shape[0] // (2 * half) for a in arrays]
    cols = sum(a.shape[1] * n for a, n in zip(arrays, repeat))
    quarter = len(order) // 4

    def body(place_ref, *refs):
        for flip in range(2):
            for spot, (mask, k) in enumerate(order):
                index = shard_of(place_ref, fsdp, mask, flip, k)
                dst, at = refs[-1], spot
                if not flip:
                    dst, at = refs[spot // quarter - 5], spot % quarter
                col = 0
                for src, n in zip(refs, repeat):
                    for m in range(n):
                        row = pl.multiple_of((index * n + m) * r, r)
                        width = src.shape[1]
                        dst[at * r : (at + 1) * r, col : col + width] = src[pl.ds(row, r), :]
                        col += width

    return pl.pallas_call(
        body,
        name="pick_rows",
        in_specs=[pl.BlockSpec(memory_space=pltpu.SMEM)]
        + [pl.BlockSpec(memory_space=pltpu.VMEM)] * len(arrays),
        out_specs=[pl.BlockSpec(memory_space=pltpu.VMEM)] * 5,
        out_shape=[jax.ShapeDtypeStruct((half // 4, cols), arrays[0].dtype)] * 4
        + [jax.ShapeDtypeStruct((half, cols), arrays[0].dtype)],
        compiler_params=PLAIN,
        cost_estimate=cost(0, 8 * half * cols),
    )(place, *arrays)


def unpack_weights(packed, r):
    total, model = packed.shape[0], (packed.shape[1] - DI) // 2
    if r % 16:
        tail = packed[:, DI:].reshape(total // r, r, 2, model).transpose(0, 2, 1, 3)
        return packed[:, :DI], tail.reshape(2 * total, model)
    per = min(total, 256)

    def body(src, gate, out):
        gate[...] = src[:, :DI]
        for i in range(per // r):
            for m in range(2):
                at, col = (2 * i + m) * r, DI + m * model
                out[at : at + r, :] = src[i * r : (i + 1) * r, col : col + model]

    return pl.pallas_call(
        body,
        name="unpack_weights",
        grid=(total // per,),
        in_specs=[rows(packed.shape[1], per=per)],
        out_specs=[rows(DI, per=per), rows(model, per=2 * per)],
        out_shape=[shape((total, DI), BF), shape((2 * total, model), BF)],
        compiler_params=PARAMS,
        cost_estimate=cost(0, 4 * total * packed.shape[1]),
    )(packed)


def gather_rows(w, place, pairs):
    r, fsdp = w.shape[0], lax.axis_size("fsdp")
    if r % 16:
        return lax.all_gather(w, ALL, axis=0, tiled=True)
    line = [w] + [swap(w, "fsdp", k) for k in range(1, fsdp)]
    orders = bit_orders(pairs)
    blocks = [
        jnp.concatenate(line[part * fsdp // 2 : (part + 1) * fsdp // 2], axis=0)
        for part in range(2)
    ]
    for level in range(len(orders[0])):
        got = [swap(a, "pair", 1 << order[level]) for a, order in zip(blocks, orders)]
        if level == 0:
            got = yield got
        blocks = [jnp.concatenate([a, b], axis=0) for a, b in zip(blocks, got)]
    held = [(a, 0, ids) for a, ids in zip(blocks, part_ids(pairs, fsdp))]
    held = held + [(swap(a, "core", 1), 1, ids) for a, _, ids in held]
    return place_rows(place, held, r, fsdp, 2 * pairs * fsdp * r)


def reduce_rows(arrays, place, pairs):
    fsdp = lax.axis_size("fsdp")
    r = arrays[0].shape[0] // (2 * pairs * fsdp)
    if r % 16:
        return [
            lax.psum_scatter(g.astype(F32), ALL, scatter_dimension=0, tiled=True) for g in arrays
        ]
    *keep, give = pick_rows(place, arrays, r, pairs, fsdp)
    (give,) = yield [give]
    (got,) = yield [swap(give, "core", 1)]
    cut = keep[0].shape[0]
    orders = bit_orders(pairs)
    quarters = [
        (a.astype(F32) + got[i * cut : (i + 1) * cut].astype(F32)).astype(BF)
        for i, a in enumerate(keep)
    ]
    near, far = quarters[0::2], quarters[1::2]
    for level in reversed(range(len(orders[0]))):
        others = yield [
            swap(a, "pair", 1 << order[level]) for a, order in zip(far, orders)
        ]
        blocks = [(a, b) for a, b in zip(near, others)]
        if level:
            cut = near[0].shape[0] // 2
            near = [
                (a[:cut].astype(F32) + b[:cut].astype(F32)).astype(BF) for a, b in blocks
            ]
            far = [(a[cut:].astype(F32) + b[cut:].astype(F32)).astype(BF) for a, b in blocks]
    blocks = [a.astype(F32) + b.astype(F32) for a, b in blocks]
    others = yield [
        swap(
            blocks[k // (fsdp // 2)][(k % (fsdp // 2)) * r :][:r].astype(BF), "fsdp", k
        )
        for k in range(1, fsdp)
    ]
    total = blocks[0][:r]
    for other in others:
        total = total + other.astype(F32)
    out, col = [], 0
    for g in arrays:
        width = g.shape[1]
        count = g.shape[0] // arrays[0].shape[0]
        out.append(
            jnp.concatenate(
                [total[:, col + m * width : col + (m + 1) * width] for m in range(count)], axis=0
            )
        )
        col += count * width
    return out


def links(pairs, fsdp):
    out = [("fsdp", 1 << b) for b in range(fsdp.bit_length() - 1)]
    out.append(("core", 1))
    return out + [("pair", 1 << b) for b in range(pairs.bit_length() - 1)]


def gather_small(vec, place_index, pairs, fsdp):
    block = vec[None]
    for axis, mask in links(pairs, fsdp):
        block = jnp.concatenate([block, swap(block, axis, mask)], axis=0)
    count = block.shape[0]
    index = jnp.arange(count)
    pick = (index[:, None] == (index[None] ^ place_index)).astype(BF)
    return jnp.dot(pick, block, preferred_element_type=F32)


def sum_small(block, pairs, fsdp):
    for axis, mask in links(pairs, fsdp):
        block = block + swap(block, axis, mask)
    return block


def hidden_of(tokens, gain):
    x = tokens.astype(F32)
    return (x * lax.rsqrt(jnp.mean(x * x, axis=-1, keepdims=True) + 1e-05) * gain).astype(BF)


def on_device(
    pairs, tokens, segment_ids, in_weight, out_weight, conv_weight, conv_bias, norm_gain,
    gate_gain, log_rate, skip_gain, step_bias, cotangent,
):
    tokens, labels, upstream = tokens[0], segment_ids[0], cotangent[0]
    count, model = tokens.shape
    chunks = count // CHUNK
    taps = conv_weight.shape[0]
    own = (conv_weight.size, conv_bias.size, norm_gain.size, gate_gain.size)
    fsdp = lax.axis_size("fsdp")
    place = jnp.stack([lax.axis_index(a) for a in ALL])
    device = (place[0] * 2 + place[1]) * fsdp + place[2]
    small = jnp.concatenate([conv_weight.reshape(-1), conv_bias, norm_gain, gate_gain])
    r, slot = in_weight.shape[0], MIX_WIDE - MIX
    small_rows = -(-small.size // slot)
    small = jnp.pad(small, (0, r * slot - small.size)).reshape(r, slot)
    mix_gather = Steps(
        gather_rows(jnp.concatenate([in_weight[:, DI:], small], axis=1), place, pairs)
    )
    packed_weights = jnp.concatenate(
        [in_weight[:, :DI], out_weight[:r], out_weight[r:]], axis=1
    )
    (packed_weights,) = mix_gather.beside(packed_weights)
    packed_weights = lax.all_gather(packed_weights, ALL, axis=0, tiled=True)
    w_mix = mix_gather.finish()
    small = w_mix[:, MIX:].reshape(-1, r, slot)[:, :small_rows].reshape(-1, small_rows * slot)
    small = small[:, : sum(own)]
    conv_full = (
        small[:, : own[0]].reshape(-1, taps, own[0] // taps).transpose(1, 0, 2)
        .reshape(taps, CHANNELS).astype(F32)
    )
    at = own[0]
    bias_full = small[:, at : at + own[1]].reshape(1, CHANNELS).astype(F32)
    at += own[1]
    norm_full = small[:, at : at + own[2]].reshape(1, model).astype(F32)
    at += own[2]
    gate_full = small[:, at :].reshape(1, DI).astype(F32)
    w_gate, w_out = unpack_weights(packed_weights, r)

    expand = jnp.asarray(np.repeat(np.eye(HEADS), HEADDIM, axis=1), BF)
    skip_wide = jnp.repeat(skip_gain, HEADDIM)[None]
    rate, sbias = log_rate[None], step_bias[None]
    before = jnp.concatenate([jnp.broadcast_to(labels[:1], (3,)), labels])
    age = sum((before[3 - d : 3 - d + count] == labels).astype(F32) for d in (1, 2, 3))
    by_chunk = labels.reshape(chunks, CHUNK)
    last = by_chunk[:, -1:]
    prior = jnp.concatenate([by_chunk[:1, :1], last[:-1]], axis=0)
    info = jnp.stack(
        [
            labels.astype(F32),
            age,
            (by_chunk == prior).astype(F32).reshape(-1),
            (by_chunk == last).astype(F32).reshape(-1),
        ]
        + [jnp.zeros((count,), F32)] * 4,
        axis=1,
    )
    label_rows = labels.astype(F32).reshape(chunks, 1, CHUNK)
    row_spec = pl.BlockSpec((1, 1, CHUNK), lambda c: (c, 0, 0))
    halo_spec = pl.BlockSpec((16, CHANNELS), lambda c: (count // 16, 0))

    tail = shift(tokens[count - 8 :], 2 * pairs, 1)
    tail = jnp.concatenate([tail, jnp.zeros_like(tail)], axis=0)
    hidden = hidden_of(tokens, norm_full)
    mix = jnp.dot(
        hidden_of(jnp.concatenate([tokens, tail], axis=0), norm_full), w_mix,
        preferred_element_type=F32,
    ).astype(BF)

    z, v, k, q, rc, rs, packed = pl.pallas_call(
        prep_kernel,
        name="conv_states",
        grid=(chunks,),
        in_specs=[
            rows(CHANNELS), raw_rows(), rows(8), halo_spec, whole((taps, CHANNELS)),
            whole((1, CHANNELS)), whole((1, HEADS)), whole((1, HEADS)), whole((HEADS, DI)),
        ],
        out_specs=[
            rows(CHANNELS), rows(DI), rows(STATE), rows(STATE), rows(HEADS),
            rows(CHUNK, per=HEADS), whole((STATE + 16, DI)),
        ],
        out_shape=[
            shape((count, CHANNELS), BF), shape((count, DI), BF), shape((count, STATE), F32),
            shape((count, STATE), F32), shape((count, HEADS), F32),
            shape((chunks * HEADS, CHUNK), F32), shape((STATE + 16, DI), F32),
        ],
        scratch_shapes=[
            vm((STATE, DI)), vm((1, DI)), vm((8, CHANNELS)), vm((CHUNK, LANES)),
        ],
        compiler_params=PARAMS,
        cost_estimate=cost(10**9, 30 * 10**6),
    )(mix, mix, info, mix, conv_full, bias_full, rate, sbias, expand)

    forward = Steps(carry_states(packed, pairs, False))
    forward.beside()

    y_local = pl.pallas_call(
        intra_kernel,
        name="intra",
        grid=(chunks,),
        in_specs=[
            rows(STATE), rows(STATE), rows(DI), rows(HEADS), rows(CHUNK, per=HEADS), rows(8),
            row_spec,
        ],
        out_specs=rows(DI),
        out_shape=shape((count, DI), F32),
        compiler_params=PARAMS,
        cost_estimate=cost(10**9, 30 * 10**6),
    )(q, k, v, rc, rs, info, label_rows)

    (y_local,) = forward.beside(y_local)
    gate = jnp.dot(hidden, w_gate, preferred_element_type=F32).astype(BF)
    grad_normed = lax.dot_general(upstream, w_out, NT, preferred_element_type=F32)
    gate, grad_normed = forward.beside(gate, grad_normed)
    incoming = forward.finish()

    normed, dy, dy_lo, dgate, u, dq, states, packed_back, gate_sums = pl.pallas_call(
        gate_kernel,
        name="gate_norm",
        grid=(chunks,),
        in_specs=[
            rows(DI), rows(STATE), rows(STATE), rows(DI), rows(HEADS), rows(CHUNK, per=HEADS),
            rows(8), rows(DI), rows(DI), whole((STATE, DI)), whole((1, DI)), whole((1, DI)),
            whole((HEADS, DI)),
        ],
        out_specs=[
            rows(DI), rows(DI), rows(DI), rows(DI), rows(HEADS), rows(STATE), rows(DI),
            whole((STATE + 16, DI)), whole((16, DI)),
        ],
        out_shape=[
            shape((count, DI), BF), shape((count, DI), BF), shape((count, DI), BF),
            shape((count, DI), BF), shape((count, HEADS), F32), shape((count, STATE), F32),
            shape((chunks * STATE, DI), BF),
            shape((STATE + 16, DI), BF), shape((16, DI), F32),
        ],
        scratch_shapes=[
            vm((STATE, DI)), vm((STATE, DI)), vm((1, DI)), vm((CHUNK, DI)), vm((CHUNK, DI)),
            vm((16, DI)), vm((LANES, CHUNK)),
        ],
        compiler_params=PARAMS,
        cost_estimate=cost(10**9, 50 * 10**6),
    )(
        y_local, q, k, v, rc, rs, info, gate, grad_normed, incoming, skip_wide, gate_full,
        expand,
    )

    backward = Steps(carry_states(packed_back, pairs, True))
    grad_gate_w = lax.dot_general(hidden, dgate, TN, preferred_element_type=F32).astype(BF)
    (grad_gate_w,) = backward.beside(grad_gate_w)
    grad_out_w = lax.dot_general(normed, upstream, TN, preferred_element_type=F32).astype(BF)
    (grad_out_w,) = backward.beside(grad_out_w)
    gate_steps = Steps(reduce_rows([grad_gate_w, grad_out_w], place, pairs))
    (normed,) = gate_steps.beside(normed)
    block_out = (
        tokens.astype(F32) + jnp.dot(normed, w_out, preferred_element_type=F32)
    ).astype(BF)
    (block_out,) = gate_steps.beside(block_out)
    block_out, dy = backward.beside(block_out, dy)

    dv, uv, dq, dk = pl.pallas_call(
        intra_back_kernel,
        name="intra_back",
        grid=(chunks,),
        in_specs=[
            rows(STATE), rows(STATE), rows(DI), rows(DI), rows(DI), rows(HEADS),
            rows(CHUNK, per=HEADS), rows(8), row_spec, whole((HEADS, DI)), rows(STATE),
        ],
        out_specs=[rows(DI), rows(HEADS), rows(STATE), rows(STATE)],
        out_shape=[
            shape((count, DI), BF), shape((count, HEADS), F32), shape((count, STATE), F32),
            shape((count, STATE), F32),
        ],
        compiler_params=PARAMS,
        cost_estimate=cost(2 * 10**9, 40 * 10**6),
    )(q, k, v, dy, dy_lo, rc, rs, info, label_rows, expand, dq)

    (dv,) = gate_steps.beside(dv)
    (dv,) = backward.beside(dv)
    coming_back = backward.finish()
    back = functools.partial(rows, count=chunks)
    grad_mix, dhalo, conv_sums, head_sums = pl.pallas_call(
        back_kernel,
        name="states_conv_back",
        grid=(chunks,),
        in_specs=[
            back(CHANNELS), raw_rows(chunks), back(CHANNELS), back(DI), back(STATE), back(STATE),
            back(HEADS), back(CHUNK, per=HEADS), back(8), back(DI), back(DI), back(HEADS),
            back(HEADS), back(STATE), back(STATE), back(DI), whole((STATE, DI)),
            halo_spec, whole((taps, CHANNELS)), whole((1, HEADS)),
            whole((1, HEADS)), whole((1, DI)), whole((HEADS, DI)),
        ],
        out_specs=[
            back(MIX_WIDE), whole((8, CHANNELS)), whole((40, CHANNELS)),
            whole((16, HEADS)),
        ],
        out_shape=[
            shape((count, MIX_WIDE), BF), shape((8, CHANNELS), F32),
            shape((40, CHANNELS), F32), shape((16, HEADS), F32),
        ],
        scratch_shapes=[
            vm((STATE, DI)), vm((8, CHANNELS)), vm((8, LANES)), vm((40, CHANNELS)),
            vm((16, HEADS)), vm((LANES, CHUNK)), vm((CHUNK, CHANNELS)),
        ],
        compiler_params=PARAMS,
        cost_estimate=cost(2 * 10**9, 60 * 10**6),
    )(
        mix, mix, z, v, k, q, rc, rs, info, dy, dv, uv, u, dq, dk, states, coming_back,
        mix, conv_full, rate, sbias, skip_wide, expand,
    )

    edge = shift(dhalo, 2 * pairs, -1)
    edge = jnp.pad(edge, ((0, 0), (0, MIX_WIDE - CHANNELS)))
    fixed = (grad_mix[count - 8 :].astype(F32) + edge).astype(BF)
    grad_mix = lax.dynamic_update_slice(grad_mix, fixed, (count - 8, 0))
    grad_mix_w = lax.dot_general(hidden, grad_mix, TN, preferred_element_type=F32).astype(BF)
    mix_steps = Steps(reduce_rows([grad_mix_w], place, pairs))
    (grad_mix,) = mix_steps.beside(grad_mix)
    grad_hidden = lax.dot_general(dgate, w_gate, NT, preferred_element_type=F32)
    grad_hidden = grad_hidden + lax.dot_general(grad_mix, w_mix, NT, preferred_element_type=F32)
    (grad_hidden,) = gate_steps.beside(grad_hidden)
    (grad_hidden,) = mix_steps.beside(grad_hidden)

    x = tokens.astype(F32)
    inv = lax.rsqrt(jnp.mean(x * x, axis=-1, keepdims=True) + 1e-05)
    unit = x * inv
    scaled = grad_hidden * norm_full
    mean = jnp.mean(scaled * unit, axis=-1, keepdims=True)
    grad_tokens = upstream.astype(F32) + inv * (scaled - unit * mean)
    grad_norm = jnp.sum(grad_hidden * unit, axis=0)
    grad_tokens, grad_norm = mix_steps.beside(grad_tokens, grad_norm)

    conv_sums = conv_sums.reshape(taps + 1, 8, CHANNELS).sum(axis=1)
    gate_sums = gate_sums.reshape(2, 8, DI).sum(axis=1)
    head_sums = head_sums.reshape(2, 8, HEADS).sum(axis=1)
    grad_skip = gate_sums[1].reshape(HEADS, HEADDIM).sum(axis=1)
    devices = 2 * pairs * fsdp
    parts = jnp.concatenate(
        [
            conv_sums.reshape(taps + 1, devices, own[1]).transpose(1, 0, 2).reshape(devices, -1),
            grad_norm.reshape(devices, -1),
            gate_sums[0].reshape(devices, -1),
            jnp.broadcast_to(
                jnp.concatenate([head_sums[0], grad_skip, head_sums[1]])[None],
                (devices, 3 * HEADS),
            ),
        ],
        axis=1,
    )
    mine = lax.dynamic_slice(
        sum_small(parts, pairs, fsdp), (device, 0), (1, parts.shape[1])
    )[0]
    ends = np.cumsum([own[0], own[1], own[2], own[3], HEADS, HEADS, HEADS]).tolist()
    conv_shard, bias_shard, norm_shard, gain_shard, *heads = [
        mine[a:b] for a, b in zip([0] + ends[:-1], ends)
    ]
    conv_shard = conv_shard.reshape(taps, -1)
    (mix_shard,) = mix_steps.finish()
    gate_shard, out_shard = gate_steps.finish()
    in_shard = jnp.concatenate([gate_shard, mix_shard[:, :MIX]], axis=1)
    return (
        block_out[None],
        grad_tokens[None],
        in_shard,
        out_shard,
        conv_shard,
        bias_shard,
        norm_shard,
        gain_shard,
        heads[0],
        heads[1],
        heads[2],
    )


def solution(mesh):
    seq, fsdp = mesh.devices.shape
    fine = Mesh(mesh.devices.reshape(seq // 2, 2, fsdp), ALL)
    line = ("pair", "core")
    tokens, labels, mat = P("fsdp", line, None), P("fsdp", line), P(ALL, None)
    weights = (mat, mat, P(None, ALL), P(ALL), P(ALL), P(ALL), P(), P(), P())
    return jax.shard_map(
        functools.partial(on_device, seq // 2),
        mesh=fine,
        in_specs=(tokens, labels) + weights + (tokens,),
        out_specs=(tokens, tokens) + weights,
        check_vma=False,
    )
```

```python
import functools

import jax
import jax.numpy as jnp
import numpy as np
from jax import lax
from jax.experimental import pallas as pl
from jax.experimental.pallas import tpu as pltpu
from jax.sharding import Mesh
from jax.sharding import PartitionSpec as P

HEADS = 32
HEADDIM = 64
STATE = 128
CHUNK = 128
LANES = 128
DI = HEADS * HEADDIM
CHANNELS = DI + 2 * STATE
WIDE = 256
MIX = CHANNELS + HEADS
MIX_WIDE = -(-MIX // 128) * 128
NEG = -1e30
LOG2E = 1.4426950408889634
ALL = ("pair", "core", "fsdp")
BF = jnp.bfloat16
F32 = jnp.float32
NT = (((1,), (1,)), ((), ()))
TN = (((0,), (0,)), ((), ()))
NN = (((1,), (0,)), ((), ()))
PARAMS = pltpu.CompilerParams(
    dimension_semantics=("arbitrary",), vmem_limit_bytes=56 * 1024 * 1024
)

PLAIN = pltpu.CompilerParams(vmem_limit_bytes=56 * 1024 * 1024)


def mm(a, b, dims=NN):
    return lax.dot_general(a, b, dims, preferred_element_type=F32)


def pieces(x, count):
    out = []
    for _ in range(count):
        part = x.astype(BF)
        out.append(part)
        x = x - part.astype(F32)
    return out


def spread(x, expand):
    both = jnp.concatenate(pieces(x, 2), axis=1)
    return mm(both, jnp.concatenate([expand, expand], axis=0))


def head_sum(x, expand):
    hi, lo = pieces(x, 2)
    if x.shape[1] == LANES:
        return mm(
            jnp.concatenate([hi, lo], axis=1), jnp.concatenate([expand, expand], axis=1), NT
        )
    return mm(hi, expand, NT) + mm(lo, expand, NT)


def cumulate(tri, x):
    a, b, c = pieces(x, 3)
    return mm(tri, a) + mm(tri, b) + mm(tri, c)


def mm3(a, b, dims=NN):
    a_hi, a_lo = pieces(a, 2)
    b_hi, b_lo = pieces(b, 2)
    return mm(a_hi, b_hi, dims) + (mm(a_lo, b_hi, dims) + mm(a_hi, b_lo, dims))


def sigmoid(x):
    return 0.5 * jnp.tanh(0.5 * x) + 0.5


def iota2(shape, dim):
    return lax.broadcasted_iota(jnp.int32, shape, dim)


def rows8(x):
    return jnp.sum(x.reshape(x.shape[0] // 8, 8, x.shape[1]), axis=0)


def prep_kernel(
    x_ref, raw_ref, info_ref, halo_ref, w_ref, b_ref, rate_ref, sbias_ref, e_ref,
    z_ref, v_ref, k_ref, q_ref, rc_ref, rs_ref, pack_ref,
    state, thru, carry, pad,
):
    step = pl.program_id(0)

    @pl.when(step == 0)
    def _():
        carry[...] = halo_ref[:8].astype(F32)
        state[...] = jnp.zeros_like(state)
        thru[...] = jnp.ones_like(thru)
        pad[...] = jnp.zeros_like(pad)

    info = info_ref[...]
    age = jnp.broadcast_to(info[:, 1:2], (CHUNK, LANES))
    masks = [(age >= d).astype(F32) for d in (1.0, 2.0, 3.0)]
    for tile in range(CHANNELS // LANES):
        sl = slice(tile * LANES, (tile + 1) * LANES)
        x = x_ref[:, sl].astype(F32)
        ext = jnp.concatenate([carry[:, sl], x], axis=0)
        z = b_ref[:, sl] + w_ref[3:4, sl] * x
        for d in (1, 2, 3):
            z = z + w_ref[3 - d : 4 - d, sl] * (ext[8 - d : 8 - d + CHUNK] * masks[d - 1])
        carry[:, sl] = x[CHUNK - 8 :]
        z_ref[:, sl] = z.astype(BF)
        value = z * sigmoid(z)
        if tile < DI // LANES:
            v_ref[:, sl] = value.astype(BF)
        elif tile == DI // LANES:
            k_ref[...] = value
        else:
            q_ref[...] = value

    raw = raw_ref[:, :HEADS].astype(F32) + sbias_ref[...]
    size = jnp.maximum(raw, 0.0) + jnp.log1p(jnp.exp(-jnp.abs(raw)))
    decay = -jnp.exp(rate_ref[...]) * size * LOG2E
    tri = (iota2((CHUNK, CHUNK), 0) >= iota2((CHUNK, CHUNK), 1)).astype(BF)
    running = cumulate(tri, decay)
    shifted = running - jnp.log2(jnp.maximum(size, 1e-37))
    rc_ref[...] = running
    pad[:, :HEADS] = shifted
    rs_ref[...] = pad[...].T[:HEADS]
    total = running[CHUNK - 1 :]
    weight = jnp.exp2(total - shifted) * info[:, 3:4]
    carried = jnp.exp2(running[CHUNK - 8 :]) * info[CHUNK - 8 :, 2:3]
    keys = k_ref[...].astype(BF)
    for g in range(DI // WIDE):
        sl = slice(g * WIDE, (g + 1) * WIDE)
        scaled = (mm(weight.astype(BF), e_ref[:, sl]) * v_ref[:, sl].astype(F32)).astype(BF)
        factor = spread(carried, e_ref[:, sl])[7:8]
        state[:, sl] = factor * state[:, sl] + mm(keys, scaled, TN)
        thru[:, sl] = factor * thru[:, sl]

    @pl.when(step == pl.num_programs(0) - 1)
    def _():
        pack_ref[:STATE] = state[...]
        hi, lo = pieces(thru[...], 2)
        row = iota2((16, DI), 0)
        pack_ref[STATE:] = jnp.where(
            row == 0, hi.astype(F32), jnp.where(row == 1, lo.astype(F32), 0.0)
        )


def shared(q_ref, k_ref, lc_ref, lr_ref):
    scores = mm3(q_ref[...], k_ref[...], NT)
    ok = (iota2((CHUNK, CHUNK), 0) >= iota2((CHUNK, CHUNK), 1)) & (
        lc_ref[:, 0:1] == lr_ref[0, 0:1, :]
    )
    bias = jnp.where(ok, 0.0, NEG)
    low_half = iota2((CHUNK, LANES), 1) < HEADDIM
    return scores, bias, low_half


def two_heads(v, low_half):
    zero = jnp.zeros_like(v)
    return jnp.concatenate([jnp.where(low_half, v, zero), jnp.where(low_half, zero, v)], axis=0)


def intra_kernel(q_ref, k_ref, v_ref, rc_ref, rs_ref, lc_ref, lr_ref, y_ref):
    scores, bias, low_half = shared(q_ref, k_ref, lc_ref, lr_ref)
    for pair in range(HEADS // 2):
        sl = slice(pair * LANES, (pair + 1) * LANES)
        mixing = []
        for h in (2 * pair, 2 * pair + 1):
            differ = (rc_ref[:, h : h + 1] - rs_ref[h : h + 1, :]) + bias
            mixing.append((jnp.exp2(differ) * scores).astype(BF))
        y_ref[:, sl] = mm(jnp.concatenate(mixing, axis=1), two_heads(v_ref[:, sl], low_half))


def gate_kernel(
    y_ref, q_ref, k_ref, v_ref, rc_ref, rs_ref, info_ref, gate_ref, dn_ref, sin_ref,
    skip_ref, gain_ref, e_ref,
    n_ref, dy_ref, dy_lo_ref, dgate_ref, u_ref, dq_ref, sc_ref, pack_ref, sums_ref,
    state, adj, reach, scan, enter, sums, pad,
):
    step = pl.program_id(0)

    @pl.when(step == 0)
    def _():
        state[...] = sin_ref[...]
        adj[...] = jnp.zeros_like(adj)
        reach[...] = jnp.ones_like(reach)
        sums[...] = jnp.zeros_like(sums)

    info = info_ref[...]
    running = rc_ref[...]
    pad[:HEADS] = rs_ref[...]
    shifted = pad[...].T[:, :HEADS]
    total = running[CHUNK - 1 :]
    weight = jnp.exp2(total - shifted) * info[:, 3:4]
    entering = jnp.exp2(running) * info[:, 2:3]
    queries, queries_lo = pieces(q_ref[...], 2)
    keys = k_ref[...].astype(BF)
    low_weight = weight.astype(BF)
    both_queries = jnp.concatenate([queries, queries_lo], axis=1)
    squares = jnp.zeros((CHUNK, LANES), F32)
    dots = jnp.zeros((CHUNK, LANES), F32)
    for g in range(DI // WIDE):
        sl = slice(g * WIDE, (g + 1) * WIDE)
        low_state, rest = pieces(state[:, sl], 2)
        sc_ref[:, sl] = low_state
        ent = spread(entering, e_ref[:, sl])
        enter[:, sl] = ent
        y = y_ref[:, sl] + ent * (
            mm(both_queries, jnp.concatenate([low_state, low_state], axis=0))
            + mm(queries, rest)
        )
        scan[:, sl] = y
        gate = gate_ref[:, sl].astype(F32)
        gated = (y + skip_ref[:, sl] * v_ref[:, sl].astype(F32)) * (gate * sigmoid(gate))
        square = gated * gated
        dot = dn_ref[:, sl] * gain_ref[:, sl] * gated
        for t in range(WIDE // LANES):
            part = slice(t * LANES, (t + 1) * LANES)
            squares = squares + square[:, part]
            dots = dots + dot[:, part]
    inv = lax.rsqrt(jnp.sum(squares, axis=1, keepdims=True) * (1.0 / DI) + 1e-05)
    coef = inv * inv * inv * jnp.sum(dots, axis=1, keepdims=True) * (1.0 / DI)
    head_dots = jnp.zeros((CHUNK, HEADS), F32)
    dq = jnp.zeros((CHUNK, STATE), F32)
    for g in range(DI // WIDE):
        sl = slice(g * WIDE, (g + 1) * WIDE)
        y = scan[:, sl]
        v = v_ref[:, sl].astype(F32)
        gate = gate_ref[:, sl].astype(F32)
        sig = sigmoid(gate)
        silu = gate * sig
        mixed = y + skip_ref[:, sl] * v
        gated = mixed * silu
        gain = gain_ref[:, sl]
        dn = dn_ref[:, sl]
        unit = gated * inv
        n_ref[:, sl] = (unit * gain).astype(BF)
        sums[0:8, sl] += rows8(dn * unit)
        dg = dn * gain * inv - gated * coef
        dgate_ref[:, sl] = (dg * mixed * (sig + silu * (1.0 - sig))).astype(BF)
        dy = dg * silu
        sums[8:16, sl] += rows8(dy * v)
        low, rest = pieces(dy, 2)
        dy_ref[:, sl] = low
        dy_lo_ref[:, sl] = rest
        head_dots = head_dots + head_sum(low.astype(F32) * y, e_ref[:, sl])
        ent = enter[:, sl]
        dy_in, dy_in_lo = pieces(ent * dy, 2)
        state_hi, state_lo = pieces(state[:, sl], 2)
        both = mm(dy_in, jnp.concatenate([state_hi, state_lo], axis=0), NT)
        dq = dq + (both[:, :STATE] + (both[:, STATE:] + mm(dy_in_lo, state_hi, NT)))
        adj[:, sl] += reach[:, sl] * mm(queries, dy_in, TN)
        factor = ent[CHUNK - 1 :]
        scaled = (mm(low_weight, e_ref[:, sl]) * v).astype(BF)
        state[:, sl] = factor * state[:, sl] + mm(keys, scaled, TN)
        reach[:, sl] = factor * reach[:, sl]
    u_ref[...] = head_dots
    dq_ref[...] = dq

    @pl.when(step == pl.num_programs(0) - 1)
    def _():
        pack_ref[:STATE] = adj[...].astype(BF)
        hi, lo = pieces(reach[...], 2)
        row = iota2((16, DI), 0)
        pack_ref[STATE:] = jnp.where(
            row == 0, hi.astype(F32), jnp.where(row == 1, lo.astype(F32), 0.0)
        ).astype(BF)
        sums_ref[...] = sums[...]


def intra_back_kernel(
    q_ref, k_ref, v_ref, dy_ref, dy_lo_ref, rc_ref, rs_ref, lc_ref, lr_ref, e_ref, dqin_ref,
    dv_ref, uv_ref, dq_ref, dk_ref,
):
    scores, bias, low_half = shared(q_ref, k_ref, lc_ref, lr_ref)
    dscores = jnp.zeros((CHUNK, CHUNK), F32)
    head_dots = jnp.zeros((CHUNK, HEADS), F32)
    for pair in range(HEADS // 2):
        sl = slice(pair * LANES, (pair + 1) * LANES)
        v = v_ref[:, sl]
        dy = dy_ref[:, sl]
        vv = two_heads(v, low_half)
        dmix = mm(
            jnp.concatenate([dy, dy_lo_ref[:, sl]], axis=1),
            jnp.concatenate([vv, vv], axis=1),
            NT,
        )
        mixing = []
        for i in range(2):
            h = 2 * pair + i
            differ = (rc_ref[:, h : h + 1] - rs_ref[h : h + 1, :]) + bias
            factor = jnp.exp2(differ)
            dscores = dscores + dmix[:, i * CHUNK : (i + 1) * CHUNK] * factor
            mixing.append((factor * scores).astype(BF).T)
        dv = mm(jnp.concatenate(mixing, axis=1), two_heads(dy, low_half))
        dv_ref[:, sl] = dv.astype(BF)
        head_dots = head_dots + head_sum(v.astype(F32) * dv, e_ref[:, sl])
    uv_ref[...] = head_dots
    dq_ref[...] = dqin_ref[...] + mm3(dscores, k_ref[...])
    dk_ref[...] = mm(dscores.astype(BF), q_ref[...].astype(BF), TN)


def back_kernel(
    x_ref, raw_ref, z_ref, v_ref, k_ref, q_ref, rc_ref, rs_ref, info_ref, dy_ref, dv_ref,
    uv_ref, u_ref, dq_ref, dk_ref, sc_ref, ain_ref, halo_ref, w_ref, rate_ref, sbias_ref,
    skip_ref, e_ref,
    dx_ref, dhalo_ref, csum_ref, hsum_ref,
    adj, nextz, nextage, csum, hsum, pad, dmix,
):
    step = pl.program_id(0)

    @pl.when(step == 0)
    def _():
        adj[...] = ain_ref[...]
        nextz[...] = jnp.zeros_like(nextz)
        nextage[...] = jnp.zeros_like(nextage)
        csum[...] = jnp.zeros_like(csum)
        hsum[...] = jnp.zeros_like(hsum)

    info = info_ref[...]
    running = rc_ref[...]
    pad[:HEADS] = rs_ref[...]
    shifted = pad[...].T[:, :HEADS]
    total = running[CHUNK - 1 :]
    weight = jnp.exp2(total - shifted) * info[:, 3:4]
    entering = jnp.exp2(running) * info[:, 2:3]
    queries = q_ref[...].astype(BF)
    keys = k_ref[...].astype(BF)
    dq = dq_ref[...]
    dk = dk_ref[...]
    low_weight = weight.astype(BF)
    low_entering = entering.astype(BF)
    later = jnp.zeros((CHUNK, HEADS), F32)
    through = jnp.zeros((8, HEADS), F32)
    for g in range(DI // WIDE):
        sl = slice(g * WIDE, (g + 1) * WIDE)
        e = e_ref[:, sl]
        v = v_ref[:, sl].astype(F32)
        dy = dy_ref[:, sl].astype(F32)
        wide = mm(low_weight, e)
        dy_in = (mm(low_entering, e) * dy).astype(BF)
        scaled = (wide * v).astype(BF)
        adjoint = adj[:, sl]
        low_adj = adjoint.astype(BF)
        states = sc_ref[:, sl]
        dv = wide * mm(keys, low_adj)
        later = later + mm((v * dv).astype(BF), e, NT)
        dk = dk + mm(scaled, low_adj, NT)
        factor = spread(entering[CHUNK - 8 :], e)[7:8]
        through = through + head_sum(rows8(adjoint * states.astype(F32)) * factor, e)
        adj[:, sl] = factor * adjoint + mm(queries, dy_in, TN)
        dmix[:, sl] = dv_ref[:, sl].astype(F32) + dv + skip_ref[:, sl] * dy
    dmix[:, DI : DI + STATE] = dk
    dmix[:, DI + STATE :] = dq

    age = jnp.broadcast_to(info[:, 1:2], (CHUNK, LANES))
    masks = [(age >= d).astype(F32) for d in (1.0, 2.0, 3.0)]
    ages = nextage[...]
    next_masks = [(ages >= d).astype(F32) for d in (1.0, 2.0, 3.0)]
    for tile in range(CHANNELS // LANES):
        sl = slice(tile * LANES, (tile + 1) * LANES)
        z = z_ref[:, sl].astype(F32)
        sig = sigmoid(z)
        dz = dmix[:, sl] * (sig + z * sig * (1.0 - sig))
        x = x_ref[:, sl].astype(F32)
        after = nextz[:, sl]
        dx = w_ref[3:4, sl] * dz
        csum[32:40, sl] += rows8(dz)
        csum[24:32, sl] += rows8(x * dz)
        for d in (1, 2, 3):
            ext = jnp.concatenate([dz * masks[d - 1], after * next_masks[d - 1]], axis=0)
            moved = ext[d : d + CHUNK]
            dx = dx + w_ref[3 - d : 4 - d, sl] * moved
            csum[8 * (3 - d) : 8 * (4 - d), sl] += rows8(x * moved)
        dx_ref[:, sl] = dx.astype(BF)
        nextz[:, sl] = dz[:8]

        @pl.when(step == pl.num_programs(0) - 1)
        def _():
            halo = halo_ref[:8, sl].astype(F32)
            acc = jnp.zeros((8, LANES), F32)
            for d in (1, 2, 3):
                ext = jnp.concatenate(
                    [jnp.zeros((8, LANES), F32), dz[:8] * masks[d - 1][:8]], axis=0
                )
                moved = ext[d : d + 8]
                acc = acc + w_ref[3 - d : 4 - d, sl] * moved
                csum[8 * (3 - d) : 8 * (4 - d), sl] += halo * moved
            dhalo_ref[:, sl] = acc
    nextage[...] = age[:8]

    row = iota2((CHUNK, CHUNK), 0)
    col = iota2((CHUNK, CHUNK), 1)
    ddecay = (
        cumulate((col >= row).astype(BF), u_ref[...] - uv_ref[...])
        + cumulate((col < row).astype(BF), later)
        + jnp.sum(through, axis=0, keepdims=True)
    )
    raw = raw_ref[:, :HEADS].astype(F32) + sbias_ref[...]
    sig = sigmoid(raw)
    size = jnp.maximum(raw, 0.0) + jnp.log1p(jnp.exp(-jnp.abs(raw)))
    rate = -jnp.exp(rate_ref[...])
    ratio = jnp.where(raw < -15.0, 1.0, sig / jnp.maximum(size, 1e-37))
    draw = (uv_ref[...] + later) * ratio + ddecay * rate * sig
    dx_ref[:, CHANNELS:MIX] = draw.astype(BF)
    dx_ref[:, MIX:] = jnp.zeros((CHUNK, MIX_WIDE - MIX), BF)
    hsum[0:8] += rows8(ddecay * rate * size)
    hsum[8:16] += rows8(draw)

    @pl.when(step == pl.num_programs(0) - 1)
    def _():
        csum_ref[...] = csum[...]
        hsum_ref[...] = hsum[...]


def whole(shape):
    return pl.BlockSpec(shape, lambda c: (0,) * len(shape))


def rows(width, count=None, per=CHUNK):
    if count is None:
        return pl.BlockSpec((per, width), lambda c: (c, 0))
    return pl.BlockSpec((per, width), lambda c: (count - 1 - c, 0))


def raw_rows(count=None):
    block = CHANNELS // LANES
    if count is None:
        return pl.BlockSpec((CHUNK, LANES), lambda c: (c, block))
    return pl.BlockSpec((CHUNK, LANES), lambda c: (count - 1 - c, block))


def shape(dims, kind):
    return jax.ShapeDtypeStruct(dims, kind)


def cost(flops, moved):
    return pl.CostEstimate(flops=flops, bytes_accessed=moved, transcendentals=0)


def vm(dims, kind=F32):
    return pltpu.VMEM(dims, kind)


def pack(state, thru, kind):
    hi, lo = pieces(thru, 2)
    return jnp.concatenate([state.astype(kind), hi.astype(kind), lo.astype(kind)], axis=0)


def unpack(packed):
    packed = packed.astype(F32)
    return packed[:STATE], packed[STATE : STATE + 1] + packed[STATE + 1 : STATE + 2]


class Steps:
    def __init__(self, steps):
        self.steps, self.result, self.flight = steps, None, None
        self.advance(None)

    def advance(self, landed):
        try:
            self.flight = self.steps.send(landed)
        except StopIteration as end:
            self.flight, self.result = None, end.value

    def beside(self, *work):
        if self.flight is None:
            return work
        landed, work = lax.optimization_barrier((self.flight, work))
        self.advance(landed)
        return work

    def finish(self):
        while self.flight is not None:
            self.advance(self.flight)
        return self.result


def carry_states(packed, pairs, backward):
    packed = packed[: STATE + 2]
    kind = packed.dtype
    core = lax.axis_index("core")
    place = lax.axis_index("pair")
    half = packed.shape[1] // 2
    left, right = packed[:, :half], packed[:, half:]
    mine = jnp.where(core == 0, left, right)
    (theirs,) = yield [swap(jnp.where(core == 0, right, left), "core", 1)]
    leads = (core == 1) if backward else (core == 0)
    first, first_thru = unpack(jnp.where(leads, mine, theirs))
    second, second_thru = unpack(jnp.where(leads, theirs, mine))
    total, total_thru = second + second_thru * first, second_thru * first_thru
    before, before_thru = jnp.zeros_like(total), jnp.ones_like(total_thru)
    distance = 1
    while distance < pairs:
        (other,) = yield [swap(pack(total, total_thru, kind), "pair", distance)]
        other, other_thru = unpack(other)
        upper = (place & distance) != 0
        follows = jnp.logical_not(upper) if backward else upper
        before = jnp.where(follows, before + before_thru * other, before)
        before_thru = jnp.where(follows, before_thru * other_thru, before_thru)
        total = jnp.where(follows, total + total_thru * other, other + other_thru * total)
        total_thru = total_thru * other_thru
        distance *= 2
    after = first + first_thru * before
    keep = jnp.where(leads, before, after)
    (other,) = yield [swap(jnp.where(leads, after, before).astype(kind), "core", 1)]
    other = other.astype(F32)
    return jnp.where(
        core == 0,
        jnp.concatenate([keep, other], axis=1),
        jnp.concatenate([other, keep], axis=1),
    )


def shift(block, count, by):
    moved = [(i, i + by) for i in range(count) if 0 <= i + by < count]
    return lax.ppermute(block, ("pair", "core"), moved)


def swap(block, axis, mask):
    count = lax.axis_size(axis)
    return lax.ppermute(block, axis, [(i, i ^ mask) for i in range(count)])


def bit_orders(pairs):
    bits = list(range(pairs.bit_length() - 1))
    cut = len(bits) // 2
    return bits, bits[cut:] + bits[:cut]


def part_ids(pairs, fsdp):
    out = []
    for part, order in enumerate(bit_orders(pairs)):
        ids = [(0, k) for k in range(part * fsdp // 2, (part + 1) * fsdp // 2)]
        for b in order:
            ids = ids + [(mask ^ (1 << b), k) for mask, k in ids]
        out.append(ids)
    return out


def shard_of(place_ref, fsdp, mask, flip, k):
    return ((place_ref[0] ^ mask) * 2 + (place_ref[1] ^ flip)) * fsdp + (place_ref[2] ^ k)


def place_rows(place, held, r, fsdp, total):
    def body(place_ref, *refs):
        dst = refs[-1]
        for src, (_, flip, ids) in zip(refs, held):
            for at, (mask, k) in enumerate(ids):
                row = pl.multiple_of(shard_of(place_ref, fsdp, mask, flip, k) * r, r)
                dst[pl.ds(row, r), :] = src[at * r : (at + 1) * r, :]

    arrays = [a for a, _, _ in held]
    cols = arrays[0].shape[1]
    return pl.pallas_call(
        body,
        name="place_rows",
        in_specs=[pl.BlockSpec(memory_space=pltpu.SMEM)]
        + [pl.BlockSpec(memory_space=pltpu.VMEM)] * len(arrays),
        out_specs=pl.BlockSpec(memory_space=pltpu.VMEM),
        out_shape=jax.ShapeDtypeStruct((total, cols), arrays[0].dtype),
        compiler_params=PLAIN,
        cost_estimate=cost(0, 4 * total * cols),
    )(place, *arrays)


def pick_rows(place, arrays, r, pairs, fsdp):
    order = [i for ids in part_ids(pairs, fsdp) for i in ids]
    half = len(order) * r
    repeat = [a.shape[0] // (2 * half) for a in arrays]
    cols = sum(a.shape[1] * n for a, n in zip(arrays, repeat))
    quarter = len(order) // 4

    def body(place_ref, *refs):
        for flip in range(2):
            for spot, (mask, k) in enumerate(order):
                index = shard_of(place_ref, fsdp, mask, flip, k)
                dst, at = refs[-1], spot
                if not flip:
                    dst, at = refs[spot // quarter - 5], spot % quarter
                col = 0
                for src, n in zip(refs, repeat):
                    for m in range(n):
                        row = pl.multiple_of((index * n + m) * r, r)
                        width = src.shape[1]
                        dst[at * r : (at + 1) * r, col : col + width] = src[pl.ds(row, r), :]
                        col += width

    return pl.pallas_call(
        body,
        name="pick_rows",
        in_specs=[pl.BlockSpec(memory_space=pltpu.SMEM)]
        + [pl.BlockSpec(memory_space=pltpu.VMEM)] * len(arrays),
        out_specs=[pl.BlockSpec(memory_space=pltpu.VMEM)] * 5,
        out_shape=[jax.ShapeDtypeStruct((half // 4, cols), arrays[0].dtype)] * 4
        + [jax.ShapeDtypeStruct((half, cols), arrays[0].dtype)],
        compiler_params=PLAIN,
        cost_estimate=cost(0, 8 * half * cols),
    )(place, *arrays)


def unpack_weights(packed, r):
    total, model = packed.shape[0], (packed.shape[1] - DI) // 2
    if r % 16:
        tail = packed[:, DI:].reshape(total // r, r, 2, model).transpose(0, 2, 1, 3)
        return packed[:, :DI], tail.reshape(2 * total, model)
    per = min(total, 256)

    def body(src, gate, out):
        gate[...] = src[:, :DI]
        for i in range(per // r):
            for m in range(2):
                at, col = (2 * i + m) * r, DI + m * model
                out[at : at + r, :] = src[i * r : (i + 1) * r, col : col + model]

    return pl.pallas_call(
        body,
        name="unpack_weights",
        grid=(total // per,),
        in_specs=[rows(packed.shape[1], per=per)],
        out_specs=[rows(DI, per=per), rows(model, per=2 * per)],
        out_shape=[shape((total, DI), BF), shape((2 * total, model), BF)],
        compiler_params=PARAMS,
        cost_estimate=cost(0, 4 * total * packed.shape[1]),
    )(packed)


def gather_rows(w, place, pairs):
    r, fsdp = w.shape[0], lax.axis_size("fsdp")
    if r % 16:
        return lax.all_gather(w, ALL, axis=0, tiled=True)
    line = [w] + [swap(w, "fsdp", k) for k in range(1, fsdp)]
    orders = bit_orders(pairs)
    blocks = [
        jnp.concatenate(line[part * fsdp // 2 : (part + 1) * fsdp // 2], axis=0)
        for part in range(2)
    ]
    for level in range(len(orders[0])):
        got = [swap(a, "pair", 1 << order[level]) for a, order in zip(blocks, orders)]
        if level == 0:
            got = yield got
        blocks = [jnp.concatenate([a, b], axis=0) for a, b in zip(blocks, got)]
    held = [(a, 0, ids) for a, ids in zip(blocks, part_ids(pairs, fsdp))]
    held = held + [(swap(a, "core", 1), 1, ids) for a, _, ids in held]
    return place_rows(place, held, r, fsdp, 2 * pairs * fsdp * r)


def reduce_rows(arrays, place, pairs):
    fsdp = lax.axis_size("fsdp")
    r = arrays[0].shape[0] // (2 * pairs * fsdp)
    if r % 16:
        return [
            lax.psum_scatter(g.astype(F32), ALL, scatter_dimension=0, tiled=True) for g in arrays
        ]
    *keep, give = pick_rows(place, arrays, r, pairs, fsdp)
    (give,) = yield [give]
    (got,) = yield [swap(give, "core", 1)]
    cut = keep[0].shape[0]
    orders = bit_orders(pairs)
    quarters = [
        (a.astype(F32) + got[i * cut : (i + 1) * cut].astype(F32)).astype(BF)
        for i, a in enumerate(keep)
    ]
    near, far = quarters[0::2], quarters[1::2]
    for level in reversed(range(len(orders[0]))):
        others = yield [
            swap(a, "pair", 1 << order[level]) for a, order in zip(far, orders)
        ]
        blocks = [(a, b) for a, b in zip(near, others)]
        if level:
            cut = near[0].shape[0] // 2
            near = [
                (a[:cut].astype(F32) + b[:cut].astype(F32)).astype(BF) for a, b in blocks
            ]
            far = [(a[cut:].astype(F32) + b[cut:].astype(F32)).astype(BF) for a, b in blocks]
    blocks = [a.astype(F32) + b.astype(F32) for a, b in blocks]
    others = yield [
        swap(
            blocks[k // (fsdp // 2)][(k % (fsdp // 2)) * r :][:r].astype(BF), "fsdp", k
        )
        for k in range(1, fsdp)
    ]
    total = blocks[0][:r]
    for other in others:
        total = total + other.astype(F32)
    out, col = [], 0
    for g in arrays:
        width = g.shape[1]
        count = g.shape[0] // arrays[0].shape[0]
        out.append(
            jnp.concatenate(
                [total[:, col + m * width : col + (m + 1) * width] for m in range(count)], axis=0
            )
        )
        col += count * width
    return out


def links(pairs, fsdp):
    out = [("fsdp", 1 << b) for b in range(fsdp.bit_length() - 1)]
    out.append(("core", 1))
    return out + [("pair", 1 << b) for b in range(pairs.bit_length() - 1)]


def gather_small(vec, place_index, pairs, fsdp):
    block = vec[None]
    for axis, mask in links(pairs, fsdp):
        block = jnp.concatenate([block, swap(block, axis, mask)], axis=0)
    count = block.shape[0]
    index = jnp.arange(count)
    pick = (index[:, None] == (index[None] ^ place_index)).astype(BF)
    return jnp.dot(pick, block, preferred_element_type=F32)


def sum_small(block, pairs, fsdp):
    for axis, mask in links(pairs, fsdp):
        (other,) = yield [swap(block, axis, mask)]
        block = block + other
    return block


def hidden_of(tokens, gain):
    x = tokens.astype(F32)
    return (x * lax.rsqrt(jnp.mean(x * x, axis=-1, keepdims=True) + 1e-05) * gain).astype(BF)


def on_device(
    pairs, tokens, segment_ids, in_weight, out_weight, conv_weight, conv_bias, norm_gain,
    gate_gain, log_rate, skip_gain, step_bias, cotangent,
):
    tokens, labels, upstream = tokens[0], segment_ids[0], cotangent[0]
    count, model = tokens.shape
    chunks = count // CHUNK
    taps = conv_weight.shape[0]
    own = (conv_weight.size, conv_bias.size, norm_gain.size, gate_gain.size)
    fsdp = lax.axis_size("fsdp")
    place = jnp.stack([lax.axis_index(a) for a in ALL])
    device = (place[0] * 2 + place[1]) * fsdp + place[2]
    small = jnp.concatenate([conv_weight.reshape(-1), conv_bias, norm_gain, gate_gain])
    r, slot = in_weight.shape[0], MIX_WIDE - MIX
    small_rows = -(-small.size // slot)
    small = jnp.pad(small, (0, r * slot - small.size)).reshape(r, slot)
    mix_gather = Steps(
        gather_rows(jnp.concatenate([in_weight[:, DI:], small], axis=1), place, pairs)
    )
    packed_weights = jnp.concatenate(
        [in_weight[:, :DI], out_weight[:r], out_weight[r:]], axis=1
    )
    (packed_weights,) = mix_gather.beside(packed_weights)
    packed_weights = lax.all_gather(packed_weights, ALL, axis=0, tiled=True)
    w_mix = mix_gather.finish()
    small = w_mix[:, MIX:].reshape(-1, r, slot)[:, :small_rows].reshape(-1, small_rows * slot)
    small = small[:, : sum(own)]
    conv_full = (
        small[:, : own[0]].reshape(-1, taps, own[0] // taps).transpose(1, 0, 2)
        .reshape(taps, CHANNELS).astype(F32)
    )
    at = own[0]
    bias_full = small[:, at : at + own[1]].reshape(1, CHANNELS).astype(F32)
    at += own[1]
    norm_full = small[:, at : at + own[2]].reshape(1, model).astype(F32)
    at += own[2]
    gate_full = small[:, at :].reshape(1, DI).astype(F32)
    w_gate, w_out = unpack_weights(packed_weights, r)

    expand = jnp.asarray(np.repeat(np.eye(HEADS), HEADDIM, axis=1), BF)
    skip_wide = jnp.repeat(skip_gain, HEADDIM)[None]
    rate, sbias = log_rate[None], step_bias[None]
    before = jnp.concatenate([jnp.broadcast_to(labels[:1], (3,)), labels])
    age = sum((before[3 - d : 3 - d + count] == labels).astype(F32) for d in (1, 2, 3))
    by_chunk = labels.reshape(chunks, CHUNK)
    last = by_chunk[:, -1:]
    prior = jnp.concatenate([by_chunk[:1, :1], last[:-1]], axis=0)
    info = jnp.stack(
        [
            labels.astype(F32),
            age,
            (by_chunk == prior).astype(F32).reshape(-1),
            (by_chunk == last).astype(F32).reshape(-1),
        ]
        + [jnp.zeros((count,), F32)] * 4,
        axis=1,
    )
    label_rows = labels.astype(F32).reshape(chunks, 1, CHUNK)
    row_spec = pl.BlockSpec((1, 1, CHUNK), lambda c: (c, 0, 0))
    halo_spec = pl.BlockSpec((16, CHANNELS), lambda c: (count // 16, 0))

    tail = shift(tokens[count - 8 :], 2 * pairs, 1)
    tail = jnp.concatenate([tail, jnp.zeros_like(tail)], axis=0)
    hidden = hidden_of(tokens, norm_full)
    mix = jnp.dot(
        hidden_of(jnp.concatenate([tokens, tail], axis=0), norm_full), w_mix,
        preferred_element_type=F32,
    ).astype(BF)

    z, v, k, q, rc, rs, packed = pl.pallas_call(
        prep_kernel,
        name="conv_states",
        grid=(chunks,),
        in_specs=[
            rows(CHANNELS), raw_rows(), rows(8), halo_spec, whole((taps, CHANNELS)),
            whole((1, CHANNELS)), whole((1, HEADS)), whole((1, HEADS)), whole((HEADS, DI)),
        ],
        out_specs=[
            rows(CHANNELS), rows(DI), rows(STATE), rows(STATE), rows(HEADS),
            rows(CHUNK, per=HEADS), whole((STATE + 16, DI)),
        ],
        out_shape=[
            shape((count, CHANNELS), BF), shape((count, DI), BF), shape((count, STATE), F32),
            shape((count, STATE), F32), shape((count, HEADS), F32),
            shape((chunks * HEADS, CHUNK), F32), shape((STATE + 16, DI), F32),
        ],
        scratch_shapes=[
            vm((STATE, DI)), vm((1, DI)), vm((8, CHANNELS)), vm((CHUNK, LANES)),
        ],
        compiler_params=PARAMS,
        cost_estimate=cost(10**9, 30 * 10**6),
    )(mix, mix, info, mix, conv_full, bias_full, rate, sbias, expand)

    forward = Steps(carry_states(packed, pairs, False))
    forward.beside()

    y_local = pl.pallas_call(
        intra_kernel,
        name="intra",
        grid=(chunks,),
        in_specs=[
            rows(STATE), rows(STATE), rows(DI), rows(HEADS), rows(CHUNK, per=HEADS), rows(8),
            row_spec,
        ],
        out_specs=rows(DI),
        out_shape=shape((count, DI), F32),
        compiler_params=PARAMS,
        cost_estimate=cost(10**9, 30 * 10**6),
    )(q, k, v, rc, rs, info, label_rows)

    (y_local,) = forward.beside(y_local)
    gate = jnp.dot(hidden, w_gate, preferred_element_type=F32).astype(BF)
    grad_normed = lax.dot_general(upstream, w_out, NT, preferred_element_type=F32)
    gate, grad_normed = forward.beside(gate, grad_normed)
    incoming = forward.finish()

    normed, dy, dy_lo, dgate, u, dq, states, packed_back, gate_sums = pl.pallas_call(
        gate_kernel,
        name="gate_norm",
        grid=(chunks,),
        in_specs=[
            rows(DI), rows(STATE), rows(STATE), rows(DI), rows(HEADS), rows(CHUNK, per=HEADS),
            rows(8), rows(DI), rows(DI), whole((STATE, DI)), whole((1, DI)), whole((1, DI)),
            whole((HEADS, DI)),
        ],
        out_specs=[
            rows(DI), rows(DI), rows(DI), rows(DI), rows(HEADS), rows(STATE), rows(DI),
            whole((STATE + 16, DI)), whole((16, DI)),
        ],
        out_shape=[
            shape((count, DI), BF), shape((count, DI), BF), shape((count, DI), BF),
            shape((count, DI), BF), shape((count, HEADS), F32), shape((count, STATE), F32),
            shape((chunks * STATE, DI), BF),
            shape((STATE + 16, DI), BF), shape((16, DI), F32),
        ],
        scratch_shapes=[
            vm((STATE, DI)), vm((STATE, DI)), vm((1, DI)), vm((CHUNK, DI)), vm((CHUNK, DI)),
            vm((16, DI)), vm((LANES, CHUNK)),
        ],
        compiler_params=PARAMS,
        cost_estimate=cost(10**9, 50 * 10**6),
    )(
        y_local, q, k, v, rc, rs, info, gate, grad_normed, incoming, skip_wide, gate_full,
        expand,
    )

    backward = Steps(carry_states(packed_back, pairs, True))
    grad_gate_w = lax.dot_general(hidden, dgate, TN, preferred_element_type=F32).astype(BF)
    (grad_gate_w,) = backward.beside(grad_gate_w)
    grad_out_w = lax.dot_general(normed, upstream, TN, preferred_element_type=F32).astype(BF)
    (grad_out_w,) = backward.beside(grad_out_w)
    gate_steps = Steps(reduce_rows([grad_gate_w, grad_out_w], place, pairs))
    (normed,) = gate_steps.beside(normed)
    block_out = (
        tokens.astype(F32) + jnp.dot(normed, w_out, preferred_element_type=F32)
    ).astype(BF)
    (block_out,) = gate_steps.beside(block_out)
    block_out, dy = backward.beside(block_out, dy)

    dv, uv, dq, dk = pl.pallas_call(
        intra_back_kernel,
        name="intra_back",
        grid=(chunks,),
        in_specs=[
            rows(STATE), rows(STATE), rows(DI), rows(DI), rows(DI), rows(HEADS),
            rows(CHUNK, per=HEADS), rows(8), row_spec, whole((HEADS, DI)), rows(STATE),
        ],
        out_specs=[rows(DI), rows(HEADS), rows(STATE), rows(STATE)],
        out_shape=[
            shape((count, DI), BF), shape((count, HEADS), F32), shape((count, STATE), F32),
            shape((count, STATE), F32),
        ],
        compiler_params=PARAMS,
        cost_estimate=cost(2 * 10**9, 40 * 10**6),
    )(q, k, v, dy, dy_lo, rc, rs, info, label_rows, expand, dq)

    (dv,) = gate_steps.beside(dv)
    (dv,) = backward.beside(dv)
    coming_back = backward.finish()
    back = functools.partial(rows, count=chunks)
    grad_mix, dhalo, conv_sums, head_sums = pl.pallas_call(
        back_kernel,
        name="states_conv_back",
        grid=(chunks,),
        in_specs=[
            back(CHANNELS), raw_rows(chunks), back(CHANNELS), back(DI), back(STATE), back(STATE),
            back(HEADS), back(CHUNK, per=HEADS), back(8), back(DI), back(DI), back(HEADS),
            back(HEADS), back(STATE), back(STATE), back(DI), whole((STATE, DI)),
            halo_spec, whole((taps, CHANNELS)), whole((1, HEADS)),
            whole((1, HEADS)), whole((1, DI)), whole((HEADS, DI)),
        ],
        out_specs=[
            back(MIX_WIDE), whole((8, CHANNELS)), whole((40, CHANNELS)),
            whole((16, HEADS)),
        ],
        out_shape=[
            shape((count, MIX_WIDE), BF), shape((8, CHANNELS), F32),
            shape((40, CHANNELS), F32), shape((16, HEADS), F32),
        ],
        scratch_shapes=[
            vm((STATE, DI)), vm((8, CHANNELS)), vm((8, LANES)), vm((40, CHANNELS)),
            vm((16, HEADS)), vm((LANES, CHUNK)), vm((CHUNK, CHANNELS)),
        ],
        compiler_params=PARAMS,
        cost_estimate=cost(2 * 10**9, 60 * 10**6),
    )(
        mix, mix, z, v, k, q, rc, rs, info, dy, dv, uv, u, dq, dk, states, coming_back,
        mix, conv_full, rate, sbias, skip_wide, expand,
    )

    grad_mix, dhalo = gate_steps.beside(grad_mix, dhalo)
    edge = shift(dhalo, 2 * pairs, -1)
    edge = jnp.pad(edge, ((0, 0), (0, MIX_WIDE - CHANNELS)))
    fixed = (grad_mix[count - 8 :].astype(F32) + edge).astype(BF)
    grad_mix = lax.dynamic_update_slice(grad_mix, fixed, (count - 8, 0))
    grad_mix_w = lax.dot_general(hidden, grad_mix, TN, preferred_element_type=F32).astype(BF)
    mix_steps = Steps(reduce_rows([grad_mix_w], place, pairs))
    (grad_mix,) = mix_steps.beside(grad_mix)
    grad_hidden = lax.dot_general(dgate, w_gate, NT, preferred_element_type=F32)
    grad_hidden = grad_hidden + lax.dot_general(grad_mix, w_mix, NT, preferred_element_type=F32)
    (grad_hidden,) = mix_steps.beside(grad_hidden)

    x = tokens.astype(F32)
    inv = lax.rsqrt(jnp.mean(x * x, axis=-1, keepdims=True) + 1e-05)
    unit = x * inv
    scaled = grad_hidden * norm_full
    mean = jnp.mean(scaled * unit, axis=-1, keepdims=True)
    grad_tokens = upstream.astype(F32) + inv * (scaled - unit * mean)
    grad_norm = jnp.sum(grad_hidden * unit, axis=0)

    conv_sums = conv_sums.reshape(taps + 1, 8, CHANNELS).sum(axis=1)
    gate_sums = gate_sums.reshape(2, 8, DI).sum(axis=1)
    head_sums = head_sums.reshape(2, 8, HEADS).sum(axis=1)
    grad_skip = gate_sums[1].reshape(HEADS, HEADDIM).sum(axis=1)
    devices = 2 * pairs * fsdp
    parts = jnp.concatenate(
        [
            conv_sums.reshape(taps + 1, devices, own[1]).transpose(1, 0, 2).reshape(devices, -1),
            grad_norm.reshape(devices, -1),
            gate_sums[0].reshape(devices, -1),
            jnp.broadcast_to(
                jnp.concatenate([head_sums[0], grad_skip, head_sums[1]])[None],
                (devices, 3 * HEADS),
            ),
        ],
        axis=1,
    )
    small_steps = Steps(sum_small(parts, pairs, fsdp))
    small_steps.beside()
    if mix_steps.flight is not None:
        grad_tokens, small_steps.flight, gate_steps.flight = mix_steps.beside(
            grad_tokens, small_steps.flight, gate_steps.flight
        )
    small_steps.beside()
    if mix_steps.flight is not None:
        (small_steps.flight,) = mix_steps.beside(small_steps.flight)
    mine = lax.dynamic_slice(small_steps.finish(), (device, 0), (1, parts.shape[1]))[0]
    ends = np.cumsum([own[0], own[1], own[2], own[3], HEADS, HEADS, HEADS]).tolist()
    conv_shard, bias_shard, norm_shard, gain_shard, *heads = [
        mine[a:b] for a, b in zip([0] + ends[:-1], ends)
    ]
    conv_shard = conv_shard.reshape(taps, -1)
    (mix_shard,) = mix_steps.finish()
    gate_shard, out_shard = gate_steps.finish()
    in_shard = jnp.concatenate([gate_shard, mix_shard[:, :MIX]], axis=1)
    return (
        block_out[None],
        grad_tokens[None],
        in_shard,
        out_shard,
        conv_shard,
        bias_shard,
        norm_shard,
        gain_shard,
        heads[0],
        heads[1],
        heads[2],
    )


def solution(mesh):
    seq, fsdp = mesh.devices.shape
    fine = Mesh(mesh.devices.reshape(seq // 2, 2, fsdp), ALL)
    line = ("pair", "core")
    tokens, labels, mat = P("fsdp", line, None), P("fsdp", line), P(ALL, None)
    weights = (mat, mat, P(None, ALL), P(ALL), P(ALL), P(ALL), P(), P(), P())
    return jax.shard_map(
        functools.partial(on_device, seq // 2),
        mesh=fine,
        in_specs=(tokens, labels) + weights + (tokens,),
        out_specs=(tokens, tokens) + weights,
        check_vma=False,
    )
```
